128 devices in a mesh: dp: 32 (over y, z, core), mp: 4 (over x).
Axes of the slice: x: 4, y: 4, z: 4, core: 2. Of those that a mesh axis runs over, the one named last changes fastest.
Arguments:
- layer_input: bfloat16 [32768, 1024], P(('dp', 'mp')), may hold values from -6 to 6
- lengths: int32 [32], P('dp'), may hold values from 769 to 1024, as said below
- routes: int32 [32768, 8], P(('dp', 'mp')), may hold values from 0 to 31, all different within a row; in each aligned block of 256 rows (0 to 255, 256 to 511, ...) at most 96 rows name the same one
- attn_gain: float32 [1024], replicated, may hold values from 0.5 to 1.5
- query_gain: float32 [64], replicated, may hold values from 0.5 to 1.5
- key_gain: float32 [64], replicated, may hold values from 0.5 to 1.5
- query_weight: bfloat16 [1024, 1024], P('dp', 'mp'), may hold values from -0.1875 to 0.1875
- key_value_weight: bfloat16 [1024, 2, 512], P('dp', None, 'mp'), may hold values from -0.1875 to 0.1875
- out_weight: bfloat16 [1024, 1024], P('dp', 'mp'), may hold values from -1.5 to 1.5
- ffn_gain: float32 [1024], replicated, may hold values from 0.5 to 1.5
- router_weight: bfloat16 [1024, 32], replicated, may hold values from -0.09375 to 0.09375
- gate_weight: bfloat16 [32, 1024, 512], P('dp'), may hold values from -0.1875 to 0.1875
- up_weight: bfloat16 [32, 1024, 512], P('dp'), may hold values from -0.1875 to 0.1875
- down_weight: bfloat16 [32, 512, 1024], P('dp'), may hold values from -0.75 to 0.75
- cotangent: bfloat16 [32768, 1024], P(('dp', 'mp')), may hold values from -6 to 6
Outputs:
- layer_output: bfloat16 [32768, 1024], P(('dp', 'mp'))
- input_grad: float32 [32768, 1024], P(('dp', 'mp'))
- attn_gain_grad: float32 [1024], replicated
- query_gain_grad: float32 [64], replicated
- key_gain_grad: float32 [64], replicated
- query_weight_grad: float32 [1024, 1024], P('dp', 'mp')
- key_value_weight_grad: float32 [1024, 2, 512], P('dp', None, 'mp')
- out_weight_grad: float32 [1024, 1024], P('dp', 'mp')
- ffn_gain_grad: float32 [1024], replicated
- router_weight_grad: float32 [1024, 32], replicated
- gate_weight_grad: float32 [32, 1024, 512], P('dp', 'mp')
- up_weight_grad: float32 [32, 1024, 512], P('dp', 'mp')
- down_weight_grad: float32 [32, 512, 1024], P('dp', 'mp')
The draws below stay inside these ranges and needn't reach their ends.
Inputs may be any that keep to these rules, and one draw needn't show every extreme that they name: `lengths`: places at or past a sequence's length are padding; some sequence has exactly 1024 tokens. `routes`: A row names 8 different experts. In each aligned block of 256 rows (the rows of one device) no expert is named by more than 96 rows, a bound that some block reaches.
All inputs are finite; a program needn't handle non-finite values.
Results may differ from the reference program's by a relative error of at most 0.024.
Values may be sent and summed in bfloat16 or wider, within the bound.
No kernel may reach another device: no remote copies, remote signals or barrier semaphores. Data moves between devices by JAX's collectives and lax.ppermute only.
A program may use at most 192 MiB of HBM per device.

```python
import math
from functools import partial
import jax
import jax.numpy as jnp
import numpy as np
from jax import lax

D = 1024
HEADS = 16
KV_HEADS = 8
HDIM = 64
FF_E = 512
TOPK = 8
LEN = 1024
EXPERTS = 32
NSEQ = 32
TOK_DEV = 256
TOKENS = 32768
CAP = 96


def draw_lengths(key, part):
    key = jax.random.fold_in(key, 11)
    first_key, second_key = jax.random.split(key)
    drawn = jax.random.randint(first_key, (NSEQ,), 3 * LEN // 4 + 1, LEN + 1)
    longest = jax.random.randint(second_key, (), 0, NSEQ)
    return jnp.where(jnp.arange(NSEQ) == longest, LEN, drawn).astype(jnp.int32)


def levels(stream_key, extent, cuts, least, top_value):
    def one(axis_at, blocks):
        heights = jax.random.uniform(jax.random.fold_in(jax.random.fold_in(stream_key, 6), axis_at), (blocks,), jnp.float32, least / len(cuts), top_value / len(cuts))
        return jnp.repeat(jnp.exp(heights), extent[axis_at] // blocks).reshape((-1,) + (1,) * (len(extent) - axis_at - 1))

    level = one(*cuts[0])
    for cut in cuts[1:]:
        level = level * one(*cut)
    return level


def routed_block(rng, own, number, rows, number_of, top, reach, slope):
    order = jax.random.permutation(rng, number_of)
    crowded, common = portions_of(number_of, rows * top, reach, slope, True), portions_of(number_of, rows * top, reach, slope, False)
    places = jnp.arange(number_of)

    def named(tallies, turn):
        used = int((tallies > 0).sum())
        fixed = max(1, used // 4)
        moved = fixed + (places - fixed + turn * (used - fixed)) % max(1, number_of - fixed)
        return jnp.zeros((number_of,), jnp.int32).at[order[jnp.where(places < fixed, places, moved)]].set(jnp.asarray(tallies, jnp.int32))

    tallies = jnp.where(number % 4 == 0, named(crowded, number // 4), named(common, number - number // 4 - 1))
    mixed = jax.random.permutation(jax.random.fold_in(own, 3), number_of)
    donor, taker = mixed[0:number_of // 2 * 2:2], mixed[1:number_of // 2 * 2:2]
    slack = jnp.minimum(tallies[donor] - 1, reach - tallies[taker]) // 2
    slack = jnp.where((donor == order[0]) | (taker == order[0]) | (tallies[taker] == 0), 0, jnp.maximum(slack, 0))
    moved = jax.random.randint(jax.random.fold_in(own, 4), (number_of // 2,), 0, 1 << 20) % (slack + 1)
    tallies = tallies.at[donor].add(-moved).at[taker].add(moved)
    members = jnp.searchsorted(jnp.cumsum(tallies), jnp.arange(rows * top), side="right").astype(jnp.int32)
    listing = members.reshape(top, rows).T
    listing = listing[jax.random.permutation(jax.random.fold_in(own, 1), rows)]
    turn = jax.random.randint(jax.random.fold_in(own, 2), (rows, 1), 0, top)
    return jnp.take_along_axis(listing, (jnp.arange(top)[None, :] + turn) % top, axis=1)


def portions_of(amount, total, reach, lean, full):
    portions = [(1 << 20) // math.isqrt(standing ** lean) + 1 for standing in range(1, amount + 1)]
    largest = reach if full else min(reach, max(-(-total // amount), total * portions[0] // sum(portions)))
    least = 1 if total - largest >= amount - 1 else 0
    given, surplus = [largest] + [least] * (amount - 1), total - largest - least * (amount - 1)
    while surplus > 0:
        candidates = [i for i in range(1, amount) if given[i] < largest] or [i for i in range(1, amount) if given[i] < reach]
        whole, budget = sum([portions[i] for i in candidates]), surplus
        for i in candidates:
            extra = min(reach - given[i], max(1, budget * portions[i] // whole), surplus)
            given[i] = given[i] + extra
            surplus = surplus - extra
    return np.array(given)


def gaussian(stream_key, dims, spread, limit, cuts=(), held_as=jnp.bfloat16):
    array = jax.random.normal(stream_key, dims, jnp.float32) * spread
    if len(cuts) > 0:
        array = levels(stream_key, dims, cuts, -0.22, 0.18) * array
    return jnp.clip(array, min=-limit, max=limit).astype(held_as)


def setup_inputs(seed: int = 0) -> dict:
    key_list = jax.random.split(jax.random.key(seed), 16)
    layer_input = gaussian(key_list[0], (TOKENS, D), 1.0, 6.0, ((0, 128),))
    lengths = draw_lengths(jax.random.fold_in(key_list[15], 71), 0)
    routes_keys = jax.random.split(jax.random.fold_in(key_list[2], 1), TOKENS // TOK_DEV)
    routes_turns = jax.random.permutation(jax.random.fold_in(key_list[2], 3), TOKENS // TOK_DEV)
    routes = jax.vmap(lambda own, number: routed_block(jax.random.fold_in(key_list[2], 2), own, number, TOK_DEV, EXPERTS, TOPK, CAP, 2))(routes_keys, routes_turns).reshape((TOKENS, TOPK))
    attn_gain = jnp.clip(1.0 + 0.1 * jax.random.normal(key_list[3], (D,), jnp.float32), 0.5, 1.5)
    query_gain = jnp.clip(1.0 + 0.1 * jax.random.normal(key_list[4], (HDIM,), jnp.float32), 0.5, 1.5)
    key_gain = jnp.clip(1.0 + 0.1 * jax.random.normal(key_list[5], (HDIM,), jnp.float32), 0.5, 1.5)
    query_weight = gaussian(key_list[6], (D, HEADS * HDIM), D ** -0.5, 0.1875, ((0, 32), (1, 4)))
    key_value_weight = gaussian(key_list[7], (D, 2, KV_HEADS * HDIM), D ** -0.5, 0.1875, ((0, 32), (2, 4)))
    out_weight = gaussian(key_list[8], (D, HEADS * HDIM), (HEADS * HDIM // 64) ** -0.5, 1.5, ((0, 32), (1, 4)))
    ffn_gain = jnp.clip(1.0 + 0.1 * jax.random.normal(key_list[9], (D,), jnp.float32), 0.5, 1.5)
    router_weight = gaussian(key_list[10], (D, EXPERTS), (4 * D) ** -0.5, 0.09375)
    gate_weight = gaussian(key_list[11], (EXPERTS, D, FF_E), D ** -0.5, 0.1875, ((0, 32),))
    up_weight = gaussian(key_list[12], (EXPERTS, D, FF_E), D ** -0.5, 0.1875, ((0, 32),))
    down_weight = gaussian(key_list[13], (EXPERTS, FF_E, D), (FF_E // 8) ** -0.5, 0.75, ((0, 32),))
    cotangent = gaussian(key_list[14], (TOKENS, D), 1.0, 6.0, ((0, 128),))
    return dict(layer_input=layer_input, lengths=lengths, routes=routes, attn_gain=attn_gain, query_gain=query_gain, key_gain=key_gain, query_weight=query_weight, key_value_weight=key_value_weight, out_weight=out_weight, ffn_gain=ffn_gain, router_weight=router_weight, gate_weight=gate_weight, up_weight=up_weight, down_weight=down_weight, cotangent=cotangent)


EPS = 1e-06
HIGH = lax.Precision.HIGHEST

@jax.custom_vjp
def low(v):
    return lax.optimization_barrier(v.astype(jnp.bfloat16)).astype(jnp.float32)

@jax.custom_vjp
def low_back(v):
    return v

def low_keep(v):
    return (low(v), None)

def low_pass(kept, grad):
    return (grad,)

def back_keep(v):
    return (v, None)

def back_low(kept, grad):
    return (low(grad),)
low.defvjp(low_keep, low_pass)
low_back.defvjp(back_keep, back_low)

def norm_rows(tensor, gain_vec):
    return tensor * lax.rsqrt(lax.optimization_barrier(jnp.mean(tensor * tensor, axis=-1, keepdims=True)) + EPS) * gain_vec

def rope_tables():
    places = jnp.arange(LEN, dtype=jnp.float32)
    inverse = jnp.power(10000.0, -2.0 * jnp.arange(HDIM // 2, dtype=jnp.float32) / HDIM)
    angles = places[:, None] * inverse[None, :]
    return (jnp.cos(angles), jnp.sin(angles))

def rotate(tensor, cos_tab, sin_tab):
    first_half = tensor[..., :HDIM // 2]
    second_half = tensor[..., HDIM // 2:]
    cos_b = cos_tab[:, None, :]
    sin_b = sin_tab[:, None, :]
    return jnp.concatenate([first_half * cos_b - second_half * sin_b, second_half * cos_b + first_half * sin_b], axis=-1)

def attend_one(packed):
    queries, keys, values, length = packed
    scores = jnp.einsum('qkgd,pkd->kgqp', queries, keys, precision=HIGH) * HDIM ** (-0.5)
    scores = low_back(scores)
    valid_keys = jnp.arange(LEN, dtype=jnp.int32) < length
    scores = jnp.where(valid_keys, scores, -1e+30)
    top_val = lax.optimization_barrier(jnp.max(scores, axis=-1, keepdims=True))
    weights = jnp.exp(scores - top_val)
    probs = weights / lax.optimization_barrier(jnp.sum(weights, axis=-1, keepdims=True))
    return jnp.einsum('kgqp,pkd->qkgd', low(probs), values, precision=HIGH)

def expert_block(gate_weight, up_weight, down_weight, packed):
    block_rows, picks, gates = packed
    flat_routes = picks.reshape(-1)
    matches = (flat_routes[:, None] == jnp.arange(EXPERTS, dtype=jnp.int32)[None, :]).astype(jnp.int32)
    rank_in = lax.optimization_barrier(jnp.sum((jnp.cumsum(matches, axis=0) - 1) * matches, axis=1))
    slot_index = (flat_routes * CAP + rank_in).astype(jnp.int32)
    owner_row = jnp.arange(TOK_DEV * TOPK, dtype=jnp.int32) // TOPK
    source = jnp.zeros((EXPERTS * CAP,), jnp.int32).at[slot_index].set(owner_row)
    live_slot = jnp.zeros((EXPERTS * CAP,), block_rows.dtype).at[slot_index].set(1.0)
    taken = low_back(block_rows[source] * live_slot[:, None]).reshape(EXPERTS, CAP, D)
    gate_act = low_back(jnp.einsum('ecd,edf->ecf', taken, gate_weight, precision=HIGH))
    up_act = low_back(jnp.einsum('ecd,edf->ecf', taken, up_weight, precision=HIGH))
    hidden = low(jax.nn.silu(gate_act) * up_act)
    result = low_back(low(jnp.einsum('ecf,efd->ecd', hidden, down_weight, precision=HIGH)))
    picked = result.reshape(EXPERTS * CAP, D)[slot_index].reshape(TOK_DEV, TOPK, D)
    return lax.optimization_barrier(jnp.sum(gates[:, :, None] * picked, axis=1))

def forward(layer_input, attn_gain, query_gain, key_gain, query_weight, key_value_weight, out_weight, ffn_gain, router_weight, gate_weight, up_weight, down_weight, lengths, routes):
    group_size = HEADS // KV_HEADS
    cos_tab, sin_tab = rope_tables()
    normed_one = low(norm_rows(layer_input, attn_gain))
    query = low_back(jnp.dot(normed_one, query_weight, precision=HIGH))
    pair = low_back(jnp.einsum('td,dch->tch', normed_one, key_value_weight, precision=HIGH))
    query = query.reshape(NSEQ, LEN, HEADS, HDIM)
    keys = pair[:, 0].reshape(NSEQ, LEN, KV_HEADS, HDIM)
    values = low(pair[:, 1]).reshape(NSEQ, LEN, KV_HEADS, HDIM)
    query = low(rotate(norm_rows(query, query_gain), cos_tab, sin_tab)).reshape(NSEQ, LEN, KV_HEADS, group_size, HDIM)
    keys = low(rotate(norm_rows(keys, key_gain), cos_tab, sin_tab))
    mixed = lax.map(jax.checkpoint(attend_one), (query, keys, values, lengths))
    mixed = low_back(low(mixed.reshape(TOKENS, HEADS * HDIM)))
    x_mid = layer_input + low_back(jnp.dot(mixed, out_weight.T, precision=HIGH))
    normed_two = low(norm_rows(x_mid, ffn_gain))
    logits = low_back(jnp.dot(normed_two, router_weight, precision=HIGH))
    chosen = jnp.take_along_axis(logits, routes, axis=1)
    top_val = lax.optimization_barrier(jnp.max(chosen, axis=1, keepdims=True))
    weights = jnp.exp(chosen - top_val)
    gates = weights / lax.optimization_barrier(jnp.sum(weights, axis=1, keepdims=True))
    blocks = TOKENS // TOK_DEV
    expert_out = lax.map(jax.checkpoint(partial(expert_block, gate_weight, up_weight, down_weight)), (normed_two.reshape(blocks, TOK_DEV, D), routes.reshape(blocks, TOK_DEV, TOPK), gates.reshape(blocks, TOK_DEV, TOPK)))
    return x_mid + expert_out.reshape(TOKENS, D)

def reference(layer_input, lengths, routes, attn_gain, query_gain, key_gain, query_weight, key_value_weight, out_weight, ffn_gain, router_weight, gate_weight, up_weight, down_weight, cotangent):
    floats = tuple((array_in.astype(jnp.float32) for array_in in (layer_input, attn_gain, query_gain, key_gain, query_weight, key_value_weight, out_weight, ffn_gain, router_weight, gate_weight, up_weight, down_weight)))

    def apply_layer(*weights):
        return forward(*weights, lengths, routes)
    output, pullback = jax.vjp(apply_layer, *floats)
    places = jnp.arange(LEN, dtype=jnp.int32)
    valid = (places[None, :] < lengths[:, None]).astype(jnp.float32).reshape(TOKENS)
    grads = pullback(cotangent.astype(jnp.float32) * valid[:, None])
    return (output.astype(jnp.bfloat16), grads[0], grads[1], grads[2], grads[3], grads[4], grads[5], grads[6], grads[7], grads[8], grads[9], grads[10], grads[11])
```

```python
from functools import partial

import jax
import jax.numpy as jnp
import numpy as np
from jax import lax
from jax.experimental import pallas as pl
from jax.experimental.pallas import tpu as pltpu
from jax.sharding import PartitionSpec as P

WIDTH = 1024
HDIM = 64
PITCH = 128
LEN = 1024
TOK = 256
CAP = 96
EXPERTS = 32
FF = 512
SIDE = 16
ROWS = TOK + SIDE
EPS = 1e-06
LOG2E = 1.4426950408889634
F32 = jnp.float32
BF16 = jnp.bfloat16
VMEM_BYTES = 60 * 1024 * 1024


def nn(left, right):
    return lax.dot_general(left, right, (((1,), (0,)), ((), ())), preferred_element_type=F32)


def nt(left, right):
    return lax.dot_general(left, right, (((1,), (1,)), ((), ())), preferred_element_type=F32)


def tn(left, right):
    return lax.dot_general(left, right, (((0,), (0,)), ((), ())), preferred_element_type=F32)


def spread(heads):
    table = np.zeros((heads * HDIM, heads * PITCH), np.float32)
    for head in range(heads):
        for lane in range(HDIM):
            table[head * HDIM + lane, head * PITCH + lane] = 1.0
    return table


def rope_tables():
    places = np.arange(LEN, dtype=np.float64)
    inverse = 10000.0 ** (-2.0 * np.arange(HDIM // 2, dtype=np.float64) / HDIM)
    angles = places[:, None] * inverse[None, :]
    cos_tab = np.zeros((LEN, PITCH), np.float32)
    sin_tab = np.zeros((LEN, PITCH), np.float32)
    cos_tab[:, : HDIM // 2] = np.cos(angles)
    cos_tab[:, HDIM // 2 : HDIM] = np.cos(angles)
    sin_tab[:, : HDIM // 2] = -np.sin(angles)
    sin_tab[:, HDIM // 2 : HDIM] = np.sin(angles)
    return cos_tab.reshape(LEN // TOK, TOK, PITCH), sin_tab.reshape(LEN // TOK, TOK, PITCH)


def lanes(shape):
    return lax.broadcasted_iota(jnp.int32, shape, 1)


def swap_halves(tensor):
    half = HDIM // 2
    ahead = pltpu.roll(tensor, PITCH - half, 1)
    behind = pltpu.roll(tensor, half, 1)
    return jnp.where(lanes(tensor.shape) < half, ahead, behind)


def head_scale(tensor):
    return lax.rsqrt(jnp.sum(tensor * tensor, axis=1, keepdims=True) * (1.0 / HDIM) + EPS)


def row_scale(tensor):
    return lax.rsqrt(jnp.mean(tensor * tensor, axis=1, keepdims=True) + EPS)


def call(body, out_shape, args, scalars=None, any_in=(), any_out=(), scratch=(), aliases=None):
    offset = 0 if scalars is None else 1
    in_specs = [pl.BlockSpec(memory_space=pl.ANY if i in any_in else pltpu.VMEM) for i in range(len(args))]
    out_specs = [pl.BlockSpec(memory_space=pl.ANY if i in any_out else pltpu.VMEM) for i in range(len(out_shape))]
    params = pltpu.CompilerParams(vmem_limit_bytes=VMEM_BYTES)
    shapes = [jax.ShapeDtypeStruct(s, d) for s, d in out_shape]
    if scalars is not None:
        in_specs = [pl.BlockSpec(memory_space=pltpu.SMEM)] + in_specs
        args = (scalars,) + tuple(args)
    return pl.pallas_call(
        body,
        out_shape=shapes,
        in_specs=in_specs,
        out_specs=out_specs,
        scratch_shapes=list(scratch),
        input_output_aliases={i + offset: o for i, o in (aliases or {}).items()},
        compiler_params=params,
    )(*args)


def start_body(sc, cot, routes, packed, ranks_out):
    base = sc[0] * TOK
    length = sc[1]
    place = base + lax.broadcasted_iota(jnp.int32, (TOK, 1), 0)
    keep = jnp.where(place < length, 1.0, 0.0)
    packed[0:TOK, :] = (cot[...].astype(F32) * keep).astype(BF16)
    names = lax.broadcasted_iota(jnp.int32, (TOK, EXPERTS), 1)
    member = jnp.zeros((TOK, EXPERTS), F32)
    for k in range(routes.shape[1]):
        member = member + jnp.where(routes[:, k : k + 1] == names, 1.0, 0.0)
    member = member.astype(BF16)
    earlier = lax.broadcasted_iota(jnp.int32, (TOK, TOK), 0)
    later = lax.broadcasted_iota(jnp.int32, (TOK, TOK), 1)
    before = jnp.where(earlier < later, 1.0, 0.0).astype(BF16)
    same = jnp.where(earlier == later, 1.0, 0.0).astype(BF16)
    counts = tn(member, before)
    chosen = tn(member, same)
    ranks = jnp.where(chosen > 0.5, counts, -1.0)
    ranks_out[...] = ranks
    quarter = EXPERTS // 4
    rows = jnp.concatenate([ranks[q * quarter : (q + 1) * quarter] for q in range(4)], axis=1)
    packed[TOK:ROWS, :] = jnp.concatenate([rows, jnp.zeros_like(rows)], axis=0).astype(BF16)


def assemble_body(sc, own, other, spread4, spread2, proj, out_w, held):
    y_at, z_at, core = sc[0], sc[1], sc[2]
    for block in range(16):
        rel = ((block // 4 - y_at + 4) % 4) * 4 + (block % 4 - z_at + 4) % 4
        mine = own[rel].astype(F32)
        theirs = other[rel].astype(F32)
        for side in range(2):
            part = jnp.where(core == side, mine, theirs).astype(BF16)
            at = (2 * block + side) * 32
            for piece in range(3):
                held[at : at + 32, piece * 256 : (piece + 1) * 256] = part[piece * 32 : (piece + 1) * 32]
    proj[:, 0:512] = nn(held[:, 0:256], spread4[...]).astype(BF16)
    proj[:, 512:768] = nn(held[:, 256:384], spread2[...]).astype(BF16)
    proj[:, 768:1024] = nn(held[:, 384:512], spread2[...]).astype(BF16)
    out_w[...] = nn(held[:, 512:768], spread4[...]).astype(BF16)


def project_body(sc, x, gain, proj, head_gain, cos, sin, h1, qa, ka, va, raw_out):
    at = sc[0]
    length = sc[1]
    xf = x[...].astype(F32)
    normed = (xf * row_scale(xf) * gain[...]).astype(BF16)
    h1[...] = normed
    raw = nn(normed, proj[...])
    raw_out[...] = raw[:, 0:768]
    cos_t = cos[at]
    sin_t = sin[at]
    lane = lanes((TOK, PITCH))
    place = at * TOK + lax.broadcasted_iota(jnp.int32, (TOK, PITCH), 0)
    bias = jnp.where(place < length, 0.0, -1e30)
    q_aug = jnp.where(lane == HDIM, 1.0, 0.0)
    k_aug = jnp.where(lane == HDIM, bias, jnp.where(lane < HDIM + 4, 1.0, 0.0))
    v_aug = jnp.where(lane < HDIM + 2, 1.0, 0.0)
    for head in range(6):
        cols = slice(head * PITCH, (head + 1) * PITCH)
        one = raw[:, cols]
        ready = one * head_scale(one) * head_gain[:, cols]
        turned = ready * cos_t + swap_halves(ready) * sin_t
        if head < 4:
            qa[:, cols] = jnp.where(lane < HDIM, turned, q_aug).astype(BF16)
        else:
            here = slice((head - 4) * PITCH, (head - 3) * PITCH)
            ka[:, here] = jnp.where(lane < HDIM, turned, k_aug).astype(BF16)
    for head in range(2):
        va[:, head * PITCH : (head + 1) * PITCH] = jnp.where(
            lane < HDIM, raw[:, 768 + head * PITCH : 768 + (head + 1) * PITCH], v_aug
        ).astype(BF16)


def attend_body(qa, k0, k1, k2, k3, v0, v1, v2, v3, out_w, branch, mixed, qb):
    lane = lanes((TOK, PITCH))
    for head in range(4):
        cols = slice(head * PITCH, (head + 1) * PITCH)
        kv = slice((head // 2) * PITCH, (head // 2 + 1) * PITCH)
        query = qa[:, cols]
        total = jnp.zeros((TOK, PITCH), F32)
        for keys, values in ((k0, v0), (k1, v1), (k2, v2), (k3, v3)):
            weight = jnp.exp2(nt(query, keys[:, kv]) * (LOG2E / 8.0)).astype(BF16)
            total = total + nn(weight, values[:, kv])
        denom = total[:, HDIM : HDIM + 1]
        mixed[:, cols] = jnp.where(lane < HDIM, total / denom, 0.0).astype(BF16)
        level = jnp.log(denom) * -8.0
        high = level.astype(BF16).astype(F32)
        middle = (level - high).astype(BF16).astype(F32)
        low = level - high - middle
        stats = jnp.where(lane == HDIM + 1, high, jnp.where(lane == HDIM + 2, middle, low))
        qb[:, cols] = jnp.where(
            (lane > HDIM) & (lane < HDIM + 4), stats, query.astype(F32)
        ).astype(BF16)
    branch[...] = nt(mixed[...], out_w[...]).astype(BF16)


def middle_body(x, p0, p1, p2, p3, gain, x_mid, h2):
    total = (
        x[...].astype(F32)
        + ((p0[...].astype(F32) + p1[...].astype(F32)) + (p2[...].astype(F32) + p3[...].astype(F32)))
    )
    x_mid[...] = total
    h2[...] = (total * row_scale(total) * gain[...]).astype(BF16)


def gates_of(logits, ranks):
    routed = ranks >= 0.0
    masked = jnp.where(routed, logits, -1e30)
    weight = jnp.where(routed, jnp.exp(masked - jnp.max(masked, axis=0, keepdims=True)), 0.0)
    return weight / jnp.sum(weight, axis=0, keepdims=True)


def gates_body(h2, router, ranks, gates):
    gates[...] = gates_of(nt(router[...], h2[...]), ranks[...])


def unfold(rows):
    return jnp.concatenate([rows[:, q * TOK : (q + 1) * TOK] for q in range(4)], axis=0)


def experts_body(pieces, unit, *refs):
    sc = refs[0]
    tokens = refs[1 : 1 + len(pieces)]
    at = 1 + len(pieces)
    cot_all, router = refs[at], refs[at + 1]
    weights = refs[at + 2 : at + 8]
    at = at + 8
    if unit > 0:
        at = at + 6
    y_out, y_back, taken_all, push_all, hidden_all, gate_all, up_all = refs[at : at + 7]
    cot, y_hold, t_hold, e_hold, h_hold, g_hold, u_hold, sems = refs[at + 7 :]
    copies_in = [pltpu.make_async_copy(cot_all.at[sc[i]], cot.at[i], sems.at[i]) for i in range(4)]
    for one in copies_in:
        one.start()
    where = []
    for index, count in enumerate(pieces):
        where += [(tokens[index], j) for j in range(count)]
    own_names = (sc[4], sc[5])
    names = lax.broadcasted_iota(jnp.int32, (EXPERTS, TOK), 0)
    slots = lax.broadcasted_iota(jnp.int32, (CAP, TOK), 0).astype(F32)
    for one in copies_in:
        one.wait()
    picks = [[], []]
    gate_rows = [[], []]
    for i in range(4):
        ref, j = where[i]
        block = ref[j]
        ranks = unfold(cot[i, TOK : TOK + EXPERTS // 4, :].astype(F32))
        gates = gates_of(nt(router[...], block), ranks)
        for e in range(2):
            hit = names == own_names[e]
            rank = jnp.sum(jnp.where(hit, ranks, 0.0), axis=0, keepdims=True)
            gate = jnp.sum(jnp.where(hit, gates, 0.0), axis=0, keepdims=True)
            pick = jnp.where(slots == rank, 1.0, 0.0)
            picks[e].append(pick.astype(BF16))
            gate_rows[e].append(jnp.sum(pick * gate, axis=1, keepdims=True))
    marks = [[], []]
    back_parts = []
    out_parts = []
    copies_out = []
    for e in range(2):
        gate_w, up_w, down_w = weights[3 * e], weights[3 * e + 1], weights[3 * e + 2]
        for i in range(4):
            ref, j = where[i]
            t_hold[e, i * CAP : (i + 1) * CAP, :] = nn(picks[e][i], ref[j]).astype(BF16)
        taken = t_hold[e]
        gate_act = nn(taken, gate_w[0])
        up_act = nn(taken, up_w[0])
        sigma = jax.nn.sigmoid(gate_act)
        silu = gate_act * sigma
        hidden = (silu * up_act).astype(BF16)
        h_hold[e] = hidden
        result = nn(hidden, down_w[0]).astype(BF16).astype(F32)
        gate_col = jnp.concatenate(gate_rows[e], axis=0)
        grad_rows = jnp.concatenate([nn(picks[e][i], cot[i, 0:TOK, :]) for i in range(4)], axis=0)
        mark = jnp.sum(grad_rows * result, axis=1, keepdims=True)
        for i in range(4):
            marks[e].append(
                jnp.sum(picks[e][i].astype(F32) * mark[i * CAP : (i + 1) * CAP], axis=0, keepdims=True)
            )
        out_parts.append((result * gate_col).astype(BF16))
        push = (grad_rows * gate_col).astype(BF16)
        e_hold[e] = push
        grad_hidden = nt(push, down_w[0])
        grad_gate = (grad_hidden * up_act * (sigma * (1.0 + gate_act * (1.0 - sigma)))).astype(BF16)
        grad_up = (grad_hidden * silu).astype(BF16)
        g_hold[e] = grad_gate
        u_hold[e] = grad_up
        back_parts.append((nt(grad_gate, gate_w[0]) + nt(grad_up, up_w[0])).astype(BF16))
    stores = (
        (t_hold, taken_all, CAP * 4),
        (e_hold, push_all, CAP * 4),
        (h_hold, hidden_all, CAP * 4),
        (g_hold, gate_all, CAP * 4),
        (u_hold, up_all, CAP * 4),
    )
    for index, (hold, target, rows) in enumerate(stores):
        for e in range(2):
            one = pltpu.make_async_copy(
                hold.at[e], target.at[e, pl.ds(unit * rows, rows)], sems.at[4 + 2 * index + e]
            )
            one.start()
            copies_out.append(one)
    for i in range(4):
        pick = jnp.concatenate([picks[0][i], picks[1][i]], axis=0)
        rows = slice(i * CAP, (i + 1) * CAP)
        y_hold[i] = tn(pick, jnp.concatenate([out_parts[0][rows], out_parts[1][rows]], axis=0)).astype(BF16)
        one = pltpu.make_async_copy(y_hold.at[i], y_out.at[sc[i]], sems.at[14 + i])
        one.start()
        copies_out.append(one)
        y_back[i, 0:TOK, :] = tn(
            pick, jnp.concatenate([back_parts[0][rows], back_parts[1][rows]], axis=0)
        ).astype(BF16)
        mark = jnp.where(names == own_names[0], marks[0][i], 0.0) + jnp.where(
            names == own_names[1], marks[1][i], 0.0
        )
        high = mark.astype(BF16).astype(F32)
        low = mark - high
        quarter = EXPERTS // 4
        fold = [
            jnp.concatenate([part[q * quarter : (q + 1) * quarter] for q in range(4)], axis=1)
            for part in (high, low)
        ]
        y_back[i, TOK:ROWS, :] = jnp.concatenate(fold, axis=0).astype(BF16)
    for one in copies_out:
        one.wait()


def token_back_body(r0, r1, r2, h2, x_mid, ranks, gates, router, gain, packed, grad_mid, branch, small):
    total = r0[...].astype(F32) + (r1[...].astype(F32) + r2[...].astype(F32))
    marks = unfold(total[TOK : TOK + 8]) + unfold(total[TOK + 8 : TOK + 16])
    gate = gates[...]
    centre = jnp.sum(gate * marks, axis=0, keepdims=True)
    grad_logits = jnp.where(ranks[...] >= 0.0, gate * (marks - centre), 0.0).astype(BF16)
    small[0:EXPERTS, :] = nn(grad_logits, h2[...])
    grad_h2 = total[0:TOK] + tn(grad_logits, router[...])
    x = x_mid[...]
    scale = row_scale(x)
    normed = x * scale
    grad_normed = grad_h2 * gain[...]
    small[EXPERTS : EXPERTS + 8, :] = jnp.broadcast_to(
        jnp.sum(grad_h2 * normed, axis=0, keepdims=True), (8, WIDTH)
    )
    out = packed[0:TOK, :].astype(F32) + scale * (
        grad_normed - normed * jnp.mean(grad_normed * normed, axis=1, keepdims=True)
    )
    grad_mid[...] = out
    branch[...] = out.astype(BF16)


def head_back(grad, raw, gain, cos_t, sin_t):
    upstream = grad * cos_t - swap_halves(grad) * sin_t
    scale = head_scale(raw)
    normed = raw * scale
    grad_normed = upstream * gain
    gain_grad = jnp.sum(upstream * normed, axis=0, keepdims=True)
    inner = jnp.sum(grad_normed * normed, axis=1, keepdims=True) * (1.0 / HDIM)
    return scale * (grad_normed - normed * inner), gain_grad


def attend_back_body(first, *refs):
    sc, rows, out_w, qb, mixed, k0, k1, k2, k3, v0, v1, v2, v3, raw, head_gain, cos, sin = refs[:17]
    rest = refs[17:] if first else refs[18:]
    before = None if first else refs[17]
    grad_query, gain_out, both = rest
    at = sc[0]
    cos_t = cos[at]
    sin_t = sin[at]
    lane = lanes((TOK, PITCH))
    pushed = nn(rows[...], out_w[...]).astype(BF16)
    gain_total = jnp.zeros((1, PITCH), F32)
    for head in range(4):
        cols = slice(head * PITCH, (head + 1) * PITCH)
        group = head // 2
        kv = slice(group * PITCH, (group + 1) * PITCH)
        grad = pushed[:, cols]
        grad_f = grad.astype(F32)
        delta = -jnp.sum(grad_f * mixed[:, cols].astype(F32), axis=1, keepdims=True)
        high = delta.astype(BF16).astype(F32)
        grad_aug = jnp.where(
            lane == HDIM, high, jnp.where(lane == HDIM + 1, delta - high, grad_f)
        ).astype(BF16)
        query = qb[:, cols]
        grad_q = jnp.zeros((TOK, PITCH), F32)
        for c, (keys, values) in enumerate(((k0, v0), (k1, v1), (k2, v2), (k3, v3))):
            probs = jnp.exp2(nt(keys[:, kv], query) * (LOG2E / 8.0))
            inner = nt(values[:, kv], grad_aug)
            grad_scores = (probs * inner).astype(BF16)
            add_k = nn(grad_scores, query)
            add_v = nn(probs.astype(BF16), grad)
            kcols = kv
            vcols = slice(256 + group * PITCH, 256 + (group + 1) * PITCH)
            if head % 2 == 0:
                if first:
                    both[c, :, kcols] = add_k
                    both[c, :, vcols] = add_v
                else:
                    both[c, :, kcols] = before[c, :, kcols] + add_k
                    both[c, :, vcols] = before[c, :, vcols] + add_v
            else:
                both[c, :, kcols] += add_k
                both[c, :, vcols] += add_v
            grad_q = grad_q + tn(grad_scores, keys[:, kv])
        grad_q = jnp.where(lane < HDIM, grad_q * 0.125, 0.0)
        back, gain_grad = head_back(grad_q, raw[:, cols], head_gain[:, cols], cos_t, sin_t)
        grad_query[:, cols] = back.astype(BF16)
        gain_total = gain_total + gain_grad
    gain_out[...] = jnp.broadcast_to(gain_total, (8, PITCH))


def finish_body(chunk, sc, both, raw, head_gain, cos, sin, grad_query, x, proj, spread4, spread2, part_out, packed, gains):
    at = sc[0]
    cos_t = cos[at]
    sin_t = sin[at]
    lane = lanes((TOK, PITCH))
    pieces = [grad_query[...]]
    key_gain = jnp.zeros((1, PITCH), F32)
    for head in range(2):
        cols = slice(head * PITCH, (head + 1) * PITCH)
        grad = jnp.where(lane < HDIM, both[chunk, :, cols] * 0.125, 0.0)
        back, gain_grad = head_back(
            grad,
            raw[:, 512 + head * PITCH : 512 + (head + 1) * PITCH],
            head_gain[:, 512 + head * PITCH : 512 + (head + 1) * PITCH],
            cos_t,
            sin_t,
        )
        pieces.append(back.astype(BF16))
        key_gain = key_gain + gain_grad
    for head in range(2):
        cols = slice(256 + head * PITCH, 256 + (head + 1) * PITCH)
        pieces.append(jnp.where(lane < HDIM, both[chunk, :, cols], 0.0).astype(BF16))
    packed[:, 0:256] = nt(pieces[0], spread4[...]).astype(BF16)
    packed[:, 256:384] = nt(jnp.concatenate(pieces[1:3], axis=1), spread2[...]).astype(BF16)
    packed[:, 384:512] = nt(jnp.concatenate(pieces[3:5], axis=1), spread2[...]).astype(BF16)
    part = nt(jnp.concatenate(pieces, axis=1), proj[...])
    part_out[...] = part.astype(BF16)
    xf = x[...].astype(F32)
    gains[0:1, :] = jnp.sum(part * (xf * row_scale(xf)), axis=0, keepdims=True)
    gains[1:8, :] = jnp.zeros((7, WIDTH), F32)
    gains[1:2, 0:PITCH] = key_gain


def weight_body(*refs):
    h1, packed, rows, mixed = refs[0:4], refs[4:8], refs[8:12], refs[12:16]
    spread4, out = refs[16], refs[17]
    total = jnp.zeros((WIDTH, 512), F32)
    other = jnp.zeros((WIDTH, 256), F32)
    for i in range(4):
        total = total + tn(h1[i][...], packed[i][...])
        other = other + tn(rows[i][...], nt(mixed[i][...], spread4[...]).astype(BF16))
    out[:, 0:512] = total.astype(BF16)
    out[:, 512:768] = other.astype(BF16)


def input_body(p0, p1, p2, p3, x, gain, grad_mid, out):
    upstream = (p0[...].astype(F32) + p1[...].astype(F32)) + (p2[...].astype(F32) + p3[...].astype(F32))
    xf = x[...].astype(F32)
    scale = row_scale(xf)
    normed = xf * scale
    grad_normed = upstream * gain[...]
    out[...] = grad_mid[...] + scale * (
        grad_normed - normed * jnp.mean(grad_normed * normed, axis=1, keepdims=True)
    )


def place_of(index):
    return index // 8, (index // 2) % 4, index % 2


def index_of(y, z, core):
    return (y % 4) * 8 + (z % 4) * 2 + core


def shift_yz(tensor, dy, dz, flip=0):
    pairs = []
    for d in range(32):
        y, z, core = place_of(d)
        pairs.append((d, index_of(y + dy, z + dz, core ^ flip)))
    return lax.ppermute(tensor, "dp", pairs)


def shift_axis(tensor, axis, step):
    pairs = []
    for d in range(32):
        y, z, core = place_of(d)
        if (core == 0) == (axis == 0):
            pairs.append((d, index_of(y + step, z, core)))
        else:
            pairs.append((d, index_of(y, z + step, core)))
    return lax.ppermute(tensor, "dp", pairs)


def shift_mp(tensor, step):
    return lax.ppermute(tensor, "mp", [(i, (i + step) % 4) for i in range(4)])


def gather_weights(shard, sc):
    along_y = [shard] + [shift_yz(shard, -s, 0) for s in (1, 2, 3)]
    rows = jnp.stack(along_y)
    along_z = [rows] + [shift_yz(rows, 0, -s) for s in (1, 2, 3)]
    own = jnp.stack(along_z, axis=1).reshape(16, *shard.shape)
    other = shift_yz(own, 0, 0, 1)
    return call(
        assemble_body,
        [((WIDTH, 1024), BF16), ((WIDTH, 512), BF16)],
        (own, other, jnp.asarray(spread(4), BF16), jnp.asarray(spread(2), BF16)),
        scalars=sc,
        scratch=[pltpu.VMEM((WIDTH, 768), BF16)],
    )


def all_sum(tensor):
    tensor = tensor + (shift_mp(tensor, 1) + shift_mp(tensor, 2) + shift_mp(tensor, 3))
    tensor = tensor + (shift_yz(tensor, 1, 0) + shift_yz(tensor, 2, 0) + shift_yz(tensor, 3, 0))
    tensor = tensor + (shift_yz(tensor, 0, 1) + shift_yz(tensor, 0, 2) + shift_yz(tensor, 0, 3))
    return tensor + shift_yz(tensor, 0, 0, 1)


def add_low(left, *others):
    total = left.astype(F32)
    for one in others:
        total = total + one.astype(F32)
    return total.astype(BF16)


PLANES = [[core + 2 * k for k in range(16)] for core in range(2)]
STEPS = (0, 1, -1, 2)


def shards(
    layer_input,
    lengths,
    routes,
    attn_gain,
    query_gain,
    key_gain,
    query_weight,
    key_value_weight,
    out_weight,
    ffn_gain,
    router_weight,
    gate_weight,
    up_weight,
    down_weight,
    cotangent,
):
    dp_at = lax.axis_index("dp").astype(jnp.int32)
    mp_at = lax.axis_index("mp").astype(jnp.int32)
    y_at, z_at, core = dp_at // 8, (dp_at // 2) % 4, dp_at % 2
    length = lengths[0].astype(jnp.int32)
    cos_np, sin_np = rope_tables()
    cos_tab, sin_tab = jnp.asarray(cos_np), jnp.asarray(sin_np)
    spread4, spread2 = jnp.asarray(spread(4), BF16), jnp.asarray(spread(2), BF16)
    attn_row = attn_gain.reshape(1, WIDTH)
    ffn_row = ffn_gain.reshape(1, WIDTH)
    pad = jnp.zeros((PITCH - HDIM,), F32)
    head_gain = jnp.concatenate([query_gain, pad] * 4 + [key_gain, pad] * 2).reshape(1, 768)
    router = router_weight.T

    chunks = [layer_input] + [shift_mp(layer_input, -s) for s in (1, 2, 3)]
    chunk_at = [(mp_at + r) % 4 for r in range(4)]
    shard = jnp.concatenate([query_weight, key_value_weight.reshape(32, 256), out_weight], axis=0)
    proj, out_w = gather_weights(shard, jnp.stack([y_at, z_at, core]))

    packed, ranks = call(
        start_body,
        [((ROWS, WIDTH), BF16), ((EXPERTS, TOK), F32)],
        (cotangent, routes),
        scalars=jnp.stack([mp_at, length]),
    )
    cot_all = lax.all_gather(packed, "dp", axis=0, tiled=False, axis_index_groups=PLANES)
    weights_own = (gate_weight, up_weight, down_weight)
    weights_other = tuple(shift_yz(w, 0, 0, 1) for w in weights_own)

    h1, qa, ka, va, raw = [], [], [], [], []
    for r in range(4):
        made = call(
            project_body,
            [
                ((TOK, WIDTH), BF16),
                ((TOK, 512), BF16),
                ((TOK, 256), BF16),
                ((TOK, 256), BF16),
                ((TOK, 768), F32),
            ],
            (chunks[r], attn_row, proj, head_gain, cos_tab, sin_tab),
            scalars=jnp.stack([chunk_at[r], length]),
        )
        for store, one in zip((h1, qa, ka, va, raw), made):
            store.append(one)

    branch, mixed, qb = [None] * 4, [None] * 4, [None] * 4
    for r in (2, 1, 3, 0):
        branch[r], mixed[r], qb[r] = call(
            attend_body,
            [((TOK, WIDTH), BF16), ((TOK, 512), BF16), ((TOK, 512), BF16)],
            (qa[r], *ka, *va, out_w),
        )
    arrived = [branch[0]] + [shift_mp(branch[r], r) for r in (1, 2, 3)]
    x_mid, h2 = call(
        middle_body,
        [((TOK, WIDTH), F32), ((TOK, WIDTH), BF16)],
        (layer_input, *arrived, ffn_row),
    )
    (gates,) = call(gates_body, [((EXPERTS, TOK), F32)], (h2, router, ranks))

    plus, minus = shift_axis(h2, 0, -1), shift_axis(h2, 0, 1)
    far_a, far_b = shift_axis(plus[: TOK // 2], 0, -1), shift_axis(minus[TOK // 2 :], 0, 1)
    near = jnp.stack([h2, plus, minus, jnp.concatenate([far_a, far_b], axis=0)])
    unit_plus, unit_minus = shift_axis(near, 1, -1), shift_axis(near, 1, 1)
    unit_far_a, unit_far_b = shift_axis(unit_plus[:2], 1, -1), shift_axis(unit_minus[2:], 1, 1)
    units = [(near,), (unit_plus,), (unit_minus,), (unit_far_a, unit_far_b)]

    first_at = jnp.where(core == 0, y_at, z_at)
    second_at = jnp.where(core == 0, z_at, y_at)
    saved = None
    backs = []
    for u, step in enumerate(STEPS):
        second = (second_at + step + 4) % 4
        order = []
        for s in STEPS:
            first = (first_at + s + 4) % 4
            order.append(jnp.where(core == 0, first * 4 + second, second * 4 + first))
        sc = jnp.stack(order + [dp_at, dp_at + 1 - 2 * core]).astype(jnp.int32)
        pieces = tuple(one.shape[0] for one in units[u])
        args = (*units[u], cot_all, router, *weights_own, *weights_other)
        any_in = [len(pieces)]
        aliases = None
        if saved is not None:
            base = len(args)
            aliases = {base + i: (0 if i == 0 else i + 1) for i in range(6)}
            any_in += list(range(base, base + 6))
            args = args + tuple(saved)
        made = call(
            partial(experts_body, pieces, u),
            [
                ((16, TOK, WIDTH), BF16),
                ((4, ROWS, WIDTH), BF16),
                ((2, 16 * CAP, WIDTH), BF16),
                ((2, 16 * CAP, WIDTH), BF16),
                ((2, 16 * CAP, FF), BF16),
                ((2, 16 * CAP, FF), BF16),
                ((2, 16 * CAP, FF), BF16),
            ],
            args,
            scalars=sc,
            any_in=any_in,
            any_out=(0, 2, 3, 4, 5, 6),
            scratch=[
                pltpu.VMEM((4, ROWS, WIDTH), BF16),
                pltpu.VMEM((4, TOK, WIDTH), BF16),
                pltpu.VMEM((2, 4 * CAP, WIDTH), BF16),
                pltpu.VMEM((2, 4 * CAP, WIDTH), BF16),
                pltpu.VMEM((2, 4 * CAP, FF), BF16),
                pltpu.VMEM((2, 4 * CAP, FF), BF16),
                pltpu.VMEM((2, 4 * CAP, FF), BF16),
                pltpu.SemaphoreType.DMA((18,)),
            ],
            aliases=aliases,
        )
        backs.append(made[1])
        saved = [made[0]] + list(made[2:])
    y_out, taken, push, hidden, grad_gate, grad_up = saved

    b0, bp, bm, bf = backs
    half_a, half_b = shift_axis(bf[:2], 1, 1), shift_axis(bf[2:], 1, -1)
    plus_late, minus_late = add_low(bp[:2], half_a), add_low(bm[2:], half_b)
    plus_a, plus_b = shift_axis(plus_late, 1, 1), shift_axis(bp[2:], 1, 1)
    minus_a, minus_b = shift_axis(bm[:2], 1, -1), shift_axis(minus_late, 1, -1)
    line_a = add_low(b0[:2], plus_a, minus_a)
    line_b = add_low(b0[2:], plus_b, minus_b)
    cut = ROWS // 2 + 8
    far_up, far_down = shift_axis(line_b[1, :cut], 0, 1), shift_axis(line_b[1, cut:], 0, -1)
    send_up = jnp.concatenate([add_low(line_a[1, :cut], far_up), line_a[1, cut:]], axis=0)
    send_down = jnp.concatenate([line_b[0, :cut], add_low(line_b[0, cut:], far_down)], axis=0)
    got_up, got_down = shift_axis(send_up, 0, 1), shift_axis(send_down, 0, -1)
    grad_mid, grad_rows, small = call(
        token_back_body,
        [((TOK, WIDTH), F32), ((TOK, WIDTH), BF16), ((EXPERTS + 8, WIDTH), F32)],
        (line_a[0], got_up, got_down, h2, x_mid, ranks, gates, router, ffn_row, packed),
    )

    def both_experts(left, right):
        def one(e, dtype):
            return lax.dot_general(
                left[e], right[e], (((0,), (0,)), ((), ())), preferred_element_type=F32
            ).astype(dtype)

        return (one(0, F32) + shift_yz(one(1, BF16), 0, 0, 1).astype(F32)).astype(BF16)

    grad_gate_w = both_experts(taken, grad_gate)
    grad_up_w = both_experts(taken, grad_up)
    grad_down_w = both_experts(hidden, push)
    stacked = jnp.concatenate(
        [grad_gate_w.reshape(4, 256, FF), grad_up_w.reshape(4, 256, FF), grad_down_w.reshape(4, 256, FF)],
        axis=1,
    ).reshape(4 * 768, FF)
    expert_grads = lax.psum_scatter(stacked, "mp", scatter_dimension=0, tiled=True).astype(F32)

    rows = [grad_rows] + [shift_mp(grad_rows, -s) for s in (1, 2, 3)]
    both = None
    grad_query, query_gains = [None] * 4, [None] * 4
    for r in (0, 1, 3, 2):
        args = (rows[r], out_w, qb[r], mixed[r], *ka, *va, raw[r], head_gain, cos_tab, sin_tab)
        first = both is None
        grad_query[r], query_gains[r], both = call(
            partial(attend_back_body, first),
            [((TOK, 512), BF16), ((8, PITCH), F32), ((4, TOK, 512), F32)],
            args if first else args + (both,),
            scalars=chunk_at[r].reshape(1),
            aliases=None if first else {len(args): 2},
        )
    parts, slim, gains = [None] * 4, [None] * 4, [None] * 4
    for r in (2, 1, 3, 0):
        parts[r], slim[r], gains[r] = call(
            partial(finish_body, r),
            [((TOK, WIDTH), BF16), ((TOK, 512), BF16), ((8, WIDTH), F32)],
            (both, raw[r], head_gain, cos_tab, sin_tab, grad_query[r], chunks[r], proj, spread4, spread2),
            scalars=chunk_at[r].reshape(1),
        )
    arrived = [parts[0]] + [shift_mp(parts[r], r) for r in (1, 2, 3)]
    (input_grad,) = call(
        input_body, [((TOK, WIDTH), F32)], (*arrived, layer_input, attn_row, grad_mid)
    )
    (weight_part,) = call(
        weight_body, [((WIDTH, 768), BF16)], (*h1, *slim, *rows, *mixed, spread4)
    )
    shared = lax.all_to_all(
        weight_part.reshape(32, 32, 768), "dp", split_axis=0, concat_axis=0, tiled=True
    )
    weight_sum = jnp.sum(shared.astype(F32), axis=0)

    router_sum = all_sum(small)
    gain_part = sum(gains)
    query_gain_part = sum(query_gains)
    gain_sum = all_sum(jnp.concatenate([gain_part[0:2], jnp.pad(query_gain_part[0:1], ((0, 0), (0, WIDTH - PITCH)))]))

    returned = lax.psum_scatter(
        y_out.reshape(16 * TOK, WIDTH), "dp", scatter_dimension=0, tiled=True, axis_index_groups=PLANES
    )
    layer_output = (x_mid + returned.astype(F32)).astype(BF16)

    return (
        layer_output,
        input_grad,
        gain_sum[0],
        gain_sum[2, :HDIM],
        gain_sum[1, :HDIM],
        weight_sum[:, 0:256],
        weight_sum[:, 256:512].reshape(32, 2, 128),
        weight_sum[:, 512:768],
        router_sum[EXPERTS],
        router_sum[:EXPERTS].T,
        expert_grads[0:256].reshape(1, 256, FF),
        expert_grads[256:512].reshape(1, 256, FF),
        expert_grads[512:768].reshape(1, 128, WIDTH),
    )


def solution(mesh):
    tokens = P(("dp", "mp"), None)
    in_specs = (
        tokens,
        P("dp"),
        tokens,
        P(),
        P(),
        P(),
        P("dp", "mp"),
        P("dp", None, "mp"),
        P("dp", "mp"),
        P(),
        P(),
        P("dp", None, None),
        P("dp", None, None),
        P("dp", None, None),
        tokens,
    )
    out_specs = (
        tokens,
        tokens,
        P(),
        P(),
        P(),
        P("dp", "mp"),
        P("dp", None, "mp"),
        P("dp", "mp"),
        P(),
        P(),
        P("dp", "mp", None),
        P("dp", "mp", None),
        P("dp", "mp", None),
    )
    return jax.shard_map(shards, mesh=mesh, in_specs=in_specs, out_specs=out_specs, check_vma=False)
```

```python
from functools import partial

import jax
import jax.numpy as jnp
import numpy as np
from jax import lax
from jax.experimental import pallas as pl
from jax.experimental.pallas import tpu as pltpu
from jax.sharding import PartitionSpec as P

WIDTH = 1024
HDIM = 64
PITCH = 128
LEN = 1024
TOK = 256
CAP = 96
EXPERTS = 32
FF = 512
SIDE = 16
ROWS = TOK + SIDE
EPS = 1e-06
LOG2E = 1.4426950408889634
F32 = jnp.float32
BF16 = jnp.bfloat16


def nn(left, right):
    return lax.dot_general(left, right, (((1,), (0,)), ((), ())), preferred_element_type=F32)


def nt(left, right):
    return lax.dot_general(left, right, (((1,), (1,)), ((), ())), preferred_element_type=F32)


def tn(left, right):
    return lax.dot_general(left, right, (((0,), (0,)), ((), ())), preferred_element_type=F32)


def spread(heads):
    table = np.zeros((heads * HDIM, heads * PITCH), np.float32)
    for head in range(heads):
        for lane in range(HDIM):
            table[head * HDIM + lane, head * PITCH + lane] = 1.0
    return table


def rope_tables():
    places = np.arange(LEN, dtype=np.float64)
    inverse = 10000.0 ** (-2.0 * np.arange(HDIM // 2, dtype=np.float64) / HDIM)
    angles = places[:, None] * inverse[None, :]
    cos_tab = np.zeros((LEN, PITCH), np.float32)
    sin_tab = np.zeros((LEN, PITCH), np.float32)
    cos_tab[:, : HDIM // 2] = np.cos(angles)
    cos_tab[:, HDIM // 2 : HDIM] = np.cos(angles)
    sin_tab[:, : HDIM // 2] = -np.sin(angles)
    sin_tab[:, HDIM // 2 : HDIM] = np.sin(angles)
    return cos_tab.reshape(LEN // TOK, TOK, PITCH), sin_tab.reshape(LEN // TOK, TOK, PITCH)


def lanes(shape):
    return lax.broadcasted_iota(jnp.int32, shape, 1)


def swap_halves(tensor):
    half = HDIM // 2
    ahead = pltpu.roll(tensor, PITCH - half, 1)
    behind = pltpu.roll(tensor, half, 1)
    return jnp.where(lanes(tensor.shape) < half, ahead, behind)


def head_scale(tensor):
    return lax.rsqrt(jnp.sum(tensor * tensor, axis=1, keepdims=True) * (1.0 / HDIM) + EPS)


def row_scale(tensor):
    return lax.rsqrt(jnp.mean(tensor * tensor, axis=1, keepdims=True) + EPS)


def call(body, out_shape, args, scalars=None, any_in=(), any_out=(), scratch=(), aliases=None, near=(), local=(), mb=24, lazy=False):
    scratch, aliases = list(scratch), aliases or {}
    offset = 0 if scalars is None else 1
    count = offset + len(args)
    fetched = [i for i in range(len(args)) if i not in any_in and i not in local]
    stored = [i for i in range(len(out_shape)) if i not in any_out and i not in near]
    holds = [pltpu.VMEM(args[i].shape, args[i].dtype) for i in fetched]
    holds += [pltpu.VMEM(*out_shape[i]) for i in stored]
    scratch = [*scratch, *holds, pltpu.SemaphoreType.DMA((max(1, len(holds)),))]

    def kernel(*refs):
        refs = list(refs)
        own, sems = refs[len(refs) - len(holds) - 1 : -1], refs[-1]
        refs = refs[: len(refs) - len(holds) - 1]
        copies = {}
        for n, i in enumerate(fetched):
            copies[i] = pltpu.make_async_copy(refs[i + offset], own[n], sems.at[n])
            copies[i].start()
            refs[i + offset] = own[n]
        stores = []
        for n, i in enumerate(stored, len(fetched)):
            stores.append(pltpu.make_async_copy(own[n], refs[i + count], sems.at[n]))
            refs[i + count] = own[n]
        if lazy:
            body(*refs, wait=lambda *which: [copies.pop(i).wait() for i in which])
        else:
            for one in copies.values():
                one.wait()
            body(*refs)
        for one in stores:
            one.start()
        for one in stores:
            one.wait()

    def placed(i, one):
        if i in any_in and i not in aliases:
            return one
        return pltpu.with_memory_space_constraint(one, pltpu.VMEM if i in local else pltpu.HBM)

    def space(i):
        return pltpu.VMEM if i in local else pl.ANY if i in any_in and i not in aliases else pltpu.HBM

    args = [placed(i, one) for i, one in enumerate(args)]
    in_specs = [pl.BlockSpec(memory_space=space(i)) for i in range(len(args))]
    out_specs = [pl.BlockSpec(memory_space=pltpu.VMEM if i in near else pltpu.HBM) for i in range(len(out_shape))]
    shapes = [pltpu.VMEM(s, d) if i in near else pltpu.HBM(s, d) for i, (s, d) in enumerate(out_shape)]
    if scalars is not None:
        in_specs = [pl.BlockSpec(memory_space=pltpu.SMEM)] + in_specs
        args = [scalars] + args
    return pl.pallas_call(
        kernel,
        out_shape=shapes,
        in_specs=in_specs,
        out_specs=out_specs,
        scratch_shapes=scratch,
        input_output_aliases={i + offset: o for i, o in aliases.items()},
        compiler_params=pltpu.CompilerParams(vmem_limit_bytes=mb * 1024 * 1024),
        cost_estimate=pl.CostEstimate(flops=1, bytes_accessed=1, transcendentals=0),
    )(*args)


def start_body(sc, cot, routes, packed, ranks_out):
    base = sc[0] * TOK
    length = sc[1]
    place = base + lax.broadcasted_iota(jnp.int32, (TOK, 1), 0)
    keep = jnp.where(place < length, 1.0, 0.0)
    packed[0:TOK, :] = (cot[...].astype(F32) * keep).astype(BF16)
    names = lax.broadcasted_iota(jnp.int32, (TOK, EXPERTS), 1)
    member = jnp.zeros((TOK, EXPERTS), F32)
    for k in range(routes.shape[1]):
        member = member + jnp.where(routes[:, k : k + 1] == names, 1.0, 0.0)
    member = member.astype(BF16)
    earlier = lax.broadcasted_iota(jnp.int32, (TOK, TOK), 0)
    later = lax.broadcasted_iota(jnp.int32, (TOK, TOK), 1)
    before = jnp.where(earlier < later, 1.0, 0.0).astype(BF16)
    same = jnp.where(earlier == later, 1.0, 0.0).astype(BF16)
    counts = tn(member, before)
    chosen = tn(member, same)
    ranks = jnp.where(chosen > 0.5, counts, -1.0)
    ranks_out[...] = ranks
    quarter = EXPERTS // 4
    rows = jnp.concatenate([ranks[q * quarter : (q + 1) * quarter] for q in range(4)], axis=1)
    packed[TOK:ROWS, :] = jnp.concatenate([rows, jnp.zeros_like(rows)], axis=0).astype(BF16)


def project_body(sc, own, other, x0, x1, x2, x3, gain, head_gain, cos, sin, spread4, spread2, *refs, wait):
    wait(0, 1)
    outs, raws, pairs, queries, ka, va, out_w, turns = (
        refs[:2], refs[2:6], refs[6:10], refs[10:14], refs[14], refs[15], refs[16], refs[17:21]
    )
    h1, raw_hold, pair_hold, proj, held, sems = refs[21:]
    y_at, z_at, core, mp_at, length = sc[0], sc[1], sc[2], sc[3], sc[4]
    for block in range(16):
        y_rel = (block // 4 - y_at + 4) % 4
        z_rel = (block % 4 - z_at + 4) % 4
        for side in range(2):
            rel = z_rel * 4 + y_rel if side == 0 else y_rel * 4 + z_rel
            part = jnp.where(core == side, own[rel].astype(F32), other[rel].astype(F32)).astype(BF16)
            at = (2 * block + side) * 32
            for piece in range(3):
                held[at : at + 32, piece * 256 : (piece + 1) * 256] = part[piece * 32 : (piece + 1) * 32]
    wait(10, 11)
    proj[:, 0:512] = nn(held[:, 0:256], spread4[...]).astype(BF16)
    proj[:, 512:768] = nn(held[:, 256:384], spread2[...]).astype(BF16)
    proj[:, 768:1024] = nn(held[:, 384:512], spread2[...]).astype(BF16)
    out_w[...] = nn(held[:, 512:768], spread4[...]).astype(BF16)
    copies = [pltpu.make_async_copy(proj, outs[1], sems.at[12])]
    copies[0].start()
    lane = lanes((TOK, PITCH))
    below = lax.broadcasted_iota(jnp.int32, (TOK, PITCH), 0)
    q_aug = jnp.where(lane == HDIM, 1.0, 0.0)
    v_aug = jnp.where(lane < HDIM + 2, 1.0, 0.0)
    for chunk, x in enumerate((x0, x1, x2, x3)):
        rows = slice(chunk * TOK, (chunk + 1) * TOK)
        at = (mp_at + chunk) % 4
        wait(*((2, 6, 7, 8, 9) if chunk == 0 else (2 + chunk,)))
        xf = x[...].astype(F32)
        normed = (xf * row_scale(xf) * gain[...]).astype(BF16)
        h1[rows, :] = normed
        raw = nn(normed, proj[...])
        raw_hold[rows, :] = raw[:, 0:512]
        pair_hold[rows, :] = raw[:, 512:768]
        cos_t = cos[at]
        sin_t = sin[at]
        turns[chunk][...] = jnp.where(lane < HDIM, cos_t, pltpu.roll(sin_t, HDIM, 1))
        bias = jnp.where(at * TOK + below < length, 0.0, -1e30)
        k_aug = jnp.where(lane == HDIM, bias, jnp.where(lane < HDIM + 4, 1.0, 0.0))
        for head in range(6):
            cols = slice(head * PITCH, (head + 1) * PITCH)
            one = raw[:, cols]
            ready = one * head_scale(one) * head_gain[:, cols]
            turned = ready * cos_t + swap_halves(ready) * sin_t
            if head < 4:
                queries[chunk][:, cols] = jnp.where(lane < HDIM, turned, q_aug).astype(BF16)
            else:
                here = slice((head - 4) * PITCH, (head - 3) * PITCH)
                ka[rows, here] = jnp.where(lane < HDIM, turned, k_aug).astype(BF16)
        for head in range(2):
            va[rows, head * PITCH : (head + 1) * PITCH] = jnp.where(
                lane < HDIM, raw[:, 768 + head * PITCH : 768 + (head + 1) * PITCH], v_aug
            ).astype(BF16)
        here = pl.ds(chunk * TOK, TOK)
        for index, (hold, target) in enumerate(
            ((h1, outs[0].at[here]), (raw_hold, raws[chunk]), (pair_hold, pairs[chunk]))
        ):
            one = pltpu.make_async_copy(hold.at[here], target, sems.at[chunk * 3 + index])
            one.start()
            copies.append(one)
    for one in copies:
        one.wait()


def turn_tables(turn):
    lane = lanes(turn.shape)
    return jnp.where(lane < HDIM, turn, 0.0), jnp.where(lane < HDIM, pltpu.roll(turn, HDIM, 1), 0.0)


def attend_body(qa, ka, va, out_w, branch, mixed, qb):
    lane = lanes((TOK, PITCH))
    for head in range(4):
        cols = slice(head * PITCH, (head + 1) * PITCH)
        kv = slice((head // 2) * PITCH, (head // 2 + 1) * PITCH)
        query = qa[:, cols]
        weight = jnp.exp2(nt(query, ka[:, kv]) * (LOG2E / 8.0)).astype(BF16)
        total = nn(weight, va[:, kv])
        denom = total[:, HDIM : HDIM + 1]
        mixed[:, cols] = jnp.where(lane < HDIM, total / denom, 0.0).astype(BF16)
        level = jnp.log(denom) * -8.0
        high = level.astype(BF16).astype(F32)
        middle = (level - high).astype(BF16).astype(F32)
        low = level - high - middle
        stats = jnp.where(lane == HDIM + 1, high, jnp.where(lane == HDIM + 2, middle, low))
        qb[:, cols] = jnp.where(
            (lane > HDIM) & (lane < HDIM + 4), stats, query.astype(F32)
        ).astype(BF16)
    branch[...] = nt(mixed[...], out_w[...]).astype(BF16)


def middle_body(x, p0, p1, p2, p3, gain, x_mid, h2):
    total = (
        x[...].astype(F32)
        + ((p0[...].astype(F32) + p1[...].astype(F32)) + (p2[...].astype(F32) + p3[...].astype(F32)))
    )
    x_mid[...] = total
    h2[...] = (total * row_scale(total) * gain[...]).astype(BF16)


def gates_of(logits, ranks):
    routed = ranks >= 0.0
    masked = jnp.where(routed, logits, -1e30)
    weight = jnp.where(routed, jnp.exp(masked - jnp.max(masked, axis=0, keepdims=True)), 0.0)
    return weight / jnp.sum(weight, axis=0, keepdims=True)


def gates_body(h2, router, ranks, gates):
    gates[...] = gates_of(nt(router[...], h2[...]), ranks[...])


def unfold(rows):
    return jnp.concatenate([rows[:, q * TOK : (q + 1) * TOK] for q in range(4)], axis=0)


def experts_body(pieces, unit, *refs):
    sc = refs[0]
    tokens = refs[1 : 1 + len(pieces)]
    at = 1 + len(pieces)
    cot_all, router = refs[at], refs[at + 1]
    weights_in = refs[at + 2 : at + 8]
    at = at + 8
    if unit > 0:
        at = at + 6
    y_out, back_a, back_b, taken_all, push_all, hidden_all, gate_all, up_all = refs[at : at + 8]
    (tok, cot, gate_v, up_v, down_v, y_hold, y_back, t_hold, e_hold, h_hold, g_hold, u_hold, sems) = refs[at + 8 :]
    cot_in = [pltpu.make_async_copy(cot_all.at[sc[i]], cot.at[i], sems.at[i]) for i in range(4)]
    tok_in = []
    for index, count in enumerate(pieces):
        for j in range(count):
            i = len(tok_in)
            tok_in.append(pltpu.make_async_copy(tokens[index].at[j], tok.at[i], sems.at[4 + i]))
    weight_in = []
    for e in range(2):
        for j, hold in enumerate((gate_v, up_v, down_v)):
            weight_in.append(
                pltpu.make_async_copy(weights_in[3 * e + j].at[0], hold.at[e], sems.at[8 + 3 * e + j])
            )
    for one in cot_in + tok_in + weight_in:
        one.start()
    own_names = (sc[4], sc[5])
    names = lax.broadcasted_iota(jnp.int32, (EXPERTS, TOK), 0)
    slots = lax.broadcasted_iota(jnp.int32, (CAP, TOK), 0).astype(F32)
    picks = [[], []]
    gate_rows = [[], []]
    for i in range(4):
        cot_in[i].wait()
        tok_in[i].wait()
        block = tok[i]
        ranks = unfold(cot[i, TOK : TOK + EXPERTS // 4, :].astype(F32))
        gates = gates_of(nt(router[...], block), ranks)
        for e in range(2):
            hit = names == own_names[e]
            rank = jnp.sum(jnp.where(hit, ranks, 0.0), axis=0, keepdims=True)
            gate = jnp.sum(jnp.where(hit, gates, 0.0), axis=0, keepdims=True)
            pick = jnp.where(slots == rank, 1.0, 0.0)
            picks[e].append(pick.astype(BF16))
            gate_rows[e].append(jnp.sum(pick * gate, axis=1, keepdims=True))
    taken_rows = [nn(jnp.concatenate([picks[0][i], picks[1][i]], axis=0), tok[i]) for i in range(4)]
    grad_rows_all = [
        nn(jnp.concatenate([picks[0][i], picks[1][i]], axis=0), cot[i, 0:TOK, :]) for i in range(4)
    ]
    marks = [[], []]
    back_parts = []
    out_parts = []
    copies_out = []

    def put(source, target, sem):
        one = pltpu.make_async_copy(source, target, sems.at[sem])
        one.start()
        copies_out.append(one)

    for e in range(2):
        half = slice(e * CAP, (e + 1) * CAP)
        here = pl.ds(unit * 4 * CAP, 4 * CAP)
        for i in range(4):
            t_hold[e, i * CAP : (i + 1) * CAP, :] = taken_rows[i][half].astype(BF16)
        put(t_hold.at[e], taken_all.at[e, here], 14 + 5 * e)
        taken = t_hold[e]
        for one in weight_in[3 * e : 3 * e + 2]:
            one.wait()
        gate_act = nn(taken, gate_v[e])
        up_act = nn(taken, up_v[e])
        sigma = jax.nn.sigmoid(gate_act)
        silu = gate_act * sigma
        hidden = (silu * up_act).astype(BF16)
        h_hold[e] = hidden
        put(h_hold.at[e], hidden_all.at[e, here], 15 + 5 * e)
        weight_in[3 * e + 2].wait()
        result = nn(hidden, down_v[e]).astype(BF16).astype(F32)
        gate_col = jnp.concatenate(gate_rows[e], axis=0)
        grad_rows = jnp.concatenate([grad_rows_all[i][half] for i in range(4)], axis=0)
        mark = jnp.sum(grad_rows * result, axis=1, keepdims=True)
        for i in range(4):
            marks[e].append(
                jnp.sum(picks[e][i].astype(F32) * mark[i * CAP : (i + 1) * CAP], axis=0, keepdims=True)
            )
        out_parts.append((result * gate_col).astype(BF16))
        push = (grad_rows * gate_col).astype(BF16)
        e_hold[e] = push
        put(e_hold.at[e], push_all.at[e, here], 16 + 5 * e)
        grad_hidden = nt(push, down_v[e])
        grad_gate = (grad_hidden * up_act * (sigma * (1.0 + gate_act * (1.0 - sigma)))).astype(BF16)
        grad_up = (grad_hidden * silu).astype(BF16)
        g_hold[e] = grad_gate
        u_hold[e] = grad_up
        put(g_hold.at[e], gate_all.at[e, here], 17 + 5 * e)
        put(u_hold.at[e], up_all.at[e, here], 18 + 5 * e)
        back_parts.append((nt(grad_gate, gate_v[e]) + nt(grad_up, up_v[e])).astype(BF16))
    for i in range(4):
        pick = jnp.concatenate([picks[0][i], picks[1][i]], axis=0)
        rows = slice(i * CAP, (i + 1) * CAP)
        y_back[i, 0:TOK, :] = tn(
            pick, jnp.concatenate([back_parts[0][rows], back_parts[1][rows]], axis=0)
        ).astype(BF16)
        mark = jnp.where(names == own_names[0], marks[0][i], 0.0) + jnp.where(
            names == own_names[1], marks[1][i], 0.0
        )
        high = mark.astype(BF16).astype(F32)
        low = mark - high
        quarter = EXPERTS // 4
        fold = [
            jnp.concatenate([part[q * quarter : (q + 1) * quarter] for q in range(4)], axis=1)
            for part in (high, low)
        ]
        y_back[i, TOK:ROWS, :] = jnp.concatenate(fold, axis=0).astype(BF16)
        put(y_back.at[i], (back_a if i < 2 else back_b).at[i % 2], 24 + i)
    for i in range(4):
        pick = jnp.concatenate([picks[0][i], picks[1][i]], axis=0)
        rows = slice(i * CAP, (i + 1) * CAP)
        y_hold[i] = tn(pick, jnp.concatenate([out_parts[0][rows], out_parts[1][rows]], axis=0)).astype(BF16)
        put(y_hold.at[i], y_out.at[sc[i]], 28 + i)
    for one in copies_out:
        one.wait()


def expert_weights_body(joined, sc, taken, push, hidden, gate, up, *refs):
    got, refs = (refs[:3], refs[3:]) if joined else ((), refs)
    outs, (gate_sum, up_sum, down_sum) = refs[:-3], refs[-3:]
    step = pl.program_id(0)

    @pl.when(step == 0)
    def _():
        gate_sum[...] = tn(taken[0], gate[0])
        up_sum[...] = tn(taken[0], up[0])
        down_sum[...] = tn(hidden[0], push[0])

    @pl.when(step > 0)
    def _():
        gate_sum[...] += tn(taken[0], gate[0])
        up_sum[...] += tn(taken[0], up[0])
        down_sum[...] += tn(hidden[0], push[0])

    @pl.when(step == pl.num_programs(0) - 1)
    def _():
        if not joined:
            for target, total in zip(outs, (gate_sum, up_sum, down_sum)):
                target[...] = total[...].astype(BF16)
            return
        for part in range(4):
            at = (sc[0] + part) % 4
            out = outs[part]
            rows = pl.ds(pl.multiple_of(at * 256, 256), 256)
            out[0:256, :] = (gate_sum[rows, :] + got[0][rows, :].astype(F32)).astype(BF16)
            out[256:512, :] = (up_sum[rows, :] + got[1][rows, :].astype(F32)).astype(BF16)
            rows = pl.ds(pl.multiple_of(at * 128, 128), 128)
            down = (down_sum[rows, :] + got[2][rows, :].astype(F32)).astype(BF16)
            out[512:640, :] = down[:, 0:FF]
            out[640:768, :] = down[:, FF:WIDTH]


def expert_weights(saved, expert, mp_at, got=()):
    widths = [one.shape[2] for one in saved]
    saved = [pltpu.with_memory_space_constraint(one, pltpu.HBM) for one in saved]
    got = [pltpu.with_memory_space_constraint(one, pltpu.VMEM) for one in got]
    rows = 4 * CAP
    shapes = [((768, FF), BF16)] * 4 if got else [((WIDTH, FF), BF16), ((WIDTH, FF), BF16), ((FF, WIDTH), BF16)]
    return pl.pallas_call(
        partial(expert_weights_body, bool(got)),
        out_shape=[jax.ShapeDtypeStruct(s, d) for s, d in shapes],
        grid=(4,),
        in_specs=[pl.BlockSpec(memory_space=pltpu.SMEM)]
        + [pl.BlockSpec((1, rows, w), lambda step: (expert, step, 0)) for w in widths]
        + [pl.BlockSpec(memory_space=pltpu.VMEM) for _ in got],
        out_specs=[pl.BlockSpec(memory_space=pltpu.VMEM) for _ in shapes],
        scratch_shapes=[pltpu.VMEM((WIDTH, FF), F32), pltpu.VMEM((WIDTH, FF), F32), pltpu.VMEM((FF, WIDTH), F32)],
        compiler_params=pltpu.CompilerParams(vmem_limit_bytes=40 * 1024 * 1024),
        cost_estimate=pl.CostEstimate(flops=1, bytes_accessed=1, transcendentals=0),
    )(mp_at.reshape(1), *saved, *got)


def token_back_body(r0, r1, r2, h2, x_mid, ranks, gates, router, gain, packed, grad_mid, branch, small):
    total = r0[...].astype(F32) + (r1[...].astype(F32) + r2[...].astype(F32))
    marks = unfold(total[TOK : TOK + 8]) + unfold(total[TOK + 8 : TOK + 16])
    gate = gates[...]
    centre = jnp.sum(gate * marks, axis=0, keepdims=True)
    grad_logits = jnp.where(ranks[...] >= 0.0, gate * (marks - centre), 0.0).astype(BF16)
    small[0:EXPERTS, :] = nn(grad_logits, h2[...])
    grad_h2 = total[0:TOK] + tn(grad_logits, router[...])
    x = x_mid[...]
    scale = row_scale(x)
    normed = x * scale
    grad_normed = grad_h2 * gain[...]
    small[EXPERTS : EXPERTS + 8, :] = jnp.broadcast_to(
        jnp.sum(grad_h2 * normed, axis=0, keepdims=True), (8, WIDTH)
    )
    out = packed[0:TOK, :].astype(F32) + scale * (
        grad_normed - normed * jnp.mean(grad_normed * normed, axis=1, keepdims=True)
    )
    grad_mid[...] = out
    branch[...] = out.astype(BF16)


def head_back(grad, raw, gain, cos_t, sin_t):
    upstream = grad * cos_t - swap_halves(grad) * sin_t
    scale = head_scale(raw)
    normed = raw * scale
    grad_normed = upstream * gain
    gain_grad = jnp.sum(upstream * normed, axis=0, keepdims=True)
    inner = jnp.sum(grad_normed * normed, axis=1, keepdims=True) * (1.0 / HDIM)
    return scale * (grad_normed - normed * inner), gain_grad


def attend_back_body(first, *refs, wait):
    rows, out_w, qb, mixed, ka, va, raw, head_gain, turn, spread4 = refs[:10]
    rest = refs[10:] if first else refs[11:]
    grad_query, gain_out, slim, both_out, both, sems = rest
    loads = []
    if not first:
        loads = [pltpu.make_async_copy(refs[10].at[g], both.at[g], sems.at[g]) for g in range(2)]
        for one in loads:
            one.start()
    stores = [pltpu.make_async_copy(both.at[g], both_out.at[g], sems.at[2 + g]) for g in range(2)]
    lane = lanes((TOK, PITCH))
    pushed = nn(rows[...], out_w[...]).astype(BF16)
    gain_total = jnp.zeros((1, PITCH), F32)
    wait(2, 3)
    for head in range(4):
        cols = slice(head * PITCH, (head + 1) * PITCH)
        group = head // 2
        kv = slice(group * PITCH, (group + 1) * PITCH)
        grad = pushed[:, cols]
        grad_f = grad.astype(F32)
        delta = -jnp.sum(grad_f * mixed[:, cols].astype(F32), axis=1, keepdims=True)
        high = delta.astype(BF16).astype(F32)
        grad_aug = jnp.where(
            lane == HDIM, high, jnp.where(lane == HDIM + 1, delta - high, grad_f)
        ).astype(BF16)
        query = qb[:, cols]
        probs = jnp.exp2(nt(ka[:, kv], query) * (LOG2E / 8.0))
        inner = nt(va[:, kv], grad_aug)
        grad_scores = (probs * inner).astype(BF16)
        add_k = nn(grad_scores, query)
        add_v = nn(probs.astype(BF16), grad)
        if head % 2 == 0 and first:
            both[group, :, 0:PITCH] = add_k
            both[group, :, PITCH : 2 * PITCH] = add_v
        else:
            if head % 2 == 0:
                loads[group].wait()
            both[group, :, 0:PITCH] += add_k
            both[group, :, PITCH : 2 * PITCH] += add_v
        if head % 2 == 1:
            stores[group].start()
        grad_q = jnp.where(lane < HDIM, tn(grad_scores, ka[:, kv]) * 0.125, 0.0)
        if head == 0:
            wait(6, 7, 8)
            cos_t, sin_t = turn_tables(turn[...])
        back, gain_grad = head_back(grad_q, raw[:, cols], head_gain[:, cols], cos_t, sin_t)
        grad_query[:, cols] = back.astype(BF16)
        gain_total = gain_total + gain_grad
    wait(9)
    slim[...] = nt(grad_query[...], spread4[...]).astype(BF16)
    gain_out[...] = jnp.broadcast_to(gain_total, (8, PITCH))
    for one in stores:
        one.wait()


def keys_back_body(*refs, wait):
    both, raws, turns, head_gain, query, proj, x = refs[0], refs[1:5], refs[5:9], refs[9], refs[10], refs[11], refs[12]
    far_up, far_down, wide, gains = refs[13:]
    half = TOK // 2
    lane = lanes((TOK, PITCH))
    key_gain = jnp.zeros((1, PITCH), F32)
    wait(0, 9)
    for chunk in (2, 0, 1, 3):
        wait(1 + chunk, 5 + chunk)
        at = slice(chunk * TOK, (chunk + 1) * TOK)
        cos_t, sin_t = turn_tables(turns[chunk][...])
        for head in range(2):
            cols = slice(head * PITCH, (head + 1) * PITCH)
            grad = jnp.where(lane < HDIM, both[head, at, 0:PITCH] * 0.125, 0.0)
            back, gain_grad = head_back(
                grad, raws[chunk][:, cols], head_gain[:, 512 + head * PITCH : 640 + head * PITCH], cos_t, sin_t
            )
            wide[at, cols] = back.astype(BF16)
            key_gain = key_gain + gain_grad
            wide[at, 256 + head * PITCH : 384 + head * PITCH] = jnp.where(
                lane < HDIM, both[head, at, PITCH : 2 * PITCH], 0.0
            ).astype(BF16)
    wait(10, 11, 12)
    part = nt(query[...], proj[:, 0:512]) + nt(wide[2 * TOK : 3 * TOK, :], proj[:, 512:1024])
    far_up[...] = part[:half].astype(BF16)
    far_down[...] = part[half:].astype(BF16)
    xf = x[...].astype(F32)
    gains[...] = jnp.zeros((8, WIDTH), F32)
    gains[0:1, :] = jnp.sum(part * (xf * row_scale(xf)), axis=0, keepdims=True)
    gains[1:2, 0:PITCH] = key_gain


def tail_body(*refs, wait):
    sc, refs = refs[0], refs[1:]
    wide, gains_in, small, spread2, spread4 = refs[0:5]
    queries, proj, xs, rows, mixed, h1, slims, query_gains = (
        refs[5:8], refs[8], refs[9:12], refs[12:16], refs[16:20], refs[20], refs[21:25], refs[25:29]
    )
    p1, p3, p0, keep, send, extra = refs[29:35]
    (slim_pair,) = refs[35:]
    y_at, z_at, core = sc[0], sc[1], sc[2]
    total = gains_in[0:1, :]
    wait(8)
    for n, (chunk, target) in enumerate(((1, p1), (3, p3), (0, p0))):
        wait(5 + n, 9 + n)
        at = slice(chunk * TOK, (chunk + 1) * TOK)
        part = nt(queries[n][...], proj[:, 0:512]) + nt(wide[at, :], proj[:, 512:1024])
        target[...] = part.astype(BF16)
        xf = xs[n][...].astype(F32)
        total = total + jnp.sum(part * (xf * row_scale(xf)), axis=0, keepdims=True)
    wait(2, 25, 26, 27, 28)
    query_gain = (query_gains[0][0:1, :] + query_gains[1][0:1, :]) + (
        query_gains[2][0:1, :] + query_gains[3][0:1, :]
    )
    extra[...] = jnp.zeros((56, 768), F32)
    extra[0:1, :] = total[:, 0:768]
    extra[1:2, 0:256] = total[:, 768:1024]
    extra[1:2, 256:384] = query_gain
    extra[1:2, 384:512] = gains_in[1:2, 0:PITCH]
    extra[8:56, :] = small[...]
    send[16] = split3(extra[0:4, :])
    send[17] = small[0:32, :].astype(BF16)
    send[18, 0:16, :] = small[32:48, :].astype(BF16)
    send[18, 16:32, :] = jnp.zeros((16, 768), BF16)
    wait(3, 4)
    slim_pair[:, 0:128] = nt(wide[:, 0:256], spread2[...]).astype(BF16)
    slim_pair[:, 128:256] = nt(wide[:, 256:512], spread2[...]).astype(BF16)
    wait(20)
    pair_rows = tn(h1[...], slim_pair[...]).astype(BF16)
    query_total = jnp.zeros((WIDTH, 256), F32)
    out_total = jnp.zeros((WIDTH, 256), F32)
    for chunk in range(4):
        wait(12 + chunk, 16 + chunk, 21 + chunk)
        at = slice(chunk * TOK, (chunk + 1) * TOK)
        query_total = query_total + tn(h1[at, :], slims[chunk][...])
        out_total = out_total + tn(rows[chunk][...], nt(mixed[chunk][...], spread4[...]).astype(BF16))
    query_rows, out_rows = query_total.astype(BF16), out_total.astype(BF16)
    for block in range(16):
        y_rel = (block // 4 - y_at + 4) % 4
        z_rel = (block % 4 - z_at + 4) % 4
        for side in range(2):
            at = (2 * block + side) * 32
            rel = y_rel * 4 + z_rel if side == 0 else z_rel * 4 + y_rel

            def put(target):
                target[rel, :, 0:256] = query_rows[at : at + 32]
                target[rel, :, 256:512] = pair_rows[at : at + 32]
                target[rel, :, 512:768] = out_rows[at : at + 32]

            pl.when(core == side)(partial(put, keep))
            pl.when(core != side)(partial(put, send))


def near_body(p1, p3, far_up, far_down, out1, out3):
    half = TOK // 2
    out1[:half, :] = (p1[:half, :].astype(F32) + far_up[...].astype(F32)).astype(BF16)
    out1[half:, :] = p1[half:, :]
    out3[:half, :] = p3[:half, :]
    out3[half:, :] = (p3[half:, :].astype(F32) + far_down[...].astype(F32)).astype(BF16)


def split3(value):
    high = value.astype(BF16).astype(F32)
    middle = (value - high).astype(BF16).astype(F32)
    low = value - high - middle
    return jnp.concatenate([high, middle, low, jnp.zeros((20, 768), F32)], axis=0).astype(BF16)


def join3(rows):
    value = rows.astype(F32)
    return value[0:4] + value[4:8] + value[8:12]


def ride_first_body(keep, got, extra, *outs):
    gain = split3(extra[0:4, :] + join3(got[16]))
    router = jnp.concatenate(
        [extra[8:40, :] + got[17].astype(F32), extra[40:56, :] + got[18, 0:16, :].astype(F32)], axis=0
    ).astype(BF16)
    for first in range(4):
        for second in range(4):
            at = first * 4 + second
            outs[first][second * 32 : (second + 1) * 32, :] = (
                keep[at].astype(F32) + got[at].astype(F32)
            ).astype(BF16)
        outs[first][128:160, :] = gain
        outs[first][160:208, :] = router


def add4(own, g1, g2, g3, start, stop):
    return own[start:stop, :].astype(F32) + (
        g1[start:stop, :].astype(F32) + (g2[start:stop, :].astype(F32) + g3[start:stop, :].astype(F32))
    )


def add_gains(own, g1, g2, g3, start):
    stop = start + 32
    return (join3(own[start:stop, :]) + join3(g1[start:stop, :])) + (
        join3(g2[start:stop, :]) + join3(g3[start:stop, :])
    )


def ride_second_body(own, g1, g2, g3, *outs):
    rows = add4(own, g1, g2, g3, 0, 128)
    gain = split3(add_gains(own, g1, g2, g3, 128))
    router = add4(own, g1, g2, g3, 160, 208).astype(BF16)
    for second in range(4):
        outs[second][0:32, :] = rows[second * 32 : (second + 1) * 32].astype(BF16)
        outs[second][32:64, :] = gain
        outs[second][64:112, :] = router


def ride_last_body(own, g1, g2, g3, rows, gain, router):
    rows[...] = add4(own, g1, g2, g3, 0, 32)
    gain[...] = add_gains(own, g1, g2, g3, 32)
    router[...] = add4(own, g1, g2, g3, 64, 112)


def input_body(p0, p1, p2, x, gain, grad_mid, out):
    upstream = p0[...].astype(F32) + (p1[...].astype(F32) + p2[...].astype(F32))
    xf = x[...].astype(F32)
    scale = row_scale(xf)
    normed = xf * scale
    grad_normed = upstream * gain[...]
    out[...] = grad_mid[...] + scale * (
        grad_normed - normed * jnp.mean(grad_normed * normed, axis=1, keepdims=True)
    )


def place_of(index):
    return index // 8, (index // 2) % 4, index % 2


def index_of(y, z, core):
    return (y % 4) * 8 + (z % 4) * 2 + core


def shift_yz(tensor, dy, dz, flip=0):
    pairs = []
    for d in range(32):
        y, z, core = place_of(d)
        pairs.append((d, index_of(y + dy, z + dz, core ^ flip)))
    return lax.ppermute(tensor, "dp", pairs)


def shift_axis(tensor, axis, step):
    pairs = []
    for d in range(32):
        y, z, core = place_of(d)
        if (core == 0) == (axis == 0):
            pairs.append((d, index_of(y + step, z, core)))
        else:
            pairs.append((d, index_of(y, z + step, core)))
    return lax.ppermute(tensor, "dp", pairs)


def shift_mp(tensor, step):
    return lax.ppermute(tensor, "mp", [(i, (i + step) % 4) for i in range(4)])


def gather_weights(shard, chunks):
    rows = jnp.stack([shard] + [shift_axis(shard, 0, -s) for s in (1, 2, 3)])
    own = jnp.concatenate([rows] + [shift_axis(rows, 1, -s) for s in (1, 2, 3)], axis=0)
    near = own
    own = after(own, chunks)
    return near, own, shift_yz(own, 0, 0, 1)


def gather_mp(tensor):
    plus, minus = shift_mp(tensor, -1), shift_mp(tensor, 1)
    half = tensor.shape[0] // 2
    far = jnp.concatenate([shift_mp(plus[:half], -1), shift_mp(minus[half:], 1)], axis=0)
    return [tensor, plus, far, minus]


def after(value, *others):
    return lax.optimization_barrier((value, others))[0]


def add_low(left, *others):
    total = left.astype(F32)
    for one in others:
        total = total + one.astype(F32)
    return total.astype(BF16)


PLANES = [[core + 2 * k for k in range(16)] for core in range(2)]
STEPS = (0, 1, -1, 2)


def shards(
    layer_input,
    lengths,
    routes,
    attn_gain,
    query_gain,
    key_gain,
    query_weight,
    key_value_weight,
    out_weight,
    ffn_gain,
    router_weight,
    gate_weight,
    up_weight,
    down_weight,
    cotangent,
):
    dp_at = lax.axis_index("dp").astype(jnp.int32)
    mp_at = lax.axis_index("mp").astype(jnp.int32)
    y_at, z_at, core = dp_at // 8, (dp_at // 2) % 4, dp_at % 2
    length = lengths[0].astype(jnp.int32)
    cos_np, sin_np = rope_tables()
    cos_tab, sin_tab = jnp.asarray(cos_np), jnp.asarray(sin_np)
    spread4, spread2 = jnp.asarray(spread(4), BF16), jnp.asarray(spread(2), BF16)
    attn_row = attn_gain.reshape(1, WIDTH)
    ffn_row = ffn_gain.reshape(1, WIDTH)
    pad = jnp.zeros((PITCH - HDIM,), F32)
    head_gain = jnp.concatenate([query_gain, pad] * 4 + [key_gain, pad] * 2).reshape(1, 768)
    router = router_weight.T

    chunks = gather_mp(layer_input)
    chunk_at = [(mp_at + r) % 4 for r in range(4)]
    shard = jnp.concatenate([query_weight, key_value_weight.reshape(32, 256), out_weight], axis=0)
    shards_near, shards_own, shards_other = gather_weights(shard, chunks)

    packed, ranks = call(
        start_body,
        [((ROWS, WIDTH), BF16), ((EXPERTS, TOK), F32)],
        after((cotangent, routes), shards_near),
        scalars=jnp.stack([mp_at, length]),
    )
    cot_all = lax.all_gather(packed, "dp", axis=0, tiled=False, axis_index_groups=PLANES)
    weights_own = (gate_weight, up_weight, down_weight)
    weights_other = tuple(shift_yz(after(w, shards_other), 0, 0, 1) for w in weights_own)

    out = call(
        project_body,
        [((LEN, WIDTH), BF16), ((WIDTH, 1024), BF16)]
        + [((TOK, 512), F32)] * 4
        + [((TOK, 256), F32)] * 4
        + [((TOK, 512), BF16)] * 4
        + [((LEN, 256), BF16), ((LEN, 256), BF16), ((WIDTH, 512), BF16)]
        + [((TOK, PITCH), F32)] * 4,
        (shards_own, shards_other, *chunks, attn_row, head_gain, cos_tab, sin_tab, spread4, spread2),
        scalars=jnp.stack([y_at, z_at, core, mp_at, length]),
        any_out=range(10),
        near=range(10, 17),
        scratch=[
            pltpu.VMEM((LEN, WIDTH), BF16),
            pltpu.VMEM((LEN, 512), F32),
            pltpu.VMEM((LEN, 256), F32),
            pltpu.VMEM((WIDTH, 1024), BF16),
            pltpu.VMEM((WIDTH, 768), BF16),
            pltpu.SemaphoreType.DMA((13,)),
        ],
        mb=40,
        lazy=True,
    )
    h1, proj, raw, raw_pair, qa = out[0], out[1], out[2:6], out[6:10], out[10:14]
    ka, va, out_w, turn_tab = out[14], out[15], out[16], out[17:21]

    qa = list(after(tuple(qa), weights_other))
    branch, mixed, qb = [None] * 4, [None] * 4, [None] * 4
    arrived = [None] * 4
    for r in (2, 1, 3, 0):
        if r == 0:
            qa[0] = after(qa[0], arrived[2])
        branch[r], mixed[r], qb[r] = call(
            attend_body,
            [((TOK, WIDTH), BF16), ((TOK, 512), BF16), ((TOK, 512), BF16)],
            (qa[r], ka, va, out_w),
            near=(0,),
            local=(0, 1, 2, 3),
        )
        arrived[r] = shift_mp(branch[r], r) if r else branch[r]
    x_mid, h2 = call(
        middle_body,
        [((TOK, WIDTH), F32), ((TOK, WIDTH), BF16)],
        (layer_input, *arrived, ffn_row),
        local=(1, 2, 3, 4),
    )
    (gates,) = call(gates_body, [((EXPERTS, TOK), F32)], (h2, router, ranks))

    plus, minus = shift_axis(h2, 0, -1), shift_axis(h2, 0, 1)
    far_a, far_b = shift_axis(plus[: TOK // 2], 0, -1), shift_axis(minus[TOK // 2 :], 0, 1)
    near_a, near_b = jnp.stack([h2, plus]), jnp.stack([minus, jnp.concatenate([far_a, far_b], axis=0)])
    plus_a, plus_b = shift_axis(near_a, 1, -1), shift_axis(near_b, 1, -1)
    minus_a, minus_b = shift_axis(near_a, 1, 1), shift_axis(near_b, 1, 1)
    units = [(near_a, near_b), (plus_a, plus_b), (minus_a, minus_b), None]

    first_at = jnp.where(core == 0, y_at, z_at)
    second_at = jnp.where(core == 0, z_at, y_at)
    saved = None
    backs = []
    for u, step in enumerate(STEPS):
        if u == 1:
            far_plus, far_minus = after((plus_a, minus_b), backs[0])
            units[3] = (shift_axis(far_plus, 1, -1), shift_axis(far_minus, 1, 1))
        second = (second_at + step + 4) % 4
        order = []
        for s in STEPS:
            first = (first_at + s + 4) % 4
            order.append(jnp.where(core == 0, first * 4 + second, second * 4 + first))
        sc = jnp.stack(order + [dp_at, dp_at + 1 - 2 * core]).astype(jnp.int32)
        pieces = tuple(one.shape[0] for one in units[u])
        args = (*units[u], cot_all, router, *weights_own, *weights_other)
        any_in = list(range(len(pieces) + 1)) + list(range(len(pieces) + 2, len(pieces) + 8))
        aliases = None
        if saved is not None:
            base = len(args)
            aliases = {base + i: (0 if i == 0 else i + 2) for i in range(6)}
            any_in += list(range(base, base + 6))
            args = args + tuple(saved)
        made = call(
            partial(experts_body, pieces, u),
            [
                ((16, TOK, WIDTH), BF16),
                ((2, ROWS, WIDTH), BF16),
                ((2, ROWS, WIDTH), BF16),
                ((2, 16 * CAP, WIDTH), BF16),
                ((2, 16 * CAP, WIDTH), BF16),
                ((2, 16 * CAP, FF), BF16),
                ((2, 16 * CAP, FF), BF16),
                ((2, 16 * CAP, FF), BF16),
            ],
            args,
            scalars=sc,
            any_in=any_in,
            any_out=range(8),
            scratch=[
                pltpu.VMEM((4, TOK, WIDTH), BF16),
                pltpu.VMEM((4, ROWS, WIDTH), BF16),
                pltpu.VMEM((2, WIDTH, FF), BF16),
                pltpu.VMEM((2, WIDTH, FF), BF16),
                pltpu.VMEM((2, FF, WIDTH), BF16),
                pltpu.VMEM((4, TOK, WIDTH), BF16),
                pltpu.VMEM((4, ROWS, WIDTH), BF16),
                pltpu.VMEM((2, 4 * CAP, WIDTH), BF16),
                pltpu.VMEM((2, 4 * CAP, WIDTH), BF16),
                pltpu.VMEM((2, 4 * CAP, FF), BF16),
                pltpu.VMEM((2, 4 * CAP, FF), BF16),
                pltpu.VMEM((2, 4 * CAP, FF), BF16),
                pltpu.SemaphoreType.DMA((32,)),
            ],
            aliases=aliases,
            mb=40,
        )
        backs.append(made[1:3])
        saved = [made[0]] + list(made[3:])
    y_out, taken, push, hidden, grad_gate, grad_up = saved

    (b0_a, b0_b), (bp_a, bp_b), (bm_a, bm_b), (bf_a, bf_b) = backs
    half_a, half_b = shift_axis(bf_a, 1, 1), shift_axis(bf_b, 1, -1)
    saved = (taken, push, hidden, grad_gate, grad_up)
    for_other = expert_weights(saved, 1, mp_at)
    from_other = [shift_yz(one, 0, 0, 1) for one in for_other]
    half_a, half_b = after((half_a, half_b), for_other)
    plus_late, minus_late = add_low(bp_a, half_a), add_low(bm_b, half_b)
    plus_a, plus_b = shift_axis(plus_late, 1, 1), shift_axis(bp_b, 1, 1)
    minus_a, minus_b = shift_axis(bm_a, 1, -1), shift_axis(minus_late, 1, -1)
    shard_grads = expert_weights(after(saved, plus_late, minus_late), 0, mp_at, from_other)
    b0_a, b0_b = after((b0_a, b0_b), shard_grads)
    line_a = add_low(b0_a, plus_a, minus_a)
    line_b = add_low(b0_b, plus_b, minus_b)
    cut = ROWS // 2 + 8
    far_up, far_down = shift_axis(line_b[1, :cut], 0, 1), shift_axis(line_b[1, cut:], 0, -1)
    send_up = jnp.concatenate([add_low(line_a[1, :cut], far_up), line_a[1, cut:]], axis=0)
    send_down = jnp.concatenate([line_b[0, :cut], add_low(line_b[0, cut:], far_down)], axis=0)
    got_up, got_down = shift_axis(send_up, 0, 1), shift_axis(send_down, 0, -1)
    shards_got = [shift_mp(shard_grads[step], step) for step in (1, 2, 3)]
    got_up, got_down = after((got_up, got_down), shards_got[0], shards_got[2])
    grad_mid, grad_rows, small = call(
        token_back_body,
        [((TOK, WIDTH), F32), ((TOK, WIDTH), BF16), ((EXPERTS + 8, WIDTH), F32)],
        (line_a[0], got_up, got_down, h2, x_mid, ranks, gates, router, ffn_row, packed),
        local=(0, 1, 2),
    )

    returned = lax.psum_scatter(
        after(y_out, grad_rows).reshape(16 * TOK, WIDTH), "dp", scatter_dimension=0, tiled=True, axis_index_groups=PLANES
    )
    both = None
    grad_query, query_gains, slim = [None] * 4, [None] * 4, [None] * 4
    def sum_mp(t):
        return t + (shift_mp(t, 1) + shift_mp(t, 2) + shift_mp(t, 3))

    rows = [grad_rows, shift_mp(grad_rows, -1), None, shift_mp(grad_rows, 1)]
    for turn, r in enumerate((0, 1, 3, 2)):
        if turn == 1:
            near_a, near_b = after((rows[1], rows[3]), grad_query[0])
            rows[2] = jnp.concatenate(
                [shift_mp(near_a[: TOK // 2], -1), shift_mp(near_b[TOK // 2 :], 1)], axis=0
            )
        if turn == 2:
            small = sum_mp(after(small, rows[2], grad_query[1]))[:36].reshape(48, 768)
        if turn == 3:
            expert_grads = shard_grads[0].astype(F32) + (
                shards_got[0].astype(F32) + (shards_got[1].astype(F32) + shards_got[2].astype(F32))
            )
            rows[r] = after(rows[r], small, expert_grads)
        args = (rows[r], out_w, qb[r], mixed[r], ka, va, raw[r], head_gain, turn_tab[r], spread4)
        first = both is None
        grad_query[r], query_gains[r], slim[r], both = call(
            partial(attend_back_body, first),
            [((TOK, 512), BF16), ((8, PITCH), F32), ((TOK, 256), BF16), ((2, LEN, 256), F32)],
            args if first else args + (both,),
            any_in=() if first else (len(args),),
            any_out=(3,),
            scratch=[pltpu.VMEM((2, LEN, 256), F32), pltpu.SemaphoreType.DMA((4,))],
            aliases=None if first else {len(args): 3},
            local=(0, 1, 4, 5),
            mb=32,
            lazy=True,
        )
    far_up, far_down, wide, gains = call(
        keys_back_body,
        [((TOK // 2, WIDTH), BF16)] * 2 + [((LEN, 512), BF16), ((8, WIDTH), F32)],
        (both, *raw_pair, *turn_tab, head_gain, grad_query[2], proj, chunks[2]),
        near=range(4),
        mb=32,
        lazy=True,
    )
    far_up, far_down = shift_mp(far_up, 1), shift_mp(far_down, -1)
    others = (1, 3, 0)
    part_up, part_down, part_own, keep, send, extra = call(
        tail_body,
        [((TOK, WIDTH), BF16)] * 3 + [((16, 32, 768), BF16), ((19, 32, 768), BF16), ((56, 768), F32)],
        (
            wide,
            gains,
            small,
            spread2,
            spread4,
            *(grad_query[r] for r in others),
            proj,
            *(chunks[r] for r in others),
            *rows,
            *mixed,
            h1,
            *slim,
            *query_gains,
        ),
        scalars=jnp.stack([y_at, z_at, core]),
        scratch=[pltpu.VMEM((LEN, 256), BF16)],
        near=range(6),
        local=(0, 1),
        mb=40,
        lazy=True,
    )
    part_up, part_down = call(
        near_body,
        [((TOK, WIDTH), BF16)] * 2,
        (part_up, part_down, far_up, far_down),
        near=(0, 1),
        local=range(4),
    )
    part_up, part_down = shift_mp(part_up, 1), shift_mp(part_down, -1)
    layer_output = (x_mid + returned.astype(F32)).astype(BF16)
    expert_outs = (
        expert_grads[0:256].reshape(1, 256, FF),
        expert_grads[256:512].reshape(1, 256, FF),
        jnp.concatenate([expert_grads[512:640], expert_grads[640:768]], axis=1).reshape(1, 128, WIDTH),
    )
    first_msg = call(
        ride_first_body,
        [((208, 768), BF16)] * 4,
        (keep, shift_yz(send, 0, 0, 1), extra),
        near=range(4),
        local=range(3),
    )
    second_msg = call(
        ride_second_body,
        [((112, 768), BF16)] * 4,
        after((first_msg[0], *(shift_axis(first_msg[s], 0, s) for s in (1, 2, 3))), part_up, part_down, layer_output, expert_outs),
        near=range(4),
        local=range(4),
    )
    weight_sum, gain_sum, router_sum = call(
        ride_last_body,
        [((32, 768), F32), ((4, 768), F32), ((48, 768), F32)],
        (second_msg[0], *(shift_axis(second_msg[s], 1, s) for s in (1, 2, 3))),
        local=range(4),
    )
    gain_sum, router_sum = sum_mp(gain_sum), router_sum.reshape(36, WIDTH)
    attn_gain_grad = jnp.concatenate([gain_sum[0], gain_sum[1, 0:256]])
    (input_grad,) = call(
        input_body,
        [((TOK, WIDTH), F32)],
        (part_own, part_up, part_down, layer_input, attn_row, grad_mid),
        local=(0, 1, 2),
    )

    return (
        layer_output,
        input_grad,
        attn_gain_grad,
        gain_sum[1, 256 : 256 + HDIM],
        gain_sum[1, 384 : 384 + HDIM],
        weight_sum[:, 0:256],
        weight_sum[:, 256:512].reshape(32, 2, 128),
        weight_sum[:, 512:768],
        router_sum[EXPERTS],
        router_sum[:EXPERTS].T,
        *expert_outs,
    )


def solution(mesh):
    tokens = P(("dp", "mp"), None)
    in_specs = (
        tokens,
        P("dp"),
        tokens,
        P(),
        P(),
        P(),
        P("dp", "mp"),
        P("dp", None, "mp"),
        P("dp", "mp"),
        P(),
        P(),
        P("dp", None, None),
        P("dp", None, None),
        P("dp", None, None),
        tokens,
    )
    out_specs = (
        tokens,
        tokens,
        P(),
        P(),
        P(),
        P("dp", "mp"),
        P("dp", None, "mp"),
        P("dp", "mp"),
        P(),
        P(),
        P("dp", "mp", None),
        P("dp", "mp", None),
        P("dp", "mp", None),
    )
    return jax.shard_map(shards, mesh=mesh, in_specs=in_specs, out_specs=out_specs, check_vma=False)
```

```python
from functools import partial

import jax
import jax.numpy as jnp
import numpy as np
from jax import lax
from jax.experimental import pallas as pl
from jax.experimental.pallas import tpu as pltpu
from jax.sharding import PartitionSpec as P

WIDTH = 1024
HDIM = 64
PITCH = 128
LEN = 1024
TOK = 256
CAP = 96
EXPERTS = 32
FF = 512
SIDE = 16
ROWS = TOK + SIDE
EPS = 1e-06
LOG2E = 1.4426950408889634
F32 = jnp.float32
BF16 = jnp.bfloat16


def nn(left, right):
    return lax.dot_general(left, right, (((1,), (0,)), ((), ())), preferred_element_type=F32)


def nt(left, right):
    return lax.dot_general(left, right, (((1,), (1,)), ((), ())), preferred_element_type=F32)


def tn(left, right):
    return lax.dot_general(left, right, (((0,), (0,)), ((), ())), preferred_element_type=F32)


def spread(heads):
    table = np.zeros((heads * HDIM, heads * PITCH), np.float32)
    for head in range(heads):
        for lane in range(HDIM):
            table[head * HDIM + lane, head * PITCH + lane] = 1.0
    return table


def rope_tables():
    places = np.arange(LEN, dtype=np.float64)
    inverse = 10000.0 ** (-2.0 * np.arange(HDIM // 2, dtype=np.float64) / HDIM)
    angles = places[:, None] * inverse[None, :]
    cos_tab = np.zeros((LEN, PITCH), np.float32)
    sin_tab = np.zeros((LEN, PITCH), np.float32)
    cos_tab[:, : HDIM // 2] = np.cos(angles)
    cos_tab[:, HDIM // 2 : HDIM] = np.cos(angles)
    sin_tab[:, : HDIM // 2] = -np.sin(angles)
    sin_tab[:, HDIM // 2 : HDIM] = np.sin(angles)
    return cos_tab.reshape(LEN // TOK, TOK, PITCH), sin_tab.reshape(LEN // TOK, TOK, PITCH)


def lanes(shape):
    return lax.broadcasted_iota(jnp.int32, shape, 1)


def swap_halves(tensor):
    half = HDIM // 2
    ahead = pltpu.roll(tensor, PITCH - half, 1)
    behind = pltpu.roll(tensor, half, 1)
    return jnp.where(lanes(tensor.shape) < half, ahead, behind)


def head_scale(tensor):
    return lax.rsqrt(jnp.sum(tensor * tensor, axis=1, keepdims=True) * (1.0 / HDIM) + EPS)


def row_scale(tensor):
    return lax.rsqrt(jnp.mean(tensor * tensor, axis=1, keepdims=True) + EPS)


def call(body, out_shape, args, scalars=None, any_in=(), any_out=(), scratch=(), aliases=None, near=(), local=(), mb=24, lazy=False):
    scratch, aliases = list(scratch), aliases or {}
    offset = 0 if scalars is None else 1
    count = offset + len(args)
    fetched = [i for i in range(len(args)) if i not in any_in and i not in local]
    stored = [i for i in range(len(out_shape)) if i not in any_out and i not in near]
    holds = [pltpu.VMEM(args[i].shape, args[i].dtype) for i in fetched]
    holds += [pltpu.VMEM(*out_shape[i]) for i in stored]
    scratch = [*scratch, *holds, pltpu.SemaphoreType.DMA((max(1, len(holds)),))]

    def kernel(*refs):
        refs = list(refs)
        own, sems = refs[len(refs) - len(holds) - 1 : -1], refs[-1]
        refs = refs[: len(refs) - len(holds) - 1]
        copies = {}
        for n, i in enumerate(fetched):
            copies[i] = pltpu.make_async_copy(refs[i + offset], own[n], sems.at[n])
            copies[i].start()
            refs[i + offset] = own[n]
        stores = []
        for n, i in enumerate(stored, len(fetched)):
            stores.append(pltpu.make_async_copy(own[n], refs[i + count], sems.at[n]))
            refs[i + count] = own[n]
        if lazy:
            body(*refs, wait=lambda *which: [copies.pop(i).wait() for i in which])
        else:
            for one in copies.values():
                one.wait()
            body(*refs)
        for one in stores:
            one.start()
        for one in stores:
            one.wait()

    def placed(i, one):
        return pltpu.with_memory_space_constraint(one, pltpu.VMEM if i in local else pltpu.HBM)

    def space(i):
        return pltpu.VMEM if i in local else pltpu.HBM

    args = [placed(i, one) for i, one in enumerate(args)]
    in_specs = [pl.BlockSpec(memory_space=space(i)) for i in range(len(args))]
    out_specs = [pl.BlockSpec(memory_space=pltpu.VMEM if i in near else pltpu.HBM) for i in range(len(out_shape))]
    shapes = [pltpu.VMEM(s, d) if i in near else pltpu.HBM(s, d) for i, (s, d) in enumerate(out_shape)]
    if scalars is not None:
        in_specs = [pl.BlockSpec(memory_space=pltpu.SMEM)] + in_specs
        args = [scalars] + args
    return pl.pallas_call(
        kernel,
        out_shape=shapes,
        in_specs=in_specs,
        out_specs=out_specs,
        scratch_shapes=scratch,
        input_output_aliases={i + offset: o for i, o in aliases.items()},
        compiler_params=pltpu.CompilerParams(vmem_limit_bytes=mb * 1024 * 1024),
        cost_estimate=pl.CostEstimate(flops=1, bytes_accessed=1, transcendentals=0),
    )(*args)


def start_body(sc, routes, ranks_out, coded):
    place = sc[0] * TOK + lax.broadcasted_iota(jnp.int32, (1, TOK), 1)
    names = lax.broadcasted_iota(jnp.int32, (TOK, EXPERTS), 1)
    member = jnp.zeros((TOK, EXPERTS), F32)
    for k in range(routes.shape[1]):
        member = member + jnp.where(routes[:, k : k + 1] == names, 1.0, 0.0)
    member = member.astype(BF16)
    earlier = lax.broadcasted_iota(jnp.int32, (TOK, TOK), 0)
    later = lax.broadcasted_iota(jnp.int32, (TOK, TOK), 1)
    before = jnp.where(earlier < later, 1.0, 0.0).astype(BF16)
    same = jnp.where(earlier == later, 1.0, 0.0).astype(BF16)
    routed = tn(member, same) > 0.5
    ranks = jnp.where(routed, tn(member, before), -1.0)
    ranks_out[...] = ranks
    ranks = jnp.where(routed & (place >= sc[1]), ranks + 128.0, ranks)
    quarter = EXPERTS // 4
    rows = jnp.concatenate([ranks[q * quarter : (q + 1) * quarter] for q in range(4)], axis=1)
    coded[...] = jnp.concatenate([rows, jnp.zeros_like(rows)], axis=0).astype(BF16)


def project_body(sc, own, other, x0, x1, x2, x3, gain, head_gain, cos, sin, spread4, spread2, *refs, wait):
    wait(0, 1)
    outs, raws, pairs, queries, ka, va, out_w, turns = (
        refs[:3], refs[3:7], refs[7:11], refs[11:15], refs[15], refs[16], refs[17], refs[18:22]
    )
    h1, raw_hold, pair_hold, proj, held, sems = refs[22:]
    y_at, z_at, core, mp_at, length = sc[0], sc[1], sc[2], sc[3], sc[4]
    for block in range(16):
        y_rel = (block // 4 - y_at + 4) % 4
        z_rel = (block % 4 - z_at + 4) % 4
        for side in range(2):
            rel = z_rel * 4 + y_rel if side == 0 else y_rel * 4 + z_rel
            part = jnp.where(core == side, own[rel].astype(F32), other[rel].astype(F32)).astype(BF16)
            at = (2 * block + side) * 32
            for piece in range(3):
                held[at : at + 32, piece * 256 : (piece + 1) * 256] = part[piece * 32 : (piece + 1) * 32]
    wait(10, 11)
    proj[:, 0:512] = nn(held[:, 0:256], spread4[...]).astype(BF16)
    proj[:, 512:768] = nn(held[:, 256:384], spread2[...]).astype(BF16)
    proj[:, 768:1024] = nn(held[:, 384:512], spread2[...]).astype(BF16)
    out_w[...] = nn(held[:, 512:768], spread4[...]).astype(BF16)
    copies = [
        pltpu.make_async_copy(proj, outs[1], sems.at[12]),
        pltpu.make_async_copy(held, outs[2], sems.at[13]),
    ]
    for one in copies:
        one.start()
    lane = lanes((TOK, PITCH))
    below = lax.broadcasted_iota(jnp.int32, (TOK, PITCH), 0)
    q_aug = jnp.where(lane == HDIM, 1.0, 0.0)
    v_aug = jnp.where(lane < HDIM + 2, 1.0, 0.0)
    for chunk, x in enumerate((x0, x1, x2, x3)):
        rows = slice(chunk * TOK, (chunk + 1) * TOK)
        at = (mp_at + chunk) % 4
        wait(*((2, 6, 7, 8, 9) if chunk == 0 else (2 + chunk,)))
        xf = x[...].astype(F32)
        normed = (xf * row_scale(xf) * gain[...]).astype(BF16)
        h1[rows, :] = normed
        raw = nn(normed, proj[...])
        raw_hold[rows, :] = raw[:, 0:512]
        pair_hold[rows, :] = raw[:, 512:768]
        cos_t = cos[at]
        sin_t = sin[at]
        turns[chunk][...] = jnp.where(lane < HDIM, cos_t, pltpu.roll(sin_t, HDIM, 1))
        bias = jnp.where(at * TOK + below < length, 0.0, -1e30)
        k_aug = jnp.where(lane == HDIM, bias, jnp.where(lane < HDIM + 4, 1.0, 0.0))
        for head in range(6):
            cols = slice(head * PITCH, (head + 1) * PITCH)
            one = raw[:, cols]
            ready = one * head_scale(one) * head_gain[:, cols]
            turned = ready * cos_t + swap_halves(ready) * sin_t
            if head < 4:
                queries[chunk][:, cols] = jnp.where(lane < HDIM, turned, q_aug).astype(BF16)
            else:
                here = slice((head - 4) * PITCH, (head - 3) * PITCH)
                ka[rows, here] = jnp.where(lane < HDIM, turned, k_aug).astype(BF16)
        for head in range(2):
            va[rows, head * PITCH : (head + 1) * PITCH] = jnp.where(
                lane < HDIM, raw[:, 768 + head * PITCH : 768 + (head + 1) * PITCH], v_aug
            ).astype(BF16)
        here = pl.ds(chunk * TOK, TOK)
        for index, (hold, target) in enumerate(
            ((h1, outs[0].at[here]), (raw_hold, raws[chunk]), (pair_hold, pairs[chunk]))
        ):
            one = pltpu.make_async_copy(hold.at[here], target, sems.at[chunk * 3 + index])
            one.start()
            copies.append(one)
    for one in copies:
        one.wait()


def turn_tables(turn):
    lane = lanes(turn.shape)
    return jnp.where(lane < HDIM, turn, 0.0), jnp.where(lane < HDIM, pltpu.roll(turn, HDIM, 1), 0.0)


def attend_body(qa, ka, va, out_w, branch, mixed, qb):
    lane = lanes((TOK, PITCH))
    for head in range(4):
        cols = slice(head * PITCH, (head + 1) * PITCH)
        kv = slice((head // 2) * PITCH, (head // 2 + 1) * PITCH)
        query = qa[:, cols]
        weight = jnp.exp2(nt(query, ka[:, kv]) * (LOG2E / 8.0)).astype(BF16)
        total = nn(weight, va[:, kv])
        denom = total[:, HDIM : HDIM + 1]
        mixed[:, cols] = jnp.where(lane < HDIM, total / denom, 0.0).astype(BF16)
        level = jnp.log(denom) * -8.0
        high = level.astype(BF16).astype(F32)
        middle = (level - high).astype(BF16).astype(F32)
        low = level - high - middle
        stats = jnp.where(lane == HDIM + 1, high, jnp.where(lane == HDIM + 2, middle, low))
        qb[:, cols] = jnp.where(
            (lane > HDIM) & (lane < HDIM + 4), stats, query.astype(F32)
        ).astype(BF16)
    branch[...] = nt(mixed[...], out_w[...]).astype(BF16)


def middle_body(x, p0, p1, p2, p3, gain, coded, x_mid, h2):
    total = (
        x[...].astype(F32)
        + ((p0[...].astype(F32) + p1[...].astype(F32)) + (p2[...].astype(F32) + p3[...].astype(F32)))
    )
    x_mid[...] = total
    h2[0:TOK, :] = (total * row_scale(total) * gain[...]).astype(BF16)
    h2[TOK:ROWS, :] = coded[...]


def gates_of(logits, ranks):
    routed = ranks >= 0.0
    masked = jnp.where(routed, logits, -1e30)
    weight = jnp.where(routed, jnp.exp(masked - jnp.max(masked, axis=0, keepdims=True)), 0.0)
    return weight / jnp.sum(weight, axis=0, keepdims=True)


def gates_body(h2, router, ranks, gates):
    gates[...] = gates_of(nt(router[...], h2[0:TOK, :]), ranks[...])


def unfold(rows):
    return jnp.concatenate([rows[:, q * TOK : (q + 1) * TOK] for q in range(4)], axis=0)


def experts_body(pieces, unit, *refs, wait):
    sc = refs[0]
    tokens = refs[1 : 1 + len(pieces)]
    at = 1 + len(pieces)
    cot_all, router = refs[at], refs[at + 1]
    weights = refs[at + 2 : at + 8]
    at = at + 8
    if unit > 0:
        at = at + 6
    y_out, back_a, back_b, taken_all, push_all, hidden_all, gate_all, up_all = refs[at : at + 8]
    cot, y_hold, y_back, t_hold, r_hold, e_hold, h_hold, g_hold, u_hold, sems = refs[at + 8 :]
    cot_in = [pltpu.make_async_copy(cot_all.at[sc[i]], cot.at[i], sems.at[i]) for i in range(4)]
    for one in cot_in:
        one.start()
    tok = [(tokens[index], j) for index, count in enumerate(pieces) for j in range(count)]
    own_names = (sc[4], sc[5])
    names = lax.broadcasted_iota(jnp.int32, (EXPERTS, TOK), 0)
    slots = lax.broadcasted_iota(jnp.int32, (CAP, TOK), 0).astype(F32)
    picks, live_picks = [[], []], [[], []]
    gate_cols = [[], []]
    all_ranks = []
    copies_out = []

    def put(source, target, sem):
        one = pltpu.make_async_copy(source, target, sems.at[sem])
        one.start()
        copies_out.append(one)

    for i in range(4):
        ref, j = tok[i]
        rows = slice(i * CAP, (i + 1) * CAP)
        ranks = unfold(ref[j, TOK : TOK + EXPERTS // 4, :].astype(F32))
        all_ranks.append(ranks)
        for e in range(2):
            rank = jnp.sum(jnp.where(names == own_names[e], ranks, 0.0), axis=0, keepdims=True)
            live_picks[e].append(jnp.where(slots == rank, 1.0, 0.0).astype(BF16))
            picks[e].append(jnp.where((slots == rank) | (slots + 128.0 == rank), 1.0, 0.0).astype(BF16))
        got = nn(jnp.concatenate([picks[0][i], picks[1][i]], axis=0), ref[j, 0:TOK, :]).astype(BF16)
        t_hold[0, rows, :] = got[:CAP]
        t_hold[1, rows, :] = got[CAP:]
    wait(len(pieces) + 1)
    for i in range(4):
        ref, j = tok[i]
        gates = gates_of(nt(router[...], ref[j, 0:TOK, :]), all_ranks[i])
        for e in range(2):
            gate = jnp.sum(jnp.where(names == own_names[e], gates, 0.0), axis=0, keepdims=True)
            gate_cols[e].append(jnp.sum(picks[e][i].astype(F32) * gate, axis=1, keepdims=True))
    here = pl.ds(unit * 4 * CAP, 4 * CAP)
    kept = []
    out_parts = []
    for e in range(2):
        gate_w, up_w, down_w = weights[3 * e : 3 * e + 3]
        put(t_hold.at[e], taken_all.at[e, here], 14 + 5 * e)
        taken = t_hold[e]
        gate_act = nn(taken, gate_w[0])
        up_act = nn(taken, up_w[0])
        sigma = jax.nn.sigmoid(gate_act)
        silu = gate_act * sigma
        slope = up_act * (sigma + silu * (1.0 - sigma))
        hidden = (silu * up_act).astype(BF16)
        h_hold[e] = hidden
        put(h_hold.at[e], hidden_all.at[e, here], 15 + 5 * e)
        result = nn(hidden, down_w[0]).astype(BF16)
        gate_col = jnp.concatenate(gate_cols[e], axis=0)
        kept.append((silu, slope, result, gate_col))
        out_parts.append((result.astype(F32) * gate_col).astype(BF16))
    for i in range(4):
        pick = jnp.concatenate([picks[0][i], picks[1][i]], axis=0)
        rows = slice(i * CAP, (i + 1) * CAP)
        y_hold[i] = tn(pick, jnp.concatenate([out_parts[0][rows], out_parts[1][rows]], axis=0)).astype(BF16)
        put(y_hold.at[i], y_out.at[sc[i]], 28 + i)
    for i in range(4):
        rows = slice(i * CAP, (i + 1) * CAP)
        cot_in[i].wait()
        got = nn(jnp.concatenate([live_picks[0][i], live_picks[1][i]], axis=0), cot[i]).astype(BF16)
        r_hold[0, rows, :] = got[:CAP]
        r_hold[1, rows, :] = got[CAP:]
    marks = [[], []]
    back_parts = []
    for e in range(2):
        gate_w, up_w, down_w = weights[3 * e : 3 * e + 3]
        silu, slope, result, gate_col = kept[e]
        grad_rows = r_hold[e].astype(F32)
        push = (grad_rows * gate_col).astype(BF16)
        e_hold[e] = push
        put(e_hold.at[e], push_all.at[e, here], 16 + 5 * e)
        grad_hidden = nt(push, down_w[0])
        grad_gate = (grad_hidden * slope).astype(BF16)
        grad_up = (grad_hidden * silu).astype(BF16)
        g_hold[e] = grad_gate
        u_hold[e] = grad_up
        put(g_hold.at[e], gate_all.at[e, here], 17 + 5 * e)
        put(u_hold.at[e], up_all.at[e, here], 18 + 5 * e)
        back_parts.append((nt(grad_gate, gate_w[0]) + nt(grad_up, up_w[0])).astype(BF16))
        mark = jnp.sum(grad_rows * result.astype(F32), axis=1, keepdims=True)
        for i in range(4):
            marks[e].append(
                jnp.sum(picks[e][i].astype(F32) * mark[i * CAP : (i + 1) * CAP], axis=0, keepdims=True)
            )
    for i in range(4):
        pick = jnp.concatenate([picks[0][i], picks[1][i]], axis=0)
        rows = slice(i * CAP, (i + 1) * CAP)
        y_back[i, 0:TOK, :] = tn(
            pick, jnp.concatenate([back_parts[0][rows], back_parts[1][rows]], axis=0)
        ).astype(BF16)
        mark = jnp.where(names == own_names[0], marks[0][i], 0.0) + jnp.where(
            names == own_names[1], marks[1][i], 0.0
        )
        high = mark.astype(BF16).astype(F32)
        low = mark - high
        quarter = EXPERTS // 4
        fold = [
            jnp.concatenate([part[q * quarter : (q + 1) * quarter] for q in range(4)], axis=1)
            for part in (high, low)
        ]
        y_back[i, TOK:ROWS, :] = jnp.concatenate(fold, axis=0).astype(BF16)
        put(y_back.at[i], (back_a if i < 2 else back_b).at[i % 2], 24 + i)
    for one in copies_out:
        one.wait()


def expert_weights_body(expert, sc, *refs):
    count = 5 + (1 - expert)
    sources, outs = refs[:5], refs[count : count + (1 if expert == 1 else 5)]
    holds, sums, sems = refs[len(refs) - 9 : len(refs) - 4], refs[len(refs) - 4 : len(refs) - 1], refs[-1]
    copies = [pltpu.make_async_copy(one.at[expert], hold, sems.at[n]) for n, (one, hold) in enumerate(zip(sources, holds))]
    for one in copies:
        one.start()
    taken, gate, up, hidden, push = holds
    copies[0].wait()
    copies[1].wait()
    sums[0][...] = tn(taken[...], gate[...])
    copies[2].wait()
    sums[1][...] = tn(taken[...], up[...])
    copies[3].wait()
    copies[4].wait()
    sums[2][...] = tn(hidden[...], push[...])
    if expert == 1:
        (out,) = outs
        out[0:1024, :] = sums[0][...].astype(BF16)
        out[1024:2048, :] = sums[1][...].astype(BF16)
        out[2048:2560, :] = sums[2][:, 0:FF].astype(BF16)
        out[2560:3072, :] = sums[2][:, FF:WIDTH].astype(BF16)
        return
    got = refs[5]
    for part in range(4):
        at = (sc[0] + part) % 4
        rows = pl.ds(pl.multiple_of(at * 256, 256), 256)

        def put(start, value):
            if part == 2:
                outs[3 + start // 384][start % 384 : start % 384 + 128, :] = value.astype(BF16)
            else:
                outs[min(part, 2)][start : start + 128, :] = value.astype(BF16)

        def more(start, count):
            return got[pl.ds(pl.multiple_of(start + at * count, count), count), :].astype(F32)

        for n, start in enumerate((0, 1024)):
            value = sums[n][rows, :] + more(start, 256)
            put(256 * n, value[0:128])
            put(256 * n + 128, value[128:256])
        rows = pl.ds(pl.multiple_of(at * 128, 128), 128)
        put(512, sums[2][rows, 0:FF] + more(2048, 128))
        put(640, sums[2][rows, FF:WIDTH] + more(2560, 128))


def shard_near_body(up, down, far_up, far_down, out_up, out_down):
    out_up[0:384, :] = (up[0:384, :].astype(F32) + far_up[...].astype(F32)).astype(BF16)
    out_up[384:768, :] = up[384:768, :]
    out_down[0:384, :] = down[0:384, :]
    out_down[384:768, :] = (down[384:768, :].astype(F32) + far_down[...].astype(F32)).astype(BF16)


def expert_weights(saved, expert, mp_at, got=()):
    taken, push, hidden, gate, up = saved
    sources = (taken, gate, up, hidden, push)
    shapes = [((3072, FF), BF16)] if expert == 1 else [((768, FF), BF16)] * 3 + [((384, FF), BF16)] * 2
    return call(
        partial(expert_weights_body, expert),
        shapes,
        (*sources, *got),
        scalars=mp_at.reshape(1),
        any_in=range(5),
        scratch=[pltpu.VMEM(one.shape[1:], one.dtype) for one in sources]
        + [pltpu.VMEM((WIDTH, FF), F32), pltpu.VMEM((WIDTH, FF), F32), pltpu.VMEM((FF, WIDTH), F32)]
        + [pltpu.SemaphoreType.DMA((5,))],
        near=range(len(shapes)),
        local=range(5, 5 + len(got)),
        mb=36,
    )


def token_back_body(sc, r0, r1, r2, h2, x_mid, ranks, gates, router, gain, cot, grad_mid, branch, small):
    total = r0[...].astype(F32) + (r1[...].astype(F32) + r2[...].astype(F32))
    marks = unfold(total[TOK : TOK + 8]) + unfold(total[TOK + 8 : TOK + 16])
    gate = gates[...]
    centre = jnp.sum(gate * marks, axis=0, keepdims=True)
    grad_logits = jnp.where(ranks[...] >= 0.0, gate * (marks - centre), 0.0).astype(BF16)
    router_part = nn(grad_logits, h2[0:TOK, :])
    small[0:32, :] = router_part[:, 0:768]
    small[32:48, 0:256] = router_part[0:16, 768:1024]
    small[32:48, 256:512] = router_part[16:32, 768:1024]
    small[32:48, 512:768] = jnp.zeros((16, 256), F32)
    grad_h2 = total[0:TOK] + tn(grad_logits, router[...])
    x = x_mid[...]
    scale = row_scale(x)
    normed = x * scale
    grad_normed = grad_h2 * gain[...]
    gain_part = jnp.sum(grad_h2 * normed, axis=0, keepdims=True)
    for quarter in range(4):
        small[32 + quarter : 33 + quarter, 512:768] = gain_part[:, quarter * 256 : (quarter + 1) * 256]
    place = sc[0] * TOK + lax.broadcasted_iota(jnp.int32, (TOK, 1), 0)
    out = cot[...].astype(F32) * jnp.where(place < sc[1], 1.0, 0.0) + scale * (
        grad_normed - normed * jnp.mean(grad_normed * normed, axis=1, keepdims=True)
    )
    grad_mid[...] = out
    branch[...] = out.astype(BF16)


def head_back(grad, raw, gain, cos_t, sin_t):
    upstream = grad * cos_t - swap_halves(grad) * sin_t
    scale = head_scale(raw)
    normed = raw * scale
    grad_normed = upstream * gain
    gain_grad = jnp.sum(upstream * normed, axis=0, keepdims=True)
    inner = jnp.sum(grad_normed * normed, axis=1, keepdims=True) * (1.0 / HDIM)
    return scale * (grad_normed - normed * inner), gain_grad


def attend_back_body(first, *refs, wait):
    rows, out_w, qb, mixed, ka, va, raw, head_gain, turn, spread4 = refs[:10]
    rest = refs[10:] if first else refs[11:]
    grad_query, gain_out, slim, both_out, both, sems = rest
    loads = []
    if not first:
        loads = [pltpu.make_async_copy(refs[10].at[g], both.at[g], sems.at[g]) for g in range(2)]
        for one in loads:
            one.start()
    stores = [pltpu.make_async_copy(both.at[g], both_out.at[g], sems.at[2 + g]) for g in range(2)]
    lane = lanes((TOK, PITCH))
    pushed = nn(rows[...], out_w[...]).astype(BF16)
    gain_total = jnp.zeros((1, PITCH), F32)
    wait(2, 3)
    for head in range(4):
        cols = slice(head * PITCH, (head + 1) * PITCH)
        group = head // 2
        kv = slice(group * PITCH, (group + 1) * PITCH)
        grad = pushed[:, cols]
        grad_f = grad.astype(F32)
        delta = -jnp.sum(grad_f * mixed[:, cols].astype(F32), axis=1, keepdims=True)
        high = delta.astype(BF16).astype(F32)
        grad_aug = jnp.where(
            lane == HDIM, high, jnp.where(lane == HDIM + 1, delta - high, grad_f)
        ).astype(BF16)
        query = qb[:, cols]
        probs = jnp.exp2(nt(ka[:, kv], query) * (LOG2E / 8.0))
        inner = nt(va[:, kv], grad_aug)
        grad_scores = (probs * inner).astype(BF16)
        add_k = nn(grad_scores, query)
        add_v = nn(probs.astype(BF16), grad)
        if head % 2 == 0 and first:
            both[group, :, 0:PITCH] = add_k
            both[group, :, PITCH : 2 * PITCH] = add_v
        else:
            if head % 2 == 0:
                loads[group].wait()
            both[group, :, 0:PITCH] += add_k
            both[group, :, PITCH : 2 * PITCH] += add_v
        if head % 2 == 1:
            stores[group].start()
        grad_q = jnp.where(lane < HDIM, tn(grad_scores, ka[:, kv]) * 0.125, 0.0)
        if head == 0:
            wait(6, 7, 8)
            cos_t, sin_t = turn_tables(turn[...])
        back, gain_grad = head_back(grad_q, raw[:, cols], head_gain[:, cols], cos_t, sin_t)
        grad_query[:, cols] = back.astype(BF16)
        gain_total = gain_total + gain_grad
    wait(9)
    slim[...] = nt(grad_query[...], spread4[...]).astype(BF16)
    gain_out[...] = jnp.broadcast_to(gain_total, (8, PITCH))
    for one in stores:
        one.wait()


def keys_back_body(*refs, wait):
    both, raws, turns, head_gain, query, proj = refs[0], refs[1:5], refs[5:9], refs[9], refs[10], refs[11]
    far_up, far_down, wide, gains = refs[12:]
    half = TOK // 2
    lane = lanes((TOK, PITCH))
    key_gain = jnp.zeros((1, PITCH), F32)
    wait(0, 9)
    for chunk in (2, 0, 1, 3):
        wait(1 + chunk, 5 + chunk)
        at = slice(chunk * TOK, (chunk + 1) * TOK)
        cos_t, sin_t = turn_tables(turns[chunk][...])
        for head in range(2):
            cols = slice(head * PITCH, (head + 1) * PITCH)
            grad = jnp.where(lane < HDIM, both[head, at, 0:PITCH] * 0.125, 0.0)
            back, gain_grad = head_back(
                grad, raws[chunk][:, cols], head_gain[:, 512 + head * PITCH : 640 + head * PITCH], cos_t, sin_t
            )
            wide[at, cols] = back.astype(BF16)
            key_gain = key_gain + gain_grad
            wide[at, 256 + head * PITCH : 384 + head * PITCH] = jnp.where(
                lane < HDIM, both[head, at, PITCH : 2 * PITCH], 0.0
            ).astype(BF16)
    wait(10, 11)
    part = nt(query[...], proj[:, 0:512]) + nt(wide[2 * TOK : 3 * TOK, :], proj[:, 512:1024])
    far_up[...] = part[:half].astype(BF16)
    far_down[...] = part[half:].astype(BF16)
    gains[...] = jnp.broadcast_to(key_gain, (8, PITCH))


def parts_body(*refs, wait):
    wide, far_up, far_down, proj, queries, outs = refs[0], refs[1], refs[2], refs[3], refs[4:7], refs[7:10]
    half = TOK // 2
    wait(3)
    for n, chunk in enumerate((1, 3, 0)):
        wait(4 + n)
        at = slice(chunk * TOK, (chunk + 1) * TOK)
        part = nt(queries[n][...], proj[:, 0:512]) + nt(wide[at, :], proj[:, 512:1024])
        if chunk == 1:
            outs[n][:half, :] = (part[:half] + far_up[...].astype(F32)).astype(BF16)
            outs[n][half:, :] = part[half:].astype(BF16)
        elif chunk == 3:
            outs[n][:half, :] = part[:half].astype(BF16)
            outs[n][half:, :] = (part[half:] + far_down[...].astype(F32)).astype(BF16)
        else:
            outs[n][...] = part.astype(BF16)


def tail_body(*refs, wait):
    sc, refs = refs[0], refs[1:]
    wide, key_gain, small, spread2, spread4, weights, gain_row = refs[0:7]
    rows, mixed, h1, slims, query_gains = refs[7:11], refs[11:15], refs[15], refs[16:20], refs[20:24]
    keep, send, extra = refs[24:27]
    (slim_pair,) = refs[27:]
    y_at, z_at, core = sc[0], sc[1], sc[2]
    wait(3, 4)
    slim_pair[:, 0:128] = nt(wide[:, 0:256], spread2[...]).astype(BF16)
    slim_pair[:, 128:256] = nt(wide[:, 256:512], spread2[...]).astype(BF16)
    wait(15)
    pair_total = tn(h1[...], slim_pair[...])
    query_total = jnp.zeros((WIDTH, 256), F32)
    out_total = jnp.zeros((WIDTH, 256), F32)
    for chunk in range(4):
        wait(7 + chunk, 11 + chunk, 16 + chunk)
        at = slice(chunk * TOK, (chunk + 1) * TOK)
        query_total = query_total + tn(h1[at, :], slims[chunk][...])
        out_total = out_total + tn(rows[chunk][...], nt(mixed[chunk][...], spread4[...]).astype(BF16))
    wait(2, 5, 6, 20, 21, 22, 23)
    shares = query_total * weights[:, 0:256].astype(F32) + pair_total * weights[:, 256:512].astype(F32)
    ones = jnp.ones((8, 256), BF16)
    high = shares.astype(BF16)
    low = (shares - high.astype(F32)).astype(BF16)
    total = (nt(ones, high) + nt(ones, low))[0:1, :] / gain_row[...]
    query_gain = (query_gains[0][0:1, :] + query_gains[1][0:1, :]) + (
        query_gains[2][0:1, :] + query_gains[3][0:1, :]
    )
    extra[0:8, :] = jnp.zeros((8, 768), F32)
    extra[8:56, :] = small[...]
    extra[0:1, :] = total[:, 0:768]
    extra[1:2, 0:256] = total[:, 768:1024]
    extra[1:2, 256:384] = query_gain
    extra[1:2, 384:512] = key_gain[0:1, :]
    query_rows, pair_rows, out_rows = query_total.astype(BF16), pair_total.astype(BF16), out_total.astype(BF16)
    for block in range(16):
        y_rel = (block // 4 - y_at + 4) % 4
        z_rel = (block % 4 - z_at + 4) % 4
        for side in range(2):
            at = (2 * block + side) * 32
            rel = y_rel * 4 + z_rel if side == 0 else z_rel * 4 + y_rel

            def put(target):
                target[rel, :, 0:256] = query_rows[at : at + 32]
                target[rel, :, 256:512] = pair_rows[at : at + 32]
                target[rel, :, 512:768] = out_rows[at : at + 32]

            pl.when(core == side)(partial(put, keep))
            pl.when(core != side)(partial(put, send))


def split3(value):
    high = value.astype(BF16).astype(F32)
    middle = (value - high).astype(BF16).astype(F32)
    low = value - high - middle
    return jnp.concatenate([high, middle, low, jnp.zeros((20, 768), F32)], axis=0).astype(BF16)


def join3(rows):
    value = rows.astype(F32)
    return value[0:4] + value[4:8] + value[8:12]


def ride_first_body(keep, got, extra, extra_got, *outs):
    gain = split3(extra[0:4, :] + extra_got[0:4, :])
    router = (extra[8:56, :] + extra_got[8:56, :]).astype(BF16)
    for first in range(4):
        for second in range(4):
            at = first * 4 + second
            outs[first][second * 32 : (second + 1) * 32, :] = (
                keep[at].astype(F32) + got[at].astype(F32)
            ).astype(BF16)
        outs[first][128:160, :] = gain
        outs[first][160:208, :] = router


def add4(own, g1, g2, g3, start, stop):
    return own[start:stop, :].astype(F32) + (
        g1[start:stop, :].astype(F32) + (g2[start:stop, :].astype(F32) + g3[start:stop, :].astype(F32))
    )


def add_gains(own, g1, g2, g3, start):
    stop = start + 32
    return (join3(own[start:stop, :]) + join3(g1[start:stop, :])) + (
        join3(g2[start:stop, :]) + join3(g3[start:stop, :])
    )


def ride_second_body(own, g1, g2, g3, *outs):
    rows = add4(own, g1, g2, g3, 0, 128)
    gain = split3(add_gains(own, g1, g2, g3, 128))
    router = add4(own, g1, g2, g3, 160, 208).astype(BF16)
    for second in range(4):
        outs[second][0:32, :] = rows[second * 32 : (second + 1) * 32].astype(BF16)
        outs[second][32:64, :] = gain
        outs[second][64:112, :] = router


def ride_last_body(own, g1, g2, g3, rows, gain, router, ffn):
    rows[...] = add4(own, g1, g2, g3, 0, 32)
    gain[...] = add_gains(own, g1, g2, g3, 32)
    total = add4(own, g1, g2, g3, 64, 112)
    whole = jnp.concatenate(
        [total[0:32], jnp.concatenate([total[32:48, 0:256], total[32:48, 256:512]], axis=0)], axis=1
    )
    router[...] = jnp.transpose(whole)
    for quarter in range(4):
        ffn[:, quarter * 256 : (quarter + 1) * 256] = total[32 + quarter : 33 + quarter, 512:768]


def input_body(p0, p1, p2, x, gain, grad_mid, out):
    upstream = p0[...].astype(F32) + (p1[...].astype(F32) + p2[...].astype(F32))
    xf = x[...].astype(F32)
    scale = row_scale(xf)
    normed = xf * scale
    grad_normed = upstream * gain[...]
    out[...] = grad_mid[...] + scale * (
        grad_normed - normed * jnp.mean(grad_normed * normed, axis=1, keepdims=True)
    )


def place_of(index):
    return index // 8, (index // 2) % 4, index % 2


def index_of(y, z, core):
    return (y % 4) * 8 + (z % 4) * 2 + core


def shift_yz(tensor, dy, dz, flip=0):
    pairs = []
    for d in range(32):
        y, z, core = place_of(d)
        pairs.append((d, index_of(y + dy, z + dz, core ^ flip)))
    return lax.ppermute(tensor, "dp", pairs)


def shift_axis(tensor, axis, step):
    pairs = []
    for d in range(32):
        y, z, core = place_of(d)
        if (core == 0) == (axis == 0):
            pairs.append((d, index_of(y + step, z, core)))
        else:
            pairs.append((d, index_of(y, z + step, core)))
    return lax.ppermute(tensor, "dp", pairs)


def shift_mp(tensor, step):
    return lax.ppermute(tensor, "mp", [(i, (i + step) % 4) for i in range(4)])


def gather_weights(shard, chunks):
    rows = jnp.stack([shard] + [shift_axis(shard, 0, -s) for s in (1, 2, 3)])
    rows = after(rows, chunks[1], chunks[3])
    own = jnp.concatenate([rows] + [shift_axis(rows, 1, -s) for s in (1, 2, 3)], axis=0)
    near = own
    own = after(own, chunks)
    return near, own, shift_yz(own, 0, 0, 1)


def gather_mp(tensor):
    plus, minus = shift_mp(tensor, -1), shift_mp(tensor, 1)
    half = tensor.shape[0] // 2
    far = jnp.concatenate([shift_mp(plus[:half], -1), shift_mp(minus[half:], 1)], axis=0)
    return [tensor, plus, far, minus]


def after(value, *others):
    return lax.optimization_barrier((value, others))[0]


def add_low(left, *others):
    total = left.astype(F32)
    for one in others:
        total = total + one.astype(F32)
    return total.astype(BF16)


PLANES = [[core + 2 * k for k in range(16)] for core in range(2)]
STEPS = (0, 1, -1, 2)


def shards(
    layer_input,
    lengths,
    routes,
    attn_gain,
    query_gain,
    key_gain,
    query_weight,
    key_value_weight,
    out_weight,
    ffn_gain,
    router_weight,
    gate_weight,
    up_weight,
    down_weight,
    cotangent,
):
    dp_at = lax.axis_index("dp").astype(jnp.int32)
    mp_at = lax.axis_index("mp").astype(jnp.int32)
    y_at, z_at, core = dp_at // 8, (dp_at // 2) % 4, dp_at % 2
    length = lengths[0].astype(jnp.int32)
    cos_np, sin_np = rope_tables()
    cos_tab, sin_tab = jnp.asarray(cos_np), jnp.asarray(sin_np)
    spread4, spread2 = jnp.asarray(spread(4), BF16), jnp.asarray(spread(2), BF16)
    attn_row = attn_gain.reshape(1, WIDTH)
    ffn_row = ffn_gain.reshape(1, WIDTH)
    pad = jnp.zeros((PITCH - HDIM,), F32)
    head_gain = jnp.concatenate([query_gain, pad] * 4 + [key_gain, pad] * 2).reshape(1, 768)
    router = router_weight.T

    chunks = gather_mp(layer_input)
    chunk_at = [(mp_at + r) % 4 for r in range(4)]
    shard = jnp.concatenate([query_weight, key_value_weight.reshape(32, 256), out_weight], axis=0)
    shards_near, shards_own, shards_other = gather_weights(shard, chunks)

    cot_all = lax.all_gather(cotangent, "dp", axis=0, tiled=False, axis_index_groups=PLANES)
    ranks, coded = call(
        start_body,
        [((EXPERTS, TOK), F32), ((SIDE, WIDTH), BF16)],
        after((routes,), shards_near),
        scalars=jnp.stack([mp_at, length]),
    )
    weights_own = (gate_weight, up_weight, down_weight)
    weights_other = tuple(shift_yz(after(w, shards_other), 0, 0, 1) for w in weights_own)

    out = call(
        project_body,
        [((LEN, WIDTH), BF16), ((WIDTH, 1024), BF16), ((WIDTH, 768), BF16)]
        + [((TOK, 512), F32)] * 4
        + [((TOK, 256), F32)] * 4
        + [((TOK, 512), BF16)] * 4
        + [((LEN, 256), BF16), ((LEN, 256), BF16), ((WIDTH, 512), BF16)]
        + [((TOK, PITCH), F32)] * 4,
        (shards_own, shards_other, *chunks, attn_row, head_gain, cos_tab, sin_tab, spread4, spread2),
        scalars=jnp.stack([y_at, z_at, core, mp_at, length]),
        any_out=range(11),
        near=range(11, 18),
        scratch=[
            pltpu.VMEM((LEN, WIDTH), BF16),
            pltpu.VMEM((LEN, 512), F32),
            pltpu.VMEM((LEN, 256), F32),
            pltpu.VMEM((WIDTH, 1024), BF16),
            pltpu.VMEM((WIDTH, 768), BF16),
            pltpu.SemaphoreType.DMA((14,)),
        ],
        mb=40,
        lazy=True,
    )
    h1, proj, weights_in, raw, raw_pair, qa = out[0], out[1], out[2], out[3:7], out[7:11], out[11:15]
    ka, va, out_w, turn_tab = out[15], out[16], out[17], out[18:22]

    qa = list(after(tuple(qa), weights_other))
    branch, mixed, qb = [None] * 4, [None] * 4, [None] * 4
    arrived = [None] * 4
    for r in (2, 1, 3, 0):
        if r == 0:
            qa[0] = after(qa[0], arrived[2])
        branch[r], mixed[r], qb[r] = call(
            attend_body,
            [((TOK, WIDTH), BF16), ((TOK, 512), BF16), ((TOK, 512), BF16)],
            (qa[r], ka, va, out_w),
            near=(0,),
            local=(0, 1, 2, 3),
        )
        arrived[r] = shift_mp(branch[r], r) if r else branch[r]
    x_mid, h2 = call(
        middle_body,
        [((TOK, WIDTH), F32), ((ROWS, WIDTH), BF16)],
        (layer_input, *arrived, ffn_row, coded),
        near=(1,),
        local=(1, 2, 3, 4),
    )
    (gates,) = call(gates_body, [((EXPERTS, TOK), F32)], (h2, router, ranks))

    plus, minus = shift_axis(h2, 0, -1), shift_axis(h2, 0, 1)
    far_a, far_b = shift_axis(plus[:144], 0, -1), shift_axis(minus[144:], 0, 1)
    near_a, near_b = jnp.stack([h2, plus]), jnp.stack([minus, jnp.concatenate([far_a, far_b], axis=0)])
    plus_a, plus_b = shift_axis(near_a, 1, -1), shift_axis(near_b, 1, -1)
    minus_a, minus_b = shift_axis(near_a, 1, 1), shift_axis(near_b, 1, 1)
    units = [(near_a, near_b), (plus_a, plus_b), (minus_a, minus_b), None]

    first_at = jnp.where(core == 0, y_at, z_at)
    second_at = jnp.where(core == 0, z_at, y_at)
    saved = None
    backs = []
    for u, step in enumerate(STEPS):
        if u == 1:
            far_plus, far_minus = after((plus_a, minus_b), backs[0])
            units[3] = (shift_axis(far_plus, 1, -1), shift_axis(far_minus, 1, 1))
            units[2] = after(units[2], units[3])
        if u == 2:
            plus_b = shift_axis(backs[1][1], 1, 1)
        if u == 3:
            minus_a = shift_axis(backs[2][0], 1, -1)
            units[3] = after(units[3], plus_b)
        second = (second_at + step + 4) % 4
        order = []
        for s in STEPS:
            first = (first_at + s + 4) % 4
            order.append(jnp.where(core == 0, first * 4 + second, second * 4 + first))
        sc = jnp.stack(order + [dp_at, dp_at + 1 - 2 * core]).astype(jnp.int32)
        pieces = tuple(one.shape[0] for one in units[u])
        args = (*units[u], cot_all, router, *weights_own, *weights_other)
        any_in = [len(pieces)]
        aliases = None
        if saved is not None:
            base = len(args)
            aliases = {base + i: (0 if i == 0 else i + 2) for i in range(6)}
            any_in += list(range(base, base + 6))
            args = args + tuple(saved)
        made = call(
            partial(experts_body, pieces, u),
            [
                ((16, TOK, WIDTH), BF16),
                ((2, ROWS, WIDTH), BF16),
                ((2, ROWS, WIDTH), BF16),
                ((2, 16 * CAP, WIDTH), BF16),
                ((2, 16 * CAP, WIDTH), BF16),
                ((2, 16 * CAP, FF), BF16),
                ((2, 16 * CAP, FF), BF16),
                ((2, 16 * CAP, FF), BF16),
            ],
            args,
            scalars=sc,
            any_in=any_in,
            any_out=range(8),
            scratch=[
                pltpu.VMEM((4, TOK, WIDTH), BF16),
                pltpu.VMEM((4, TOK, WIDTH), BF16),
                pltpu.VMEM((4, ROWS, WIDTH), BF16),
                pltpu.VMEM((2, 4 * CAP, WIDTH), BF16),
                pltpu.VMEM((2, 4 * CAP, WIDTH), BF16),
                pltpu.VMEM((2, 4 * CAP, WIDTH), BF16),
                pltpu.VMEM((2, 4 * CAP, FF), BF16),
                pltpu.VMEM((2, 4 * CAP, FF), BF16),
                pltpu.VMEM((2, 4 * CAP, FF), BF16),
                pltpu.SemaphoreType.DMA((32,)),
            ],
            aliases=aliases,
            local=(*range(len(pieces)), *range(len(pieces) + 2, len(pieces) + 8)),
            mb=36,
            lazy=True,
        )
        backs.append(made[1:3])
        saved = [made[0]] + list(made[3:])
    y_out, taken, push, hidden, grad_gate, grad_up = saved

    (b0_a, b0_b), (bp_a, _), (_, bm_b), (bf_a, bf_b) = backs
    half_a, half_b = shift_axis(bf_a, 1, 1), shift_axis(bf_b, 1, -1)
    saved = (taken, push, hidden, grad_gate, grad_up)
    for_other = expert_weights(after(saved, minus_a), 1, mp_at)
    for_other = after(for_other, half_a, half_b)
    plus_late, minus_late = add_low(bp_a, half_a), add_low(bm_b, half_b)
    plus_a, minus_b = shift_axis(plus_late, 1, 1), shift_axis(minus_late, 1, -1)
    from_other = shift_yz(for_other[0], 0, 0, 1)
    shard_grads = expert_weights(after(saved, plus_late, minus_late), 0, mp_at, (from_other,))
    shard_far = shift_mp(shard_grads[3], 1), shift_mp(shard_grads[4], -1)
    b0_a, b0_b = after((b0_a, b0_b), shard_grads)
    line_a = add_low(b0_a, plus_a, minus_a)
    line_b = add_low(b0_b, plus_b, minus_b)
    cut = ROWS // 2 + 8
    far_up, far_down = shift_axis(line_b[1, :cut], 0, 1), shift_axis(line_b[1, cut:], 0, -1)
    send_up = jnp.concatenate([add_low(line_a[1, :cut], far_up), line_a[1, cut:]], axis=0)
    send_down = jnp.concatenate([line_b[0, :cut], add_low(line_b[0, cut:], far_down)], axis=0)
    shard_near = call(
        shard_near_body,
        [((768, FF), BF16)] * 2,
        (shard_grads[1], shard_grads[2], *shard_far),
        near=(0, 1),
        local=range(4),
    )
    send_up, send_down = after((send_up, send_down), shard_near)
    got_up, got_down = shift_axis(send_up, 0, 1), shift_axis(send_down, 0, -1)
    grad_mid, grad_rows, small = call(
        token_back_body,
        [((TOK, WIDTH), F32), ((TOK, WIDTH), BF16), ((48, 768), F32)],
        (line_a[0], got_up, got_down, h2, x_mid, ranks, gates, router, ffn_row, cotangent),
        scalars=jnp.stack([mp_at, length]),
        local=(0, 1, 2),
    )

    returned = lax.psum_scatter(
        after(y_out, grad_rows).reshape(16 * TOK, WIDTH), "dp", scatter_dimension=0, tiled=True, axis_index_groups=PLANES
    )
    both = None
    grad_query, query_gains, slim = [None] * 4, [None] * 4, [None] * 4
    def sum_mp(t):
        return t + (shift_mp(t, 1) + shift_mp(t, 2) + shift_mp(t, 3))

    rows = [grad_rows, shift_mp(grad_rows, -1), None, shift_mp(grad_rows, 1)]
    for turn, r in enumerate((0, 1, 3, 2)):
        if turn == 2:
            near_a, near_b = after((rows[1], rows[3]), grad_query[1])
            rows[2] = jnp.concatenate(
                [shift_mp(near_a[: TOK // 2], -1), shift_mp(near_b[TOK // 2 :], 1)], axis=0
            )
        if turn == 1:
            shard_near = after(shard_near, rows[1], rows[3], grad_query[0])
            shards_got = shift_mp(shard_near[0], 1), shift_mp(shard_near[1], -1)
            rows[r] = after(rows[r], rows[3])
        args = (rows[r], out_w, qb[r], mixed[r], ka, va, raw[r], head_gain, turn_tab[r], spread4)
        first = both is None
        grad_query[r], query_gains[r], slim[r], both = call(
            partial(attend_back_body, first),
            [((TOK, 512), BF16), ((8, PITCH), F32), ((TOK, 256), BF16), ((2, LEN, 256), F32)],
            args if first else args + (both,),
            any_in=() if first else (len(args),),
            any_out=(3,),
            scratch=[pltpu.VMEM((2, LEN, 256), F32), pltpu.SemaphoreType.DMA((4,))],
            aliases=None if first else {len(args): 3},
            local=(0, 1, 4, 5),
            mb=32,
            lazy=True,
        )
    far_up, far_down, wide, key_gain_part = call(
        keys_back_body,
        [((TOK // 2, WIDTH), BF16)] * 2 + [((LEN, 512), BF16), ((8, PITCH), F32)],
        (after(both, shards_got), *raw_pair, *turn_tab, head_gain, grad_query[2], proj),
        near=range(4),
        mb=32,
        lazy=True,
    )
    far_up, far_down = shift_mp(far_up, 1), shift_mp(far_down, -1)
    keep, send, extra = call(
        tail_body,
        [((16, 32, 768), BF16), ((16, 32, 768), BF16), ((56, 768), F32)],
        (
            wide,
            key_gain_part,
            small,
            spread2,
            spread4,
            weights_in,
            attn_row,
            *rows,
            *mixed,
            h1,
            *slim,
            *query_gains,
        ),
        scalars=jnp.stack([y_at, z_at, core]),
        scratch=[pltpu.VMEM((LEN, 256), BF16)],
        near=range(3),
        local=(0, 1),
        mb=40,
        lazy=True,
    )
    send = after(send, far_up, far_down)
    extra = sum_mp(extra)
    part_up, part_down, part_own = call(
        parts_body,
        [((TOK, WIDTH), BF16)] * 3,
        (wide, far_up, far_down, proj, *(grad_query[r] for r in (1, 3, 0))),
        near=range(3),
        local=(0, 1, 2),
        lazy=True,
    )
    part_up, part_down = shift_mp(part_up, 1), shift_mp(part_down, -1)
    layer_output = (x_mid + returned.astype(F32)).astype(BF16)
    expert_grads = shard_grads[0].astype(F32) + (shards_got[0].astype(F32) + shards_got[1].astype(F32))
    expert_outs = (
        expert_grads[0:256].reshape(1, 256, FF),
        expert_grads[256:512].reshape(1, 256, FF),
        jnp.concatenate([expert_grads[512:640], expert_grads[640:768]], axis=1).reshape(1, 128, WIDTH),
    )
    first_msg = call(
        ride_first_body,
        [((208, 768), BF16)] * 4,
        (keep, shift_yz(send, 0, 0, 1), extra, shift_yz(extra, 0, 0, 1)),
        near=range(4),
        local=range(4),
    )
    second_msg = call(
        ride_second_body,
        [((112, 768), BF16)] * 4,
        after((first_msg[0], *(shift_axis(first_msg[s], 0, s) for s in (1, 2, 3))), part_up, part_down, layer_output, expert_outs),
        near=range(4),
        local=range(4),
    )
    weight_sum, gain_sum, router_grad, ffn_grad = call(
        ride_last_body,
        [((32, 768), F32), ((4, 768), F32), ((WIDTH, EXPERTS), F32), ((1, WIDTH), F32)],
        (second_msg[0], *(shift_axis(second_msg[s], 1, s) for s in (1, 2, 3))),
        local=range(4),
    )
    attn_gain_grad = jnp.concatenate([gain_sum[0], gain_sum[1, 0:256]])
    (input_grad,) = call(
        input_body,
        [((TOK, WIDTH), F32)],
        (part_own, part_up, part_down, layer_input, attn_row, grad_mid),
        local=(0, 1, 2),
    )

    return (
        layer_output,
        input_grad,
        attn_gain_grad,
        gain_sum[1, 256 : 256 + HDIM],
        gain_sum[1, 384 : 384 + HDIM],
        weight_sum[:, 0:256],
        weight_sum[:, 256:512].reshape(32, 2, 128),
        weight_sum[:, 512:768],
        ffn_grad.reshape(WIDTH),
        router_grad,
        *expert_outs,
    )


def solution(mesh):
    tokens = P(("dp", "mp"), None)
    in_specs = (
        tokens,
        P("dp"),
        tokens,
        P(),
        P(),
        P(),
        P("dp", "mp"),
        P("dp", None, "mp"),
        P("dp", "mp"),
        P(),
        P(),
        P("dp", None, None),
        P("dp", None, None),
        P("dp", None, None),
        tokens,
    )
    out_specs = (
        tokens,
        tokens,
        P(),
        P(),
        P(),
        P("dp", "mp"),
        P("dp", None, "mp"),
        P("dp", "mp"),
        P(),
        P(),
        P("dp", "mp", None),
        P("dp", "mp", None),
        P("dp", "mp", None),
    )
    return jax.shard_map(shards, mesh=mesh, in_specs=in_specs, out_specs=out_specs, check_vma=False)
```

```python
from functools import partial

import jax
import jax.numpy as jnp
import numpy as np
from jax import lax
from jax.experimental import pallas as pl
from jax.experimental.pallas import tpu as pltpu
from jax.sharding import PartitionSpec as P

WIDTH = 1024
HDIM = 64
PITCH = 128
LEN = 1024
TOK = 256
CAP = 96
EXPERTS = 32
FF = 512
SIDE = 16
ROWS = TOK + SIDE
EPS = 1e-06
LOG2E = 1.4426950408889634
F32 = jnp.float32
BF16 = jnp.bfloat16


def nn(left, right):
    return lax.dot_general(left, right, (((1,), (0,)), ((), ())), preferred_element_type=F32)


def nt(left, right):
    return lax.dot_general(left, right, (((1,), (1,)), ((), ())), preferred_element_type=F32)


def tn(left, right):
    return lax.dot_general(left, right, (((0,), (0,)), ((), ())), preferred_element_type=F32)


def spread(heads):
    table = np.zeros((heads * HDIM, heads * PITCH), np.float32)
    for head in range(heads):
        for lane in range(HDIM):
            table[head * HDIM + lane, head * PITCH + lane] = 1.0
    return table


def rope_tables():
    places = np.arange(LEN, dtype=np.float64)
    inverse = 10000.0 ** (-2.0 * np.arange(HDIM // 2, dtype=np.float64) / HDIM)
    angles = places[:, None] * inverse[None, :]
    cos_tab = np.zeros((LEN, PITCH), np.float32)
    sin_tab = np.zeros((LEN, PITCH), np.float32)
    cos_tab[:, : HDIM // 2] = np.cos(angles)
    cos_tab[:, HDIM // 2 : HDIM] = np.cos(angles)
    sin_tab[:, : HDIM // 2] = -np.sin(angles)
    sin_tab[:, HDIM // 2 : HDIM] = np.sin(angles)
    return cos_tab.reshape(LEN // TOK, TOK, PITCH), sin_tab.reshape(LEN // TOK, TOK, PITCH)


def lanes(shape):
    return lax.broadcasted_iota(jnp.int32, shape, 1)


def swap_halves(tensor):
    half = HDIM // 2
    ahead = pltpu.roll(tensor, PITCH - half, 1)
    behind = pltpu.roll(tensor, half, 1)
    return jnp.where(lanes(tensor.shape) < half, ahead, behind)


def head_scale(tensor):
    return lax.rsqrt(jnp.sum(tensor * tensor, axis=1, keepdims=True) * (1.0 / HDIM) + EPS)


def row_scale(tensor):
    return lax.rsqrt(jnp.mean(tensor * tensor, axis=1, keepdims=True) + EPS)


def call(body, out_shape, args, scalars=None, any_in=(), any_out=(), scratch=(), aliases=None, near=(), local=(), mb=24, lazy=False):
    scratch, aliases = list(scratch), aliases or {}
    offset = 0 if scalars is None else 1
    count = offset + len(args)
    fetched = [i for i in range(len(args)) if i not in any_in and i not in local]
    stored = [i for i in range(len(out_shape)) if i not in any_out and i not in near]
    holds = [pltpu.VMEM(args[i].shape, args[i].dtype) for i in fetched]
    holds += [pltpu.VMEM(*out_shape[i]) for i in stored]
    scratch = [*scratch, *holds, pltpu.SemaphoreType.DMA((max(1, len(holds)),))]

    def kernel(*refs):
        refs = list(refs)
        own, sems = refs[len(refs) - len(holds) - 1 : -1], refs[-1]
        refs = refs[: len(refs) - len(holds) - 1]
        copies = {}
        for n, i in enumerate(fetched):
            copies[i] = pltpu.make_async_copy(refs[i + offset], own[n], sems.at[n])
            copies[i].start()
            refs[i + offset] = own[n]
        stores = []
        for n, i in enumerate(stored, len(fetched)):
            stores.append(pltpu.make_async_copy(own[n], refs[i + count], sems.at[n]))
            refs[i + count] = own[n]
        if lazy:
            body(*refs, wait=lambda *which: [copies.pop(i).wait() for i in which])
        else:
            for one in copies.values():
                one.wait()
            body(*refs)
        for one in stores:
            one.start()
        for one in stores:
            one.wait()

    def placed(i, one):
        return pltpu.with_memory_space_constraint(one, pltpu.VMEM if i in local else pltpu.HBM)

    def space(i):
        return pltpu.VMEM if i in local else pltpu.HBM

    args = [placed(i, one) for i, one in enumerate(args)]
    in_specs = [pl.BlockSpec(memory_space=space(i)) for i in range(len(args))]
    out_specs = [pl.BlockSpec(memory_space=pltpu.VMEM if i in near else pltpu.HBM) for i in range(len(out_shape))]
    shapes = [pltpu.VMEM(s, d) if i in near else pltpu.HBM(s, d) for i, (s, d) in enumerate(out_shape)]
    if scalars is not None:
        in_specs = [pl.BlockSpec(memory_space=pltpu.SMEM)] + in_specs
        args = [scalars] + args
    return pl.pallas_call(
        kernel,
        out_shape=shapes,
        in_specs=in_specs,
        out_specs=out_specs,
        scratch_shapes=scratch,
        input_output_aliases={i + offset: o for i, o in aliases.items()},
        compiler_params=pltpu.CompilerParams(vmem_limit_bytes=mb * 1024 * 1024),
        cost_estimate=pl.CostEstimate(flops=1, bytes_accessed=1, transcendentals=0),
    )(*args)


def start_body(sc, routes, ranks_out, coded):
    place = sc[0] * TOK + lax.broadcasted_iota(jnp.int32, (1, TOK), 1)
    names = lax.broadcasted_iota(jnp.int32, (TOK, EXPERTS), 1)
    member = jnp.zeros((TOK, EXPERTS), F32)
    for k in range(routes.shape[1]):
        member = member + jnp.where(routes[:, k : k + 1] == names, 1.0, 0.0)
    member = member.astype(BF16)
    earlier = lax.broadcasted_iota(jnp.int32, (TOK, TOK), 0)
    later = lax.broadcasted_iota(jnp.int32, (TOK, TOK), 1)
    before = jnp.where(earlier < later, 1.0, 0.0).astype(BF16)
    same = jnp.where(earlier == later, 1.0, 0.0).astype(BF16)
    routed = tn(member, same) > 0.5
    ranks = jnp.where(routed, tn(member, before), -1.0)
    ranks_out[...] = ranks
    ranks = jnp.where(routed & (place >= sc[1]), ranks + 128.0, ranks)
    quarter = EXPERTS // 4
    rows = jnp.concatenate([ranks[q * quarter : (q + 1) * quarter] for q in range(4)], axis=1)
    coded[...] = jnp.concatenate([rows, jnp.zeros_like(rows)], axis=0).astype(BF16)


def project_body(sc, own, other, x0, x1, x2, x3, gain, head_gain, cos, sin, spread4, spread2, *refs, wait):
    wait(0, 1)
    outs, raws, pairs, queries, ka, va, out_w, turns = (
        refs[:3], refs[3:7], refs[7:11], refs[11:15], refs[15], refs[16], refs[17], refs[18:22]
    )
    h1, raw_hold, pair_hold, proj, held, sems = refs[22:]
    y_at, z_at, core, mp_at, length = sc[0], sc[1], sc[2], sc[3], sc[4]
    for block in range(16):
        y_rel = (block // 4 - y_at + 4) % 4
        z_rel = (block % 4 - z_at + 4) % 4
        for side in range(2):
            rel = z_rel * 4 + y_rel if side == 0 else y_rel * 4 + z_rel
            part = jnp.where(core == side, own[rel].astype(F32), other[rel].astype(F32)).astype(BF16)
            at = (2 * block + side) * 32
            for piece in range(3):
                held[at : at + 32, piece * 256 : (piece + 1) * 256] = part[piece * 32 : (piece + 1) * 32]
    wait(10, 11)
    proj[:, 0:512] = nn(held[:, 0:256], spread4[...]).astype(BF16)
    proj[:, 512:768] = nn(held[:, 256:384], spread2[...]).astype(BF16)
    proj[:, 768:1024] = nn(held[:, 384:512], spread2[...]).astype(BF16)
    out_w[...] = nn(held[:, 512:768], spread4[...]).astype(BF16)
    copies = [
        pltpu.make_async_copy(proj, outs[1], sems.at[12]),
        pltpu.make_async_copy(held, outs[2], sems.at[13]),
    ]
    for one in copies:
        one.start()
    lane = lanes((TOK, PITCH))
    below = lax.broadcasted_iota(jnp.int32, (TOK, PITCH), 0)
    q_aug = jnp.where(lane == HDIM, 1.0, 0.0)
    v_aug = jnp.where(lane < HDIM + 2, 1.0, 0.0)
    for chunk, x in enumerate((x0, x1, x2, x3)):
        rows = slice(chunk * TOK, (chunk + 1) * TOK)
        at = (mp_at + chunk) % 4
        wait(*((2, 6, 7, 8, 9) if chunk == 0 else (2 + chunk,)))
        xf = x[...].astype(F32)
        normed = (xf * row_scale(xf) * gain[...]).astype(BF16)
        h1[rows, :] = normed
        raw = nn(normed, proj[...])
        raw_hold[rows, :] = raw[:, 0:512]
        pair_hold[rows, :] = raw[:, 512:768]
        cos_t = cos[at]
        sin_t = sin[at]
        turns[chunk][...] = jnp.where(lane < HDIM, cos_t, pltpu.roll(sin_t, HDIM, 1))
        bias = jnp.where(at * TOK + below < length, 0.0, -1e30)
        k_aug = jnp.where(lane == HDIM, bias, jnp.where(lane < HDIM + 4, 1.0, 0.0))
        for head in range(6):
            cols = slice(head * PITCH, (head + 1) * PITCH)
            one = raw[:, cols]
            ready = one * head_scale(one) * head_gain[:, cols]
            turned = ready * cos_t + swap_halves(ready) * sin_t
            if head < 4:
                queries[chunk][:, cols] = jnp.where(lane < HDIM, turned, q_aug).astype(BF16)
            else:
                here = slice((head - 4) * PITCH, (head - 3) * PITCH)
                ka[rows, here] = jnp.where(lane < HDIM, turned, k_aug).astype(BF16)
        for head in range(2):
            va[rows, head * PITCH : (head + 1) * PITCH] = jnp.where(
                lane < HDIM, raw[:, 768 + head * PITCH : 768 + (head + 1) * PITCH], v_aug
            ).astype(BF16)
        here = pl.ds(chunk * TOK, TOK)
        for index, (hold, target) in enumerate(
            ((h1, outs[0].at[here]), (raw_hold, raws[chunk]), (pair_hold, pairs[chunk]))
        ):
            one = pltpu.make_async_copy(hold.at[here], target, sems.at[chunk * 3 + index])
            one.start()
            copies.append(one)
    for one in copies:
        one.wait()


def turn_tables(turn):
    lane = lanes(turn.shape)
    return jnp.where(lane < HDIM, turn, 0.0), jnp.where(lane < HDIM, pltpu.roll(turn, HDIM, 1), 0.0)


def attend_body(qa, ka, va, out_w, *refs):
    branches, (mixed_out, qb_out, mixed, qb, sems) = refs[:-5], refs[-5:]
    lane = lanes((TOK, PITCH))
    for head in range(4):
        cols = slice(head * PITCH, (head + 1) * PITCH)
        kv = slice((head // 2) * PITCH, (head // 2 + 1) * PITCH)
        query = qa[:, cols]
        weight = jnp.exp2(nt(query, ka[:, kv]) * (LOG2E / 8.0)).astype(BF16)
        total = nn(weight, va[:, kv])
        denom = total[:, HDIM : HDIM + 1]
        mixed[:, cols] = jnp.where(lane < HDIM, total / denom, 0.0).astype(BF16)
        level = jnp.log(denom) * -8.0
        high = level.astype(BF16).astype(F32)
        middle = (level - high).astype(BF16).astype(F32)
        low = level - high - middle
        stats = jnp.where(lane == HDIM + 1, high, jnp.where(lane == HDIM + 2, middle, low))
        qb[:, cols] = jnp.where(
            (lane > HDIM) & (lane < HDIM + 4), stats, query.astype(F32)
        ).astype(BF16)
    copies = [
        pltpu.make_async_copy(mixed, mixed_out, sems.at[0]),
        pltpu.make_async_copy(qb, qb_out, sems.at[1]),
    ]
    for one in copies:
        one.start()
    branch = nt(mixed[...], out_w[...]).astype(BF16)
    rows = TOK // len(branches)
    for n, target in enumerate(branches):
        target[...] = branch[n * rows : (n + 1) * rows]
    for one in copies:
        one.wait()


def near_body(up, down, far_up, far_down, out_up, out_down):
    half = TOK // 2
    out_up[:half, :] = (up[:half, :].astype(F32) + far_up[...].astype(F32)).astype(BF16)
    out_up[half:, :] = up[half:, :]
    out_down[:half, :] = down[:half, :]
    out_down[half:, :] = (down[half:, :].astype(F32) + far_down[...].astype(F32)).astype(BF16)


def middle_body(x, p0, p1, p2, gain, coded, x_mid, h2):
    total = x[...].astype(F32) + (p0[...].astype(F32) + (p1[...].astype(F32) + p2[...].astype(F32)))
    x_mid[...] = total
    h2[0:TOK, :] = (total * row_scale(total) * gain[...]).astype(BF16)
    h2[TOK:ROWS, :] = coded[...]


def gates_of(logits, ranks):
    routed = ranks >= 0.0
    masked = jnp.where(routed, logits, -1e30)
    weight = jnp.where(routed, jnp.exp(masked - jnp.max(masked, axis=0, keepdims=True)), 0.0)
    return weight / jnp.sum(weight, axis=0, keepdims=True)


def gates_body(h2, router, ranks, gates):
    gates[...] = gates_of(nt(router[...], h2[0:TOK, :]), ranks[...])


def unfold(rows):
    return jnp.concatenate([rows[:, q * TOK : (q + 1) * TOK] for q in range(4)], axis=0)


def experts_body(pieces, unit, *refs, wait):
    sc = refs[0]
    tokens = refs[1 : 1 + len(pieces)]
    at = 1 + len(pieces)
    cot_all, router = refs[at], refs[at + 1]
    weights = refs[at + 2 : at + 8]
    at = at + 8
    if unit > 0:
        at = at + 6
    y_out, back_a, back_b, taken_all, push_all, hidden_all, gate_all, up_all = refs[at : at + 8]
    cot, y_hold, y_back, t_hold, r_hold, e_hold, h_hold, g_hold, u_hold, sems = refs[at + 8 :]
    cot_in = [pltpu.make_async_copy(cot_all.at[sc[i]], cot.at[i], sems.at[i]) for i in range(4)]
    for one in cot_in:
        one.start()
    tok = [(tokens[index], j) for index, count in enumerate(pieces) for j in range(count)]
    own_names = (sc[4], sc[5])
    names = lax.broadcasted_iota(jnp.int32, (EXPERTS, TOK), 0)
    slots = lax.broadcasted_iota(jnp.int32, (CAP, TOK), 0).astype(F32)
    picks, live_picks = [[], []], [[], []]
    gate_cols = [[], []]
    all_ranks = []
    copies_out = []

    def put(source, target, sem):
        one = pltpu.make_async_copy(source, target, sems.at[sem])
        one.start()
        copies_out.append(one)

    for i in range(4):
        ref, j = tok[i]
        rows = slice(i * CAP, (i + 1) * CAP)
        ranks = unfold(ref[j, TOK : TOK + EXPERTS // 4, :].astype(F32))
        all_ranks.append(ranks)
        for e in range(2):
            rank = jnp.sum(jnp.where(names == own_names[e], ranks, 0.0), axis=0, keepdims=True)
            live_picks[e].append(jnp.where(slots == rank, 1.0, 0.0).astype(BF16))
            picks[e].append(jnp.where((slots == rank) | (slots + 128.0 == rank), 1.0, 0.0).astype(BF16))
        got = nn(jnp.concatenate([picks[0][i], picks[1][i]], axis=0), ref[j, 0:TOK, :]).astype(BF16)
        t_hold[0, rows, :] = got[:CAP]
        t_hold[1, rows, :] = got[CAP:]
    wait(len(pieces) + 1)
    for i in range(4):
        ref, j = tok[i]
        gates = gates_of(nt(router[...], ref[j, 0:TOK, :]), all_ranks[i])
        for e in range(2):
            gate = jnp.sum(jnp.where(names == own_names[e], gates, 0.0), axis=0, keepdims=True)
            gate_cols[e].append(jnp.sum(picks[e][i].astype(F32) * gate, axis=1, keepdims=True))
    here = pl.ds(unit * 4 * CAP, 4 * CAP)
    kept = []
    out_parts = []
    for e in range(2):
        gate_w, up_w, down_w = weights[3 * e : 3 * e + 3]
        put(t_hold.at[e], taken_all.at[e, here], 14 + 5 * e)
        taken = t_hold[e]
        gate_act = nn(taken, gate_w[0])
        up_act = nn(taken, up_w[0])
        sigma = jax.nn.sigmoid(gate_act)
        silu = gate_act * sigma
        slope = up_act * (sigma + silu * (1.0 - sigma))
        hidden = (silu * up_act).astype(BF16)
        h_hold[e] = hidden
        put(h_hold.at[e], hidden_all.at[e, here], 15 + 5 * e)
        result = nn(hidden, down_w[0]).astype(BF16)
        gate_col = jnp.concatenate(gate_cols[e], axis=0)
        kept.append((silu, slope, result, gate_col))
        out_parts.append((result.astype(F32) * gate_col).astype(BF16))
    for i in range(4):
        pick = jnp.concatenate([picks[0][i], picks[1][i]], axis=0)
        rows = slice(i * CAP, (i + 1) * CAP)
        y_hold[i] = tn(pick, jnp.concatenate([out_parts[0][rows], out_parts[1][rows]], axis=0)).astype(BF16)
        put(y_hold.at[i], y_out.at[sc[i]], 28 + i)
    for i in range(4):
        rows = slice(i * CAP, (i + 1) * CAP)
        cot_in[i].wait()
        got = nn(jnp.concatenate([live_picks[0][i], live_picks[1][i]], axis=0), cot[i]).astype(BF16)
        r_hold[0, rows, :] = got[:CAP]
        r_hold[1, rows, :] = got[CAP:]
    marks = [[], []]
    back_parts = []
    for e in range(2):
        gate_w, up_w, down_w = weights[3 * e : 3 * e + 3]
        silu, slope, result, gate_col = kept[e]
        grad_rows = r_hold[e].astype(F32)
        push = (grad_rows * gate_col).astype(BF16)
        e_hold[e] = push
        put(e_hold.at[e], push_all.at[e, here], 16 + 5 * e)
        grad_hidden = nt(push, down_w[0])
        grad_gate = (grad_hidden * slope).astype(BF16)
        grad_up = (grad_hidden * silu).astype(BF16)
        g_hold[e] = grad_gate
        u_hold[e] = grad_up
        put(g_hold.at[e], gate_all.at[e, here], 17 + 5 * e)
        put(u_hold.at[e], up_all.at[e, here], 18 + 5 * e)
        back_parts.append((nt(grad_gate, gate_w[0]) + nt(grad_up, up_w[0])).astype(BF16))
        mark = jnp.sum(grad_rows * result.astype(F32), axis=1, keepdims=True)
        for i in range(4):
            marks[e].append(
                jnp.sum(picks[e][i].astype(F32) * mark[i * CAP : (i + 1) * CAP], axis=0, keepdims=True)
            )
    for i in range(4):
        pick = jnp.concatenate([picks[0][i], picks[1][i]], axis=0)
        rows = slice(i * CAP, (i + 1) * CAP)
        y_back[i, 0:TOK, :] = tn(
            pick, jnp.concatenate([back_parts[0][rows], back_parts[1][rows]], axis=0)
        ).astype(BF16)
        mark = jnp.where(names == own_names[0], marks[0][i], 0.0) + jnp.where(
            names == own_names[1], marks[1][i], 0.0
        )
        high = mark.astype(BF16).astype(F32)
        low = mark - high
        quarter = EXPERTS // 4
        fold = [
            jnp.concatenate([part[q * quarter : (q + 1) * quarter] for q in range(4)], axis=1)
            for part in (high, low)
        ]
        y_back[i, TOK:ROWS, :] = jnp.concatenate(fold, axis=0).astype(BF16)
        put(y_back.at[i], (back_a if i < 2 else back_b).at[i % 2], 24 + i)
    for one in copies_out:
        one.wait()


def expert_weights_body(expert, sc, *refs):
    count = 5 + (1 - expert)
    sources, outs = refs[:5], refs[count : count + (1 if expert == 1 else 5)]
    holds, sums, sems = refs[len(refs) - 9 : len(refs) - 4], refs[len(refs) - 4 : len(refs) - 1], refs[-1]
    copies = [pltpu.make_async_copy(one.at[expert], hold, sems.at[n]) for n, (one, hold) in enumerate(zip(sources, holds))]
    for one in copies:
        one.start()
    taken, gate, up, hidden, push = holds
    copies[0].wait()
    copies[1].wait()
    sums[0][...] = tn(taken[...], gate[...])
    copies[2].wait()
    sums[1][...] = tn(taken[...], up[...])
    copies[3].wait()
    copies[4].wait()
    sums[2][...] = tn(hidden[...], push[...])
    if expert == 1:
        (out,) = outs
        out[0:1024, :] = sums[0][...].astype(BF16)
        out[1024:2048, :] = sums[1][...].astype(BF16)
        out[2048:2560, :] = sums[2][:, 0:FF].astype(BF16)
        out[2560:3072, :] = sums[2][:, FF:WIDTH].astype(BF16)
        return
    got = refs[5]
    for part in range(4):
        at = (sc[0] + part) % 4
        rows = pl.ds(pl.multiple_of(at * 256, 256), 256)

        def put(start, value):
            if part == 2:
                outs[3 + start // 384][start % 384 : start % 384 + 128, :] = value.astype(BF16)
            else:
                outs[min(part, 2)][start : start + 128, :] = value.astype(BF16)

        def more(start, count):
            return got[pl.ds(pl.multiple_of(start + at * count, count), count), :].astype(F32)

        for n, start in enumerate((0, 1024)):
            value = sums[n][rows, :] + more(start, 256)
            put(256 * n, value[0:128])
            put(256 * n + 128, value[128:256])
        rows = pl.ds(pl.multiple_of(at * 128, 128), 128)
        put(512, sums[2][rows, 0:FF] + more(2048, 128))
        put(640, sums[2][rows, FF:WIDTH] + more(2560, 128))


def shard_near_body(up, down, far_up, far_down, out_up, out_down):
    out_up[0:384, :] = (up[0:384, :].astype(F32) + far_up[...].astype(F32)).astype(BF16)
    out_up[384:768, :] = up[384:768, :]
    out_down[0:384, :] = down[0:384, :]
    out_down[384:768, :] = (down[384:768, :].astype(F32) + far_down[...].astype(F32)).astype(BF16)


def expert_weights(saved, expert, mp_at, got=()):
    taken, push, hidden, gate, up = saved
    sources = (taken, gate, up, hidden, push)
    shapes = [((3072, FF), BF16)] if expert == 1 else [((768, FF), BF16)] * 3 + [((384, FF), BF16)] * 2
    return call(
        partial(expert_weights_body, expert),
        shapes,
        (*sources, *got),
        scalars=mp_at.reshape(1),
        any_in=range(5),
        scratch=[pltpu.VMEM(one.shape[1:], one.dtype) for one in sources]
        + [pltpu.VMEM((WIDTH, FF), F32), pltpu.VMEM((WIDTH, FF), F32), pltpu.VMEM((FF, WIDTH), F32)]
        + [pltpu.SemaphoreType.DMA((5,))],
        near=range(len(shapes)),
        local=range(5, 5 + len(got)),
        mb=36,
    )


def token_back_body(sc, r0, r1, r2, h2, x_mid, ranks, gates, router, gain, cot, grad_mid, branch, small):
    total = r0[...].astype(F32) + (r1[...].astype(F32) + r2[...].astype(F32))
    marks = unfold(total[TOK : TOK + 8]) + unfold(total[TOK + 8 : TOK + 16])
    gate = gates[...]
    centre = jnp.sum(gate * marks, axis=0, keepdims=True)
    grad_logits = jnp.where(ranks[...] >= 0.0, gate * (marks - centre), 0.0).astype(BF16)
    router_part = nn(grad_logits, h2[0:TOK, :])
    small[0:32, :] = router_part[:, 0:768]
    small[32:48, 0:256] = router_part[0:16, 768:1024]
    small[32:48, 256:512] = router_part[16:32, 768:1024]
    small[32:48, 512:768] = jnp.zeros((16, 256), F32)
    grad_h2 = total[0:TOK] + tn(grad_logits, router[...])
    x = x_mid[...]
    scale = row_scale(x)
    normed = x * scale
    grad_normed = grad_h2 * gain[...]
    gain_part = jnp.sum(grad_h2 * normed, axis=0, keepdims=True)
    for quarter in range(4):
        small[32 + quarter : 33 + quarter, 512:768] = gain_part[:, quarter * 256 : (quarter + 1) * 256]
    place = sc[0] * TOK + lax.broadcasted_iota(jnp.int32, (TOK, 1), 0)
    out = cot[...].astype(F32) * jnp.where(place < sc[1], 1.0, 0.0) + scale * (
        grad_normed - normed * jnp.mean(grad_normed * normed, axis=1, keepdims=True)
    )
    grad_mid[...] = out
    branch[...] = out.astype(BF16)


def head_back(grad, raw, gain, cos_t, sin_t):
    upstream = grad * cos_t - swap_halves(grad) * sin_t
    scale = head_scale(raw)
    normed = raw * scale
    grad_normed = upstream * gain
    gain_grad = jnp.sum(upstream * normed, axis=0, keepdims=True)
    inner = jnp.sum(grad_normed * normed, axis=1, keepdims=True) * (1.0 / HDIM)
    return scale * (grad_normed - normed * inner), gain_grad


def attend_back_body(first, *refs, wait):
    rows, out_w, qb, mixed, ka, va, raw, head_gain, turn, spread4 = refs[:10]
    rest = refs[10:] if first else refs[11:]
    grad_query, gain_out, slim, both_out, both, sems = rest
    loads = []
    if not first:
        loads = [pltpu.make_async_copy(refs[10].at[g], both.at[g], sems.at[g]) for g in range(2)]
        for one in loads:
            one.start()
    stores = [pltpu.make_async_copy(both.at[g], both_out.at[g], sems.at[2 + g]) for g in range(2)]
    lane = lanes((TOK, PITCH))
    pushed = nn(rows[...], out_w[...]).astype(BF16)
    gain_total = jnp.zeros((1, PITCH), F32)
    wait(2, 3)
    for head in range(4):
        cols = slice(head * PITCH, (head + 1) * PITCH)
        group = head // 2
        kv = slice(group * PITCH, (group + 1) * PITCH)
        grad = pushed[:, cols]
        grad_f = grad.astype(F32)
        delta = -jnp.sum(grad_f * mixed[:, cols].astype(F32), axis=1, keepdims=True)
        high = delta.astype(BF16).astype(F32)
        grad_aug = jnp.where(
            lane == HDIM, high, jnp.where(lane == HDIM + 1, delta - high, grad_f)
        ).astype(BF16)
        query = qb[:, cols]
        probs = jnp.exp2(nt(ka[:, kv], query) * (LOG2E / 8.0))
        inner = nt(va[:, kv], grad_aug)
        grad_scores = (probs * inner).astype(BF16)
        add_k = nn(grad_scores, query)
        add_v = nn(probs.astype(BF16), grad)
        if head % 2 == 0 and first:
            both[group, :, 0:PITCH] = add_k
            both[group, :, PITCH : 2 * PITCH] = add_v
        else:
            if head % 2 == 0:
                loads[group].wait()
            both[group, :, 0:PITCH] += add_k
            both[group, :, PITCH : 2 * PITCH] += add_v
        if head % 2 == 1:
            stores[group].start()
        grad_q = jnp.where(lane < HDIM, tn(grad_scores, ka[:, kv]) * 0.125, 0.0)
        if head == 0:
            wait(6, 7, 8)
            cos_t, sin_t = turn_tables(turn[...])
        back, gain_grad = head_back(grad_q, raw[:, cols], head_gain[:, cols], cos_t, sin_t)
        grad_query[:, cols] = back.astype(BF16)
        gain_total = gain_total + gain_grad
    wait(9)
    slim[...] = nt(grad_query[...], spread4[...]).astype(BF16)
    gain_out[...] = jnp.broadcast_to(gain_total, (8, PITCH))
    for one in stores:
        one.wait()


def keys_back_body(*refs, wait):
    both, raws, turns, head_gain, query, proj = refs[0], refs[1:5], refs[5:9], refs[9], refs[10], refs[11]
    far_up, far_down, wide, gains = refs[12:]
    half = TOK // 2
    lane = lanes((TOK, PITCH))
    key_gain = jnp.zeros((1, PITCH), F32)
    wait(0, 9)
    for chunk in (2, 0, 1, 3):
        wait(1 + chunk, 5 + chunk)
        at = slice(chunk * TOK, (chunk + 1) * TOK)
        cos_t, sin_t = turn_tables(turns[chunk][...])
        for head in range(2):
            cols = slice(head * PITCH, (head + 1) * PITCH)
            grad = jnp.where(lane < HDIM, both[head, at, 0:PITCH] * 0.125, 0.0)
            back, gain_grad = head_back(
                grad, raws[chunk][:, cols], head_gain[:, 512 + head * PITCH : 640 + head * PITCH], cos_t, sin_t
            )
            wide[at, cols] = back.astype(BF16)
            key_gain = key_gain + gain_grad
            wide[at, 256 + head * PITCH : 384 + head * PITCH] = jnp.where(
                lane < HDIM, both[head, at, PITCH : 2 * PITCH], 0.0
            ).astype(BF16)
    wait(10, 11)
    part = nt(query[...], proj[:, 0:512]) + nt(wide[2 * TOK : 3 * TOK, :], proj[:, 512:1024])
    far_up[...] = part[:half].astype(BF16)
    far_down[...] = part[half:].astype(BF16)
    gains[...] = jnp.broadcast_to(key_gain, (8, PITCH))


def parts_body(*refs, wait):
    wide, far_up, far_down, proj, queries, outs = refs[0], refs[1], refs[2], refs[3], refs[4:7], refs[7:10]
    half = TOK // 2
    wait(3)
    for n, chunk in enumerate((1, 3, 0)):
        wait(4 + n)
        at = slice(chunk * TOK, (chunk + 1) * TOK)
        part = nt(queries[n][...], proj[:, 0:512]) + nt(wide[at, :], proj[:, 512:1024])
        if chunk == 1:
            outs[n][:half, :] = (part[:half] + far_up[...].astype(F32)).astype(BF16)
            outs[n][half:, :] = part[half:].astype(BF16)
        elif chunk == 3:
            outs[n][:half, :] = part[:half].astype(BF16)
            outs[n][half:, :] = (part[half:] + far_down[...].astype(F32)).astype(BF16)
        else:
            outs[n][...] = part.astype(BF16)


def tail_body(*refs, wait):
    sc, refs = refs[0], refs[1:]
    wide, key_gain, small, spread2, spread4, weights, gain_row = refs[0:7]
    rows, mixed, h1, slims, query_gains = refs[7:11], refs[11:15], refs[15], refs[16:20], refs[20:24]
    keep, send, extra = refs[24:27]
    (slim_pair,) = refs[27:]
    y_at, z_at, core = sc[0], sc[1], sc[2]
    wait(3, 4)
    slim_pair[:, 0:128] = nt(wide[:, 0:256], spread2[...]).astype(BF16)
    slim_pair[:, 128:256] = nt(wide[:, 256:512], spread2[...]).astype(BF16)
    wait(15)
    pair_total = tn(h1[...], slim_pair[...])
    query_total = jnp.zeros((WIDTH, 256), F32)
    out_total = jnp.zeros((WIDTH, 256), F32)
    for chunk in range(4):
        wait(7 + chunk, 11 + chunk, 16 + chunk)
        at = slice(chunk * TOK, (chunk + 1) * TOK)
        query_total = query_total + tn(h1[at, :], slims[chunk][...])
        out_total = out_total + tn(rows[chunk][...], nt(mixed[chunk][...], spread4[...]).astype(BF16))
    wait(2, 5, 6, 20, 21, 22, 23)
    shares = query_total * weights[:, 0:256].astype(F32) + pair_total * weights[:, 256:512].astype(F32)
    ones = jnp.ones((8, 256), BF16)
    high = shares.astype(BF16)
    low = (shares - high.astype(F32)).astype(BF16)
    total = (nt(ones, high) + nt(ones, low))[0:1, :] / gain_row[...]
    query_gain = (query_gains[0][0:1, :] + query_gains[1][0:1, :]) + (
        query_gains[2][0:1, :] + query_gains[3][0:1, :]
    )
    extra[0:8, :] = jnp.zeros((8, 768), F32)
    extra[8:56, :] = small[...]
    extra[0:1, :] = total[:, 0:768]
    extra[1:2, 0:256] = total[:, 768:1024]
    extra[1:2, 256:384] = query_gain
    extra[1:2, 384:512] = key_gain[0:1, :]
    query_rows, pair_rows, out_rows = query_total.astype(BF16), pair_total.astype(BF16), out_total.astype(BF16)
    for block in range(16):
        y_rel = (block // 4 - y_at + 4) % 4
        z_rel = (block % 4 - z_at + 4) % 4
        for side in range(2):
            at = (2 * block + side) * 32
            rel = y_rel * 4 + z_rel if side == 0 else z_rel * 4 + y_rel

            def put(target):
                target[rel, :, 0:256] = query_rows[at : at + 32]
                target[rel, :, 256:512] = pair_rows[at : at + 32]
                target[rel, :, 512:768] = out_rows[at : at + 32]

            pl.when(core == side)(partial(put, keep))
            pl.when(core != side)(partial(put, send))


def split3(value):
    high = value.astype(BF16).astype(F32)
    middle = (value - high).astype(BF16).astype(F32)
    low = value - high - middle
    return jnp.concatenate([high, middle, low, jnp.zeros((20, 768), F32)], axis=0).astype(BF16)


def join3(rows):
    value = rows.astype(F32)
    return value[0:4] + value[4:8] + value[8:12]


def ride_first_body(keep, got, extra, extra_got, *outs):
    gain = split3(extra[0:4, :] + extra_got[0:4, :])
    router = (extra[8:56, :] + extra_got[8:56, :]).astype(BF16)
    for first in range(4):
        for second in range(4):
            at = first * 4 + second
            outs[first][second * 32 : (second + 1) * 32, :] = (
                keep[at].astype(F32) + got[at].astype(F32)
            ).astype(BF16)
        outs[first][128:160, :] = gain
        outs[first][160:208, :] = router


def add4(own, g1, g2, g3, start, stop):
    return own[start:stop, :].astype(F32) + (
        g1[start:stop, :].astype(F32) + (g2[start:stop, :].astype(F32) + g3[start:stop, :].astype(F32))
    )


def add_gains(own, g1, g2, g3, start):
    stop = start + 32
    return (join3(own[start:stop, :]) + join3(g1[start:stop, :])) + (
        join3(g2[start:stop, :]) + join3(g3[start:stop, :])
    )


def ride_second_body(own, g1, g2, g3, *outs):
    rows = add4(own, g1, g2, g3, 0, 128)
    gain = split3(add_gains(own, g1, g2, g3, 128))
    router = add4(own, g1, g2, g3, 160, 208).astype(BF16)
    for second in range(4):
        outs[second][0:32, :] = rows[second * 32 : (second + 1) * 32].astype(BF16)
        outs[second][32:64, :] = gain
        outs[second][64:112, :] = router


def ride_last_body(own, g1, g2, g3, query, pair, out_w, attn, query_gain, key_gain, router, ffn):
    rows = add4(own, g1, g2, g3, 0, 32)
    query[...] = rows[:, 0:256]
    pair[:, 0, :] = rows[:, 256:384]
    pair[:, 1, :] = rows[:, 384:512]
    out_w[...] = rows[:, 512:768]
    gain = add_gains(own, g1, g2, g3, 32)
    attn[:, 0:768] = gain[0:1, :]
    attn[:, 768:1024] = gain[1:2, 0:256]
    query_gain[...] = gain[1:2, 256:384]
    key_gain[...] = gain[1:2, 384:512]
    total = add4(own, g1, g2, g3, 64, 112)
    router[:, 0:768] = total[0:32]
    router[0:16, 768:1024] = total[32:48, 0:256]
    router[16:32, 768:1024] = total[32:48, 256:512]
    for quarter in range(4):
        ffn[:, quarter * 256 : (quarter + 1) * 256] = total[32 + quarter : 33 + quarter, 512:768]


def input_body(p0, p1, p2, x, gain, grad_mid, out):
    upstream = p0[...].astype(F32) + (p1[...].astype(F32) + p2[...].astype(F32))
    xf = x[...].astype(F32)
    scale = row_scale(xf)
    normed = xf * scale
    grad_normed = upstream * gain[...]
    out[...] = grad_mid[...] + scale * (
        grad_normed - normed * jnp.mean(grad_normed * normed, axis=1, keepdims=True)
    )


def place_of(index):
    return index // 8, (index // 2) % 4, index % 2


def index_of(y, z, core):
    return (y % 4) * 8 + (z % 4) * 2 + core


def shift_yz(tensor, dy, dz, flip=0):
    pairs = []
    for d in range(32):
        y, z, core = place_of(d)
        pairs.append((d, index_of(y + dy, z + dz, core ^ flip)))
    return lax.ppermute(tensor, "dp", pairs)


def shift_axis(tensor, axis, step):
    pairs = []
    for d in range(32):
        y, z, core = place_of(d)
        if (core == 0) == (axis == 0):
            pairs.append((d, index_of(y + step, z, core)))
        else:
            pairs.append((d, index_of(y, z + step, core)))
    return lax.ppermute(tensor, "dp", pairs)


def shift_mp(tensor, step):
    return lax.ppermute(tensor, "mp", [(i, (i + step) % 4) for i in range(4)])


def gather_weights(shard, chunks):
    rows = jnp.stack([shard] + [shift_axis(shard, 0, -s) for s in (1, 2, 3)])
    rows = after(rows, chunks[1], chunks[3])
    own = jnp.concatenate([rows] + [shift_axis(rows, 1, -s) for s in (1, 2, 3)], axis=0)
    near = own
    own = after(own, chunks)
    return near, own, shift_yz(own, 0, 0, 1)


def gather_mp(tensor):
    plus, minus = shift_mp(tensor, -1), shift_mp(tensor, 1)
    half = tensor.shape[0] // 2
    far = jnp.concatenate([shift_mp(plus[:half], -1), shift_mp(minus[half:], 1)], axis=0)
    return [tensor, plus, far, minus]


def after(value, *others):
    return lax.optimization_barrier((value, others))[0]


def add_low(left, *others):
    total = left.astype(F32)
    for one in others:
        total = total + one.astype(F32)
    return total.astype(BF16)


PLANES = [[core + 2 * k for k in range(16)] for core in range(2)]
STEPS = (0, 1, -1, 2)


def shards(
    layer_input,
    lengths,
    routes,
    attn_gain,
    query_gain,
    key_gain,
    query_weight,
    key_value_weight,
    out_weight,
    ffn_gain,
    router_weight,
    gate_weight,
    up_weight,
    down_weight,
    cotangent,
):
    dp_at = lax.axis_index("dp").astype(jnp.int32)
    mp_at = lax.axis_index("mp").astype(jnp.int32)
    y_at, z_at, core = dp_at // 8, (dp_at // 2) % 4, dp_at % 2
    length = lengths[0].astype(jnp.int32)
    cos_np, sin_np = rope_tables()
    cos_tab, sin_tab = jnp.asarray(cos_np), jnp.asarray(sin_np)
    spread4, spread2 = jnp.asarray(spread(4), BF16), jnp.asarray(spread(2), BF16)
    attn_row = attn_gain.reshape(1, WIDTH)
    ffn_row = ffn_gain.reshape(1, WIDTH)
    pad = jnp.zeros((PITCH - HDIM,), F32)
    head_gain = jnp.concatenate([query_gain, pad] * 4 + [key_gain, pad] * 2).reshape(1, 768)
    router = router_weight.T

    chunks = gather_mp(layer_input)
    chunk_at = [(mp_at + r) % 4 for r in range(4)]
    shard = jnp.concatenate([query_weight, key_value_weight.reshape(32, 256), out_weight], axis=0)
    shards_near, shards_own, shards_other = gather_weights(shard, chunks)

    cot_all = lax.all_gather(cotangent, "dp", axis=0, tiled=False, axis_index_groups=PLANES)
    ranks, coded = call(
        start_body,
        [((EXPERTS, TOK), F32), ((SIDE, WIDTH), BF16)],
        after((routes,), shards_near),
        scalars=jnp.stack([mp_at, length]),
    )
    weights_own = (gate_weight, up_weight, down_weight)
    weights_other = tuple(shift_yz(after(w, shards_other), 0, 0, 1) for w in weights_own)

    out = call(
        project_body,
        [((LEN, WIDTH), BF16), ((WIDTH, 1024), BF16), ((WIDTH, 768), BF16)]
        + [((TOK, 512), F32)] * 4
        + [((TOK, 256), F32)] * 4
        + [((TOK, 512), BF16)] * 4
        + [((LEN, 256), BF16), ((LEN, 256), BF16), ((WIDTH, 512), BF16)]
        + [((TOK, PITCH), F32)] * 4,
        (shards_own, shards_other, *chunks, attn_row, head_gain, cos_tab, sin_tab, spread4, spread2),
        scalars=jnp.stack([y_at, z_at, core, mp_at, length]),
        any_out=range(11),
        near=range(11, 18),
        scratch=[
            pltpu.VMEM((LEN, WIDTH), BF16),
            pltpu.VMEM((LEN, 512), F32),
            pltpu.VMEM((LEN, 256), F32),
            pltpu.VMEM((WIDTH, 1024), BF16),
            pltpu.VMEM((WIDTH, 768), BF16),
            pltpu.SemaphoreType.DMA((14,)),
        ],
        mb=40,
        lazy=True,
    )
    h1, proj, weights_in, raw, raw_pair, qa = out[0], out[1], out[2], out[3:7], out[7:11], out[11:15]
    ka, va, out_w, turn_tab = out[15], out[16], out[17], out[18:22]

    qa = list(after(tuple(qa), weights_other))
    mixed, qb = [None] * 4, [None] * 4
    def attend(r, parts=1):
        *made, mixed[r], qb[r] = call(
            attend_body,
            [((TOK // parts, WIDTH), BF16)] * parts + [((TOK, 512), BF16)] * 2,
            (qa[r], ka, va, out_w),
            any_out=(parts, parts + 1),
            scratch=[pltpu.VMEM((TOK, 512), BF16), pltpu.VMEM((TOK, 512), BF16), pltpu.SemaphoreType.DMA((2,))],
            near=range(parts),
            local=(0, 1, 2, 3),
        )
        return made

    branch_up, branch_down = attend(2, 2)
    branch_up, branch_down = shift_mp(branch_up, 1), shift_mp(branch_down, -1)
    (part_up,), (part_down,) = attend(1), attend(3)
    part_up, part_down = call(
        near_body,
        [((TOK, WIDTH), BF16)] * 2,
        (part_up, part_down, branch_up, branch_down),
        near=(0, 1),
        local=range(4),
    )
    (branch,) = attend(0)
    arrived = (branch, shift_mp(part_up, 1), shift_mp(part_down, -1))
    x_mid, h2 = call(
        middle_body,
        [((TOK, WIDTH), F32), ((ROWS, WIDTH), BF16)],
        (layer_input, *arrived, ffn_row, coded),
        near=(1,),
        local=(1, 2, 3),
    )
    (gates,) = call(gates_body, [((EXPERTS, TOK), F32)], (h2, router, ranks))

    plus, minus = shift_axis(h2, 0, -1), shift_axis(h2, 0, 1)
    far_a, far_b = shift_axis(plus[:144], 0, -1), shift_axis(minus[144:], 0, 1)
    near_a, near_b = jnp.stack([h2, plus]), jnp.stack([minus, jnp.concatenate([far_a, far_b], axis=0)])
    plus_a, plus_b = shift_axis(near_a, 1, -1), shift_axis(near_b, 1, -1)
    minus_a, minus_b = shift_axis(near_a, 1, 1), shift_axis(near_b, 1, 1)
    units = [(near_a, near_b), (plus_a, plus_b), (minus_a, minus_b), None]

    first_at = jnp.where(core == 0, y_at, z_at)
    second_at = jnp.where(core == 0, z_at, y_at)
    saved = None
    backs = []
    for u, step in enumerate(STEPS):
        if u == 1:
            far_plus, far_minus = after((plus_a, minus_b), backs[0])
            units[3] = (shift_axis(far_plus, 1, -1), shift_axis(far_minus, 1, 1))
            units[2] = after(units[2], units[3])
        if u == 2:
            plus_b = shift_axis(backs[1][1], 1, 1)
        if u == 3:
            minus_a = shift_axis(backs[2][0], 1, -1)
            units[3] = after(units[3], plus_b)
        second = (second_at + step + 4) % 4
        order = []
        for s in STEPS:
            first = (first_at + s + 4) % 4
            order.append(jnp.where(core == 0, first * 4 + second, second * 4 + first))
        sc = jnp.stack(order + [dp_at, dp_at + 1 - 2 * core]).astype(jnp.int32)
        pieces = tuple(one.shape[0] for one in units[u])
        args = (*units[u], cot_all, router, *weights_own, *weights_other)
        any_in = [len(pieces)]
        aliases = None
        if saved is not None:
            base = len(args)
            aliases = {base + i: (0 if i == 0 else i + 2) for i in range(6)}
            any_in += list(range(base, base + 6))
            args = args + tuple(saved)
        made = call(
            partial(experts_body, pieces, u),
            [
                ((16, TOK, WIDTH), BF16),
                ((2, ROWS, WIDTH), BF16),
                ((2, ROWS, WIDTH), BF16),
                ((2, 16 * CAP, WIDTH), BF16),
                ((2, 16 * CAP, WIDTH), BF16),
                ((2, 16 * CAP, FF), BF16),
                ((2, 16 * CAP, FF), BF16),
                ((2, 16 * CAP, FF), BF16),
            ],
            args,
            scalars=sc,
            any_in=any_in,
            any_out=range(8),
            scratch=[
                pltpu.VMEM((4, TOK, WIDTH), BF16),
                pltpu.VMEM((4, TOK, WIDTH), BF16),
                pltpu.VMEM((4, ROWS, WIDTH), BF16),
                pltpu.VMEM((2, 4 * CAP, WIDTH), BF16),
                pltpu.VMEM((2, 4 * CAP, WIDTH), BF16),
                pltpu.VMEM((2, 4 * CAP, WIDTH), BF16),
                pltpu.VMEM((2, 4 * CAP, FF), BF16),
                pltpu.VMEM((2, 4 * CAP, FF), BF16),
                pltpu.VMEM((2, 4 * CAP, FF), BF16),
                pltpu.SemaphoreType.DMA((32,)),
            ],
            aliases=aliases,
            local=(*range(len(pieces)), *range(len(pieces) + 2, len(pieces) + 8)),
            mb=36,
            lazy=True,
        )
        backs.append(made[1:3])
        saved = [made[0]] + list(made[3:])
    y_out, taken, push, hidden, grad_gate, grad_up = saved

    (b0_a, b0_b), (bp_a, _), (_, bm_b), (bf_a, bf_b) = backs
    half_a, half_b = shift_axis(bf_a, 1, 1), shift_axis(bf_b, 1, -1)
    saved = (taken, push, hidden, grad_gate, grad_up)
    for_other = expert_weights(after(saved, minus_a), 1, mp_at)
    for_other = after(for_other, half_a, half_b)
    plus_late, minus_late = add_low(bp_a, half_a), add_low(bm_b, half_b)
    plus_a, minus_b = shift_axis(plus_late, 1, 1), shift_axis(minus_late, 1, -1)
    from_other = shift_yz(for_other[0], 0, 0, 1)
    shard_grads = expert_weights(after(saved, plus_late, minus_late), 0, mp_at, (from_other,))
    shard_far = shift_mp(shard_grads[3], 1), shift_mp(shard_grads[4], -1)
    b0_a, b0_b = after((b0_a, b0_b), shard_grads)
    line_a = add_low(b0_a, plus_a, minus_a)
    line_b = add_low(b0_b, plus_b, minus_b)
    cut = ROWS // 2 + 8
    far_up, far_down = shift_axis(line_b[1, :cut], 0, 1), shift_axis(line_b[1, cut:], 0, -1)
    send_up = jnp.concatenate([add_low(line_a[1, :cut], far_up), line_a[1, cut:]], axis=0)
    send_down = jnp.concatenate([line_b[0, :cut], add_low(line_b[0, cut:], far_down)], axis=0)
    shard_near = call(
        shard_near_body,
        [((768, FF), BF16)] * 2,
        (shard_grads[1], shard_grads[2], *shard_far),
        near=(0, 1),
        local=range(4),
    )
    send_up, send_down = after((send_up, send_down), shard_near)
    got_up, got_down = shift_axis(send_up, 0, 1), shift_axis(send_down, 0, -1)
    grad_mid, grad_rows, small = call(
        token_back_body,
        [((TOK, WIDTH), F32), ((TOK, WIDTH), BF16), ((48, 768), F32)],
        (line_a[0], got_up, got_down, h2, x_mid, ranks, gates, router, ffn_row, cotangent),
        scalars=jnp.stack([mp_at, length]),
        local=(0, 1, 2),
    )

    returned = lax.psum_scatter(
        after(y_out, grad_rows).reshape(16 * TOK, WIDTH), "dp", scatter_dimension=0, tiled=True, axis_index_groups=PLANES
    )
    both = None
    grad_query, query_gains, slim = [None] * 4, [None] * 4, [None] * 4
    def sum_mp(t):
        return t + (shift_mp(t, 1) + shift_mp(t, 2) + shift_mp(t, 3))

    rows = [grad_rows, shift_mp(grad_rows, -1), None, shift_mp(grad_rows, 1)]
    for turn, r in enumerate((0, 1, 3, 2)):
        if turn == 2:
            near_a, near_b = after((rows[1], rows[3]), grad_query[1])
            rows[2] = jnp.concatenate(
                [shift_mp(near_a[: TOK // 2], -1), shift_mp(near_b[TOK // 2 :], 1)], axis=0
            )
        if turn == 1:
            shard_near = after(shard_near, rows[1], rows[3], grad_query[0])
            shards_got = shift_mp(shard_near[0], 1), shift_mp(shard_near[1], -1)
            rows[r] = after(rows[r], rows[3])
        args = (rows[r], out_w, qb[r], mixed[r], ka, va, raw[r], head_gain, turn_tab[r], spread4)
        first = both is None
        grad_query[r], query_gains[r], slim[r], both = call(
            partial(attend_back_body, first),
            [((TOK, 512), BF16), ((8, PITCH), F32), ((TOK, 256), BF16), ((2, LEN, 256), F32)],
            args if first else args + (both,),
            any_in=() if first else (len(args),),
            any_out=(3,),
            scratch=[pltpu.VMEM((2, LEN, 256), F32), pltpu.SemaphoreType.DMA((4,))],
            aliases=None if first else {len(args): 3},
            local=(0, 1, 4, 5),
            mb=32,
            lazy=True,
        )
    far_up, far_down, wide, key_gain_part = call(
        keys_back_body,
        [((TOK // 2, WIDTH), BF16)] * 2 + [((LEN, 512), BF16), ((8, PITCH), F32)],
        (after(both, shards_got), *raw_pair, *turn_tab, head_gain, grad_query[2], proj),
        near=range(4),
        mb=32,
        lazy=True,
    )
    far_up, far_down = shift_mp(far_up, 1), shift_mp(far_down, -1)
    keep, send, extra = call(
        tail_body,
        [((16, 32, 768), BF16), ((16, 32, 768), BF16), ((56, 768), F32)],
        (
            wide,
            key_gain_part,
            small,
            spread2,
            spread4,
            weights_in,
            attn_row,
            *rows,
            *mixed,
            h1,
            *slim,
            *query_gains,
        ),
        scalars=jnp.stack([y_at, z_at, core]),
        scratch=[pltpu.VMEM((LEN, 256), BF16)],
        near=range(3),
        local=(0, 1),
        mb=40,
        lazy=True,
    )
    send = after(send, far_up, far_down)
    extra = sum_mp(extra)
    part_up, part_down, part_own = call(
        parts_body,
        [((TOK, WIDTH), BF16)] * 3,
        (wide, far_up, far_down, proj, *(grad_query[r] for r in (1, 3, 0))),
        near=range(3),
        local=(0, 1, 2),
        lazy=True,
    )
    part_up, part_down = shift_mp(part_up, 1), shift_mp(part_down, -1)
    layer_output = (x_mid + returned.astype(F32)).astype(BF16)
    expert_grads = shard_grads[0].astype(F32) + (shards_got[0].astype(F32) + shards_got[1].astype(F32))
    expert_outs = (
        expert_grads[0:256].reshape(1, 256, FF),
        expert_grads[256:512].reshape(1, 256, FF),
        jnp.concatenate([expert_grads[512:640], expert_grads[640:768]], axis=1).reshape(1, 128, WIDTH),
    )
    first_msg = call(
        ride_first_body,
        [((208, 768), BF16)] * 4,
        (keep, shift_yz(send, 0, 0, 1), extra, shift_yz(extra, 0, 0, 1)),
        near=range(4),
        local=range(4),
    )
    second_msg = call(
        ride_second_body,
        [((112, 768), BF16)] * 4,
        after((first_msg[0], *(shift_axis(first_msg[s], 0, s) for s in (1, 2, 3))), part_up, part_down, layer_output, expert_outs),
        near=range(4),
        local=range(4),
    )
    query_w_grad, pair_w_grad, out_w_grad, attn_grad, query_gain_grad, key_gain_grad, router_grad, ffn_grad = call(
        ride_last_body,
        [
            ((32, 256), F32),
            ((32, 2, 128), F32),
            ((32, 256), F32),
            ((1, WIDTH), F32),
            ((1, PITCH), F32),
            ((1, PITCH), F32),
            ((EXPERTS, WIDTH), F32),
            ((1, WIDTH), F32),
        ],
        (second_msg[0], *(shift_axis(second_msg[s], 1, s) for s in (1, 2, 3))),
        local=range(4),
    )
    (input_grad,) = call(
        input_body,
        [((TOK, WIDTH), F32)],
        (part_own, part_up, part_down, layer_input, attn_row, grad_mid),
        local=(0, 1, 2),
    )

    return (
        layer_output,
        input_grad,
        attn_grad.reshape(WIDTH),
        query_gain_grad[0, :HDIM],
        key_gain_grad[0, :HDIM],
        query_w_grad,
        pair_w_grad,
        out_w_grad,
        ffn_grad.reshape(WIDTH),
        router_grad.T,
        *expert_outs,
    )


def solution(mesh):
    tokens = P(("dp", "mp"), None)
    in_specs = (
        tokens,
        P("dp"),
        tokens,
        P(),
        P(),
        P(),
        P("dp", "mp"),
        P("dp", None, "mp"),
        P("dp", "mp"),
        P(),
        P(),
        P("dp", None, None),
        P("dp", None, None),
        P("dp", None, None),
        tokens,
    )
    out_specs = (
        tokens,
        tokens,
        P(),
        P(),
        P(),
        P("dp", "mp"),
        P("dp", None, "mp"),
        P("dp", "mp"),
        P(),
        P(),
        P("dp", "mp", None),
        P("dp", "mp", None),
        P("dp", "mp", None),
    )
    return jax.shard_map(shards, mesh=mesh, in_specs=in_specs, out_specs=out_specs, check_vma=False)
```

```python
from functools import partial

import jax
import jax.numpy as jnp
import numpy as np
from jax import lax
from jax.experimental import pallas as pl
from jax.experimental.pallas import tpu as pltpu
from jax.sharding import PartitionSpec as P

WIDTH = 1024
HDIM = 64
PITCH = 128
LEN = 1024
TOK = 256
CAP = 96
EXPERTS = 32
FF = 512
SIDE = 16
ROWS = TOK + SIDE
EPS = 1e-06
LOG2E = 1.4426950408889634
F32 = jnp.float32
BF16 = jnp.bfloat16


def nn(left, right):
    return lax.dot_general(left, right, (((1,), (0,)), ((), ())), preferred_element_type=F32)


def nt(left, right):
    return lax.dot_general(left, right, (((1,), (1,)), ((), ())), preferred_element_type=F32)


def tn(left, right):
    return lax.dot_general(left, right, (((0,), (0,)), ((), ())), preferred_element_type=F32)


def spread(heads):
    table = np.zeros((heads * HDIM, heads * PITCH), np.float32)
    for head in range(heads):
        for lane in range(HDIM):
            table[head * HDIM + lane, head * PITCH + lane] = 1.0
    return table


def rope_tables():
    places = np.arange(LEN, dtype=np.float64)
    inverse = 10000.0 ** (-2.0 * np.arange(HDIM // 2, dtype=np.float64) / HDIM)
    angles = places[:, None] * inverse[None, :]
    cos_tab = np.zeros((LEN, PITCH), np.float32)
    sin_tab = np.zeros((LEN, PITCH), np.float32)
    cos_tab[:, : HDIM // 2] = np.cos(angles)
    cos_tab[:, HDIM // 2 : HDIM] = np.cos(angles)
    sin_tab[:, : HDIM // 2] = -np.sin(angles)
    sin_tab[:, HDIM // 2 : HDIM] = np.sin(angles)
    return cos_tab.reshape(LEN // TOK, TOK, PITCH), sin_tab.reshape(LEN // TOK, TOK, PITCH)


def lanes(shape):
    return lax.broadcasted_iota(jnp.int32, shape, 1)


def swap_halves(tensor):
    half = HDIM // 2
    ahead = pltpu.roll(tensor, PITCH - half, 1)
    behind = pltpu.roll(tensor, half, 1)
    return jnp.where(lanes(tensor.shape) < half, ahead, behind)


def head_scale(tensor):
    return lax.rsqrt(jnp.sum(tensor * tensor, axis=1, keepdims=True) * (1.0 / HDIM) + EPS)


def row_scale(tensor):
    return lax.rsqrt(jnp.mean(tensor * tensor, axis=1, keepdims=True) + EPS)


def call(body, out_shape, args, scalars=None, any_in=(), any_out=(), scratch=(), aliases=None, near=(), local=(), mb=24, lazy=False):
    scratch, aliases = list(scratch), aliases or {}
    offset = 0 if scalars is None else 1
    count = offset + len(args)
    fetched = [i for i in range(len(args)) if i not in any_in and i not in local]
    stored = [i for i in range(len(out_shape)) if i not in any_out and i not in near]
    holds = [pltpu.VMEM(args[i].shape, args[i].dtype) for i in fetched]
    holds += [pltpu.VMEM(*out_shape[i]) for i in stored]
    scratch = [*scratch, *holds, pltpu.SemaphoreType.DMA((max(1, len(holds)),))]

    def kernel(*refs):
        refs = list(refs)
        own, sems = refs[len(refs) - len(holds) - 1 : -1], refs[-1]
        refs = refs[: len(refs) - len(holds) - 1]
        copies = {}
        for n, i in enumerate(fetched):
            copies[i] = pltpu.make_async_copy(refs[i + offset], own[n], sems.at[n])
            copies[i].start()
            refs[i + offset] = own[n]
        stores = []
        for n, i in enumerate(stored, len(fetched)):
            stores.append(pltpu.make_async_copy(own[n], refs[i + count], sems.at[n]))
            refs[i + count] = own[n]
        if lazy:
            body(*refs, wait=lambda *which: [copies.pop(i).wait() for i in which])
        else:
            for one in copies.values():
                one.wait()
            body(*refs)
        for one in stores:
            one.start()
        for one in stores:
            one.wait()

    def placed(i, one):
        return pltpu.with_memory_space_constraint(one, pltpu.VMEM if i in local else pltpu.HBM)

    def space(i):
        return pltpu.VMEM if i in local else pltpu.HBM

    args = [placed(i, one) for i, one in enumerate(args)]
    in_specs = [pl.BlockSpec(memory_space=space(i)) for i in range(len(args))]
    out_specs = [pl.BlockSpec(memory_space=pltpu.VMEM if i in near else pltpu.HBM) for i in range(len(out_shape))]
    shapes = [pltpu.VMEM(s, d) if i in near else pltpu.HBM(s, d) for i, (s, d) in enumerate(out_shape)]
    if scalars is not None:
        in_specs = [pl.BlockSpec(memory_space=pltpu.SMEM)] + in_specs
        args = [scalars] + args
    return pl.pallas_call(
        kernel,
        out_shape=shapes,
        in_specs=in_specs,
        out_specs=out_specs,
        scratch_shapes=scratch,
        input_output_aliases={i + offset: o for i, o in aliases.items()},
        compiler_params=pltpu.CompilerParams(vmem_limit_bytes=mb * 1024 * 1024),
        cost_estimate=pl.CostEstimate(flops=1, bytes_accessed=1, transcendentals=0),
    )(*args)


def start_body(sc, routes, ranks_out, coded):
    place = sc[0] * TOK + lax.broadcasted_iota(jnp.int32, (1, TOK), 1)
    names = lax.broadcasted_iota(jnp.int32, (TOK, EXPERTS), 1)
    member = jnp.zeros((TOK, EXPERTS), F32)
    for k in range(routes.shape[1]):
        member = member + jnp.where(routes[:, k : k + 1] == names, 1.0, 0.0)
    member = member.astype(BF16)
    earlier = lax.broadcasted_iota(jnp.int32, (TOK, TOK), 0)
    later = lax.broadcasted_iota(jnp.int32, (TOK, TOK), 1)
    before = jnp.where(earlier < later, 1.0, 0.0).astype(BF16)
    same = jnp.where(earlier == later, 1.0, 0.0).astype(BF16)
    routed = tn(member, same) > 0.5
    ranks = jnp.where(routed, tn(member, before), -1.0)
    ranks_out[...] = ranks
    ranks = jnp.where(routed & (place >= sc[1]), ranks + 128.0, ranks)
    quarter = EXPERTS // 4
    rows = jnp.concatenate([ranks[q * quarter : (q + 1) * quarter] for q in range(4)], axis=1)
    coded[...] = jnp.concatenate([rows, jnp.zeros_like(rows)], axis=0).astype(BF16)


def project_body(sc, own, other, x0, x1, x2, x3, gain, head_gain, cos, sin, spread4, spread2, *refs, wait):
    wait(0, 1)
    outs, raws, pairs, queries, ka, va, out_w, turns = (
        refs[:3], refs[3:7], refs[7:11], refs[11:15], refs[15], refs[16], refs[17], refs[18:22]
    )
    h1, raw_hold, pair_hold, proj, held, sems = refs[22:]
    y_at, z_at, core, mp_at, length = sc[0], sc[1], sc[2], sc[3], sc[4]
    for block in range(16):
        y_rel = (block // 4 - y_at + 4) % 4
        z_rel = (block % 4 - z_at + 4) % 4
        for side in range(2):
            rel = z_rel * 4 + y_rel if side == 0 else y_rel * 4 + z_rel
            part = jnp.where(core == side, own[rel].astype(F32), other[rel].astype(F32)).astype(BF16)
            at = (2 * block + side) * 32
            for piece in range(3):
                held[at : at + 32, piece * 256 : (piece + 1) * 256] = part[piece * 32 : (piece + 1) * 32]
    wait(10, 11)
    proj[:, 0:512] = nn(held[:, 0:256], spread4[...]).astype(BF16)
    proj[:, 512:768] = nn(held[:, 256:384], spread2[...]).astype(BF16)
    proj[:, 768:1024] = nn(held[:, 384:512], spread2[...]).astype(BF16)
    out_w[...] = nn(held[:, 512:768], spread4[...]).astype(BF16)
    copies = [
        pltpu.make_async_copy(proj, outs[1], sems.at[12]),
        pltpu.make_async_copy(held, outs[2], sems.at[13]),
    ]
    for one in copies:
        one.start()
    lane = lanes((TOK, PITCH))
    below = lax.broadcasted_iota(jnp.int32, (TOK, PITCH), 0)
    q_aug = jnp.where(lane == HDIM, 1.0, 0.0)
    v_aug = jnp.where(lane < HDIM + 2, 1.0, 0.0)
    for chunk, x in enumerate((x0, x1, x2, x3)):
        rows = slice(chunk * TOK, (chunk + 1) * TOK)
        at = (mp_at + chunk) % 4
        wait(*((2, 6, 7, 8, 9) if chunk == 0 else (2 + chunk,)))
        xf = x[...].astype(F32)
        normed = (xf * row_scale(xf) * gain[...]).astype(BF16)
        h1[rows, :] = normed
        raw = nn(normed, proj[...])
        raw_hold[rows, :] = raw[:, 0:512]
        pair_hold[rows, :] = raw[:, 512:768]
        cos_t = cos[at]
        sin_t = sin[at]
        turns[chunk][...] = jnp.where(lane < HDIM, cos_t, pltpu.roll(sin_t, HDIM, 1))
        bias = jnp.where(at * TOK + below < length, 0.0, -1e30)
        k_aug = jnp.where(lane == HDIM, bias, jnp.where(lane < HDIM + 4, 1.0, 0.0))
        for head in range(6):
            cols = slice(head * PITCH, (head + 1) * PITCH)
            one = raw[:, cols]
            ready = one * head_scale(one) * head_gain[:, cols]
            turned = ready * cos_t + swap_halves(ready) * sin_t
            if head < 4:
                queries[chunk][:, cols] = jnp.where(lane < HDIM, turned, q_aug).astype(BF16)
            else:
                here = slice((head - 4) * PITCH, (head - 3) * PITCH)
                ka[rows, here] = jnp.where(lane < HDIM, turned, k_aug).astype(BF16)
        for head in range(2):
            va[rows, head * PITCH : (head + 1) * PITCH] = jnp.where(
                lane < HDIM, raw[:, 768 + head * PITCH : 768 + (head + 1) * PITCH], v_aug
            ).astype(BF16)
        here = pl.ds(chunk * TOK, TOK)
        for index, (hold, target) in enumerate(
            ((h1, outs[0].at[here]), (raw_hold, raws[chunk]), (pair_hold, pairs[chunk]))
        ):
            one = pltpu.make_async_copy(hold.at[here], target, sems.at[chunk * 3 + index])
            one.start()
            copies.append(one)
    for one in copies:
        one.wait()


def turn_tables(turn):
    lane = lanes(turn.shape)
    return jnp.where(lane < HDIM, turn, 0.0), jnp.where(lane < HDIM, pltpu.roll(turn, HDIM, 1), 0.0)


def attend_body(qa, ka, va, out_w, *refs):
    branches, (mixed_out, qb_out, mixed, qb, sems) = refs[:-5], refs[-5:]
    lane = lanes((TOK, PITCH))
    for head in range(4):
        cols = slice(head * PITCH, (head + 1) * PITCH)
        kv = slice((head // 2) * PITCH, (head // 2 + 1) * PITCH)
        query = qa[:, cols]
        weight = jnp.exp2(nt(query, ka[:, kv]) * (LOG2E / 8.0)).astype(BF16)
        total = nn(weight, va[:, kv])
        denom = total[:, HDIM : HDIM + 1]
        mixed[:, cols] = jnp.where(lane < HDIM, total / denom, 0.0).astype(BF16)
        level = jnp.log(denom) * -8.0
        high = level.astype(BF16).astype(F32)
        middle = (level - high).astype(BF16).astype(F32)
        low = level - high - middle
        stats = jnp.where(lane == HDIM + 1, high, jnp.where(lane == HDIM + 2, middle, low))
        qb[:, cols] = jnp.where(
            (lane > HDIM) & (lane < HDIM + 4), stats, query.astype(F32)
        ).astype(BF16)
    copies = [
        pltpu.make_async_copy(mixed, mixed_out, sems.at[0]),
        pltpu.make_async_copy(qb, qb_out, sems.at[1]),
    ]
    for one in copies:
        one.start()
    branch = nt(mixed[...], out_w[...]).astype(BF16)
    rows = TOK // len(branches)
    for n, target in enumerate(branches):
        target[...] = branch[n * rows : (n + 1) * rows]
    for one in copies:
        one.wait()


def near_body(up, down, far_up, far_down, out_up, out_down):
    half = TOK // 2
    out_up[:half, :] = (up[:half, :].astype(F32) + far_up[...].astype(F32)).astype(BF16)
    out_up[half:, :] = up[half:, :]
    out_down[:half, :] = down[:half, :]
    out_down[half:, :] = (down[half:, :].astype(F32) + far_down[...].astype(F32)).astype(BF16)


def middle_body(x, p0, p1, p2, gain, coded, x_mid, h2):
    total = x[...].astype(F32) + (p0[...].astype(F32) + (p1[...].astype(F32) + p2[...].astype(F32)))
    x_mid[...] = total
    h2[0:TOK, :] = (total * row_scale(total) * gain[...]).astype(BF16)
    h2[TOK:ROWS, :] = coded[...]


def gates_of(logits, ranks):
    routed = ranks >= 0.0
    masked = jnp.where(routed, logits, -1e30)
    weight = jnp.where(routed, jnp.exp(masked - jnp.max(masked, axis=0, keepdims=True)), 0.0)
    return weight / jnp.sum(weight, axis=0, keepdims=True)


def gates_body(h2, router, ranks, gates):
    gates[...] = gates_of(nt(router[...], h2[0:TOK, :]), ranks[...])


def unfold(rows):
    return jnp.concatenate([rows[:, q * TOK : (q + 1) * TOK] for q in range(4)], axis=0)


def experts_body(pieces, unit, *refs, wait):
    sc = refs[0]
    tokens = refs[1 : 1 + len(pieces)]
    at = 1 + len(pieces)
    cot_all, router = refs[at], refs[at + 1]
    weights = refs[at + 2 : at + 8]
    at = at + 8
    if unit > 0:
        at = at + 6
    y_out, back_a, back_b, taken_all, push_all, hidden_all, gate_all, up_all = refs[at : at + 8]
    cot, y_hold, y_back, t_hold, r_hold, e_hold, h_hold, g_hold, u_hold, sems = refs[at + 8 :]
    cot_in = [pltpu.make_async_copy(cot_all.at[sc[i]], cot.at[i], sems.at[i]) for i in range(4)]
    for one in cot_in:
        one.start()
    tok = [(tokens[index], j) for index, count in enumerate(pieces) for j in range(count)]
    own_names = (sc[4], sc[5])
    names = lax.broadcasted_iota(jnp.int32, (EXPERTS, TOK), 0)
    slots = lax.broadcasted_iota(jnp.int32, (CAP, TOK), 0).astype(F32)
    picks, live_picks = [[], []], [[], []]
    gate_cols = [[], []]
    all_ranks = []
    copies_out = []

    def put(source, target, sem):
        one = pltpu.make_async_copy(source, target, sems.at[sem])
        one.start()
        copies_out.append(one)

    for i in range(4):
        ref, j = tok[i]
        rows = slice(i * CAP, (i + 1) * CAP)
        ranks = unfold(ref[j, TOK:ROWS, :].astype(F32)[: EXPERTS // 4])
        all_ranks.append(ranks)
        for e in range(2):
            rank = jnp.sum(jnp.where(names == own_names[e], ranks, 0.0), axis=0, keepdims=True)
            live_picks[e].append(jnp.where(slots == rank, 1.0, 0.0).astype(BF16))
            picks[e].append(jnp.where((slots == rank) | (slots + 128.0 == rank), 1.0, 0.0).astype(BF16))
        got = nn(jnp.concatenate([picks[0][i], picks[1][i]], axis=0), ref[j, 0:TOK, :]).astype(BF16)
        t_hold[0, rows, :] = got[:CAP]
        t_hold[1, rows, :] = got[CAP:]
    wait(len(pieces) + 1)
    for i in range(4):
        ref, j = tok[i]
        gates = gates_of(nt(router[...], ref[j, 0:TOK, :]), all_ranks[i])
        for e in range(2):
            gate = jnp.sum(jnp.where(names == own_names[e], gates, 0.0), axis=0, keepdims=True)
            gate_cols[e].append(jnp.sum(picks[e][i].astype(F32) * gate, axis=1, keepdims=True))
    here = pl.ds(unit * 4 * CAP, 4 * CAP)
    kept = []
    out_parts = []
    for e in range(2):
        gate_w, up_w, down_w = weights[3 * e : 3 * e + 3]
        put(t_hold.at[e], taken_all.at[e, here], 14 + 5 * e)
        taken = t_hold[e]
        gate_act = nn(taken, gate_w[0])
        up_act = nn(taken, up_w[0])
        sigma = jax.nn.sigmoid(gate_act)
        silu = gate_act * sigma
        slope = up_act * (sigma + silu * (1.0 - sigma))
        hidden = (silu * up_act).astype(BF16)
        h_hold[e] = hidden
        put(h_hold.at[e], hidden_all.at[e, here], 15 + 5 * e)
        result = nn(hidden, down_w[0]).astype(BF16)
        gate_col = jnp.concatenate(gate_cols[e], axis=0)
        kept.append((silu, slope, result, gate_col))
        out_parts.append((result.astype(F32) * gate_col).astype(BF16))
    for i in range(4):
        pick = jnp.concatenate([picks[0][i], picks[1][i]], axis=0)
        rows = slice(i * CAP, (i + 1) * CAP)
        y_hold[i] = tn(pick, jnp.concatenate([out_parts[0][rows], out_parts[1][rows]], axis=0)).astype(BF16)
        put(y_hold.at[i], y_out.at[sc[i]], 28 + i)
    for i in range(4):
        rows = slice(i * CAP, (i + 1) * CAP)
        cot_in[i].wait()
        got = nn(jnp.concatenate([live_picks[0][i], live_picks[1][i]], axis=0), cot[i]).astype(BF16)
        r_hold[0, rows, :] = got[:CAP]
        r_hold[1, rows, :] = got[CAP:]
    marks = [[], []]
    back_parts = []
    for e in range(2):
        gate_w, up_w, down_w = weights[3 * e : 3 * e + 3]
        silu, slope, result, gate_col = kept[e]
        grad_rows = r_hold[e].astype(F32)
        push = (grad_rows * gate_col).astype(BF16)
        e_hold[e] = push
        put(e_hold.at[e], push_all.at[e, here], 16 + 5 * e)
        grad_hidden = nt(push, down_w[0])
        grad_gate = (grad_hidden * slope).astype(BF16)
        grad_up = (grad_hidden * silu).astype(BF16)
        g_hold[e] = grad_gate
        u_hold[e] = grad_up
        put(g_hold.at[e], gate_all.at[e, here], 17 + 5 * e)
        put(u_hold.at[e], up_all.at[e, here], 18 + 5 * e)
        back_parts.append((nt(grad_gate, gate_w[0]) + nt(grad_up, up_w[0])).astype(BF16))
        mark = jnp.sum(grad_rows * result.astype(F32), axis=1, keepdims=True)
        for i in range(4):
            marks[e].append(
                jnp.sum(picks[e][i].astype(F32) * mark[i * CAP : (i + 1) * CAP], axis=0, keepdims=True)
            )
    for i in range(4):
        pick = jnp.concatenate([picks[0][i], picks[1][i]], axis=0)
        rows = slice(i * CAP, (i + 1) * CAP)
        y_back[i, 0:TOK, :] = tn(
            pick, jnp.concatenate([back_parts[0][rows], back_parts[1][rows]], axis=0)
        ).astype(BF16)
        mark = jnp.where(names == own_names[0], marks[0][i], 0.0) + jnp.where(
            names == own_names[1], marks[1][i], 0.0
        )
        high = mark.astype(BF16).astype(F32)
        low = mark - high
        quarter = EXPERTS // 4
        fold = [
            jnp.concatenate([part[q * quarter : (q + 1) * quarter] for q in range(4)], axis=1)
            for part in (high, low)
        ]
        y_back[i, TOK:ROWS, :] = jnp.concatenate(fold, axis=0).astype(BF16)
        put(y_back.at[i], (back_a if i < 2 else back_b).at[i % 2], 24 + i)
    for one in copies_out:
        one.wait()


def expert_weights_body(expert, sc, *refs):
    count = 5 + (1 - expert)
    sources, outs = refs[:5], refs[count : count + (1 if expert == 1 else 5)]
    holds, sums, sems = refs[len(refs) - 9 : len(refs) - 4], refs[len(refs) - 4 : len(refs) - 1], refs[-1]
    copies = [pltpu.make_async_copy(one.at[expert], hold, sems.at[n]) for n, (one, hold) in enumerate(zip(sources, holds))]
    for one in copies:
        one.start()
    taken, gate, up, hidden, push = holds
    copies[0].wait()
    copies[1].wait()
    sums[0][...] = tn(taken[...], gate[...])
    copies[2].wait()
    sums[1][...] = tn(taken[...], up[...])
    copies[3].wait()
    copies[4].wait()
    sums[2][...] = tn(hidden[...], push[...])
    if expert == 1:
        (out,) = outs
        out[0:1024, :] = sums[0][...].astype(BF16)
        out[1024:2048, :] = sums[1][...].astype(BF16)
        out[2048:2560, :] = sums[2][:, 0:FF].astype(BF16)
        out[2560:3072, :] = sums[2][:, FF:WIDTH].astype(BF16)
        return
    got = refs[5]
    for part in range(4):
        at = (sc[0] + part) % 4
        rows = pl.ds(pl.multiple_of(at * 256, 256), 256)

        def put(start, value):
            if part == 2:
                outs[3 + start // 384][start % 384 : start % 384 + 128, :] = value.astype(BF16)
            else:
                outs[min(part, 2)][start : start + 128, :] = value.astype(BF16)

        def more(start, count):
            return got[pl.ds(pl.multiple_of(start + at * count, count), count), :].astype(F32)

        for n, start in enumerate((0, 1024)):
            value = sums[n][rows, :] + more(start, 256)
            put(256 * n, value[0:128])
            put(256 * n + 128, value[128:256])
        rows = pl.ds(pl.multiple_of(at * 128, 128), 128)
        put(512, sums[2][rows, 0:FF] + more(2048, 128))
        put(640, sums[2][rows, FF:WIDTH] + more(2560, 128))


def shard_near_body(up, down, far_up, far_down, out_up, out_down):
    out_up[0:384, :] = (up[0:384, :].astype(F32) + far_up[...].astype(F32)).astype(BF16)
    out_up[384:768, :] = up[384:768, :]
    out_down[0:384, :] = down[0:384, :]
    out_down[384:768, :] = (down[384:768, :].astype(F32) + far_down[...].astype(F32)).astype(BF16)


def expert_weights(saved, expert, mp_at, got=()):
    taken, push, hidden, gate, up = saved
    sources = (taken, gate, up, hidden, push)
    shapes = [((3072, FF), BF16)] if expert == 1 else [((768, FF), BF16)] * 3 + [((384, FF), BF16)] * 2
    return call(
        partial(expert_weights_body, expert),
        shapes,
        (*sources, *got),
        scalars=mp_at.reshape(1),
        any_in=range(5),
        scratch=[pltpu.VMEM(one.shape[1:], one.dtype) for one in sources]
        + [pltpu.VMEM((WIDTH, FF), F32), pltpu.VMEM((WIDTH, FF), F32), pltpu.VMEM((FF, WIDTH), F32)]
        + [pltpu.SemaphoreType.DMA((5,))],
        near=range(len(shapes)),
        local=range(5, 5 + len(got)),
        mb=36,
    )


def token_back_body(sc, r0, r1, r2, h2, x_mid, ranks, gates, router, gain, cot, grad_mid, branch, small, wait):
    total = r0[...].astype(F32) + (r1[...].astype(F32) + r2[...].astype(F32))
    marks = unfold(total[TOK : TOK + 8]) + unfold(total[TOK + 8 : TOK + 16])
    wait(5, 6)
    gate = gates[...]
    centre = jnp.sum(gate * marks, axis=0, keepdims=True)
    grad_logits = jnp.where(ranks[...] >= 0.0, gate * (marks - centre), 0.0).astype(BF16)
    wait(3)
    router_part = nn(grad_logits, h2[0:TOK, :])
    small[0:32, :] = router_part[:, 0:768]
    small[32:48, 0:256] = router_part[0:16, 768:1024]
    small[32:48, 256:512] = router_part[16:32, 768:1024]
    small[32:48, 512:768] = jnp.zeros((16, 256), F32)
    wait(7)
    grad_h2 = total[0:TOK] + tn(grad_logits, router[...])
    wait(4, 8, 9)
    x = x_mid[...]
    scale = row_scale(x)
    normed = x * scale
    grad_normed = grad_h2 * gain[...]
    gain_part = jnp.sum(grad_h2 * normed, axis=0, keepdims=True)
    for quarter in range(4):
        small[32 + quarter : 33 + quarter, 512:768] = gain_part[:, quarter * 256 : (quarter + 1) * 256]
    place = sc[0] * TOK + lax.broadcasted_iota(jnp.int32, (TOK, 1), 0)
    out = cot[...].astype(F32) * jnp.where(place < sc[1], 1.0, 0.0) + scale * (
        grad_normed - normed * jnp.mean(grad_normed * normed, axis=1, keepdims=True)
    )
    grad_mid[...] = out
    branch[...] = out.astype(BF16)


def head_back(grad, raw, gain, cos_t, sin_t):
    upstream = grad * cos_t - swap_halves(grad) * sin_t
    scale = head_scale(raw)
    normed = raw * scale
    grad_normed = upstream * gain
    gain_grad = jnp.sum(upstream * normed, axis=0, keepdims=True)
    inner = jnp.sum(grad_normed * normed, axis=1, keepdims=True) * (1.0 / HDIM)
    return scale * (grad_normed - normed * inner), gain_grad


def attend_back_body(first, *refs, wait):
    rows, out_w, qb, mixed, ka, va, raw, head_gain, turn, spread4 = refs[:10]
    rest = refs[10:] if first else refs[11:]
    grad_query, gain_out, slim, both_out, both, sems = rest
    loads = []
    if not first:
        loads = [pltpu.make_async_copy(refs[10].at[g], both.at[g], sems.at[g]) for g in range(2)]
        for one in loads:
            one.start()
    stores = [pltpu.make_async_copy(both.at[g], both_out.at[g], sems.at[2 + g]) for g in range(2)]
    lane = lanes((TOK, PITCH))
    pushed = nn(rows[...], out_w[...]).astype(BF16)
    gain_total = jnp.zeros((1, PITCH), F32)
    wait(2, 3)
    for head in range(4):
        cols = slice(head * PITCH, (head + 1) * PITCH)
        group = head // 2
        kv = slice(group * PITCH, (group + 1) * PITCH)
        grad = pushed[:, cols]
        grad_f = grad.astype(F32)
        delta = -jnp.sum(grad_f * mixed[:, cols].astype(F32), axis=1, keepdims=True)
        high = delta.astype(BF16).astype(F32)
        grad_aug = jnp.where(
            lane == HDIM, high, jnp.where(lane == HDIM + 1, delta - high, grad_f)
        ).astype(BF16)
        query = qb[:, cols]
        probs = jnp.exp2(nt(ka[:, kv], query) * (LOG2E / 8.0))
        inner = nt(va[:, kv], grad_aug)
        grad_scores = (probs * inner).astype(BF16)
        add_k = nn(grad_scores, query)
        add_v = nn(probs.astype(BF16), grad)
        if head % 2 == 0 and first:
            both[group, :, 0:PITCH] = add_k
            both[group, :, PITCH : 2 * PITCH] = add_v
        else:
            if head % 2 == 0:
                loads[group].wait()
            both[group, :, 0:PITCH] += add_k
            both[group, :, PITCH : 2 * PITCH] += add_v
        if head % 2 == 1:
            stores[group].start()
        grad_q = jnp.where(lane < HDIM, tn(grad_scores, ka[:, kv]) * 0.125, 0.0)
        if head == 0:
            wait(6, 7, 8)
            cos_t, sin_t = turn_tables(turn[...])
        back, gain_grad = head_back(grad_q, raw[:, cols], head_gain[:, cols], cos_t, sin_t)
        grad_query[:, cols] = back.astype(BF16)
        gain_total = gain_total + gain_grad
    wait(9)
    slim[...] = nt(grad_query[...], spread4[...]).astype(BF16)
    gain_out[...] = jnp.broadcast_to(gain_total, (8, PITCH))
    for one in stores:
        one.wait()


def keys_back_body(*refs, wait):
    both, raws, turns, head_gain, query, proj = refs[0], refs[1:5], refs[5:9], refs[9], refs[10], refs[11]
    far_up, far_down, wide, gains = refs[12:]
    half = TOK // 2
    lane = lanes((TOK, PITCH))
    key_gain = jnp.zeros((1, PITCH), F32)
    wait(0, 9)
    for chunk in (2, 0, 1, 3):
        wait(1 + chunk, 5 + chunk)
        at = slice(chunk * TOK, (chunk + 1) * TOK)
        cos_t, sin_t = turn_tables(turns[chunk][...])
        for head in range(2):
            cols = slice(head * PITCH, (head + 1) * PITCH)
            grad = jnp.where(lane < HDIM, both[head, at, 0:PITCH] * 0.125, 0.0)
            back, gain_grad = head_back(
                grad, raws[chunk][:, cols], head_gain[:, 512 + head * PITCH : 640 + head * PITCH], cos_t, sin_t
            )
            wide[at, cols] = back.astype(BF16)
            key_gain = key_gain + gain_grad
            wide[at, 256 + head * PITCH : 384 + head * PITCH] = jnp.where(
                lane < HDIM, both[head, at, PITCH : 2 * PITCH], 0.0
            ).astype(BF16)
    wait(10, 11)
    part = nt(query[...], proj[:, 0:512]) + nt(wide[2 * TOK : 3 * TOK, :], proj[:, 512:1024])
    far_up[...] = part[:half].astype(BF16)
    far_down[...] = part[half:].astype(BF16)
    gains[...] = jnp.broadcast_to(key_gain, (8, PITCH))


def parts_body(*refs, wait):
    wide, far_up, far_down, proj, queries, outs = refs[0], refs[1], refs[2], refs[3], refs[4:7], refs[7:10]
    half = TOK // 2
    wait(3)
    for n, chunk in enumerate((1, 3, 0)):
        wait(4 + n)
        at = slice(chunk * TOK, (chunk + 1) * TOK)
        part = nt(queries[n][...], proj[:, 0:512]) + nt(wide[at, :], proj[:, 512:1024])
        if chunk == 1:
            outs[n][:half, :] = (part[:half] + far_up[...].astype(F32)).astype(BF16)
            outs[n][half:, :] = part[half:].astype(BF16)
        elif chunk == 3:
            outs[n][:half, :] = part[:half].astype(BF16)
            outs[n][half:, :] = (part[half:] + far_down[...].astype(F32)).astype(BF16)
        else:
            outs[n][...] = part.astype(BF16)


def tail_body(*refs, wait):
    sc, refs = refs[0], refs[1:]
    wide, key_gain, small, spread2, spread4, weights, gain_row = refs[0:7]
    rows, mixed, h1, slims, query_gains = refs[7:11], refs[11:15], refs[15], refs[16:20], refs[20:24]
    keep, send, extra = refs[24:27]
    (slim_pair,) = refs[27:]
    y_at, z_at, core = sc[0], sc[1], sc[2]
    wait(3, 4)
    slim_pair[:, 0:128] = nt(wide[:, 0:256], spread2[...]).astype(BF16)
    slim_pair[:, 128:256] = nt(wide[:, 256:512], spread2[...]).astype(BF16)
    out_total = jnp.zeros((WIDTH, 256), F32)
    for chunk in range(4):
        wait(7 + chunk, 11 + chunk)
        out_total = out_total + tn(rows[chunk][...], nt(mixed[chunk][...], spread4[...]).astype(BF16))
    wait(15)
    pair_total = tn(h1[...], slim_pair[...])
    query_total = jnp.zeros((WIDTH, 256), F32)
    for chunk in range(4):
        wait(16 + chunk)
        at = slice(chunk * TOK, (chunk + 1) * TOK)
        query_total = query_total + tn(h1[at, :], slims[chunk][...])
    wait(2, 5, 6, 20, 21, 22, 23)
    shares = query_total * weights[:, 0:256].astype(F32) + pair_total * weights[:, 256:512].astype(F32)
    ones = jnp.ones((8, 256), BF16)
    high = shares.astype(BF16)
    low = (shares - high.astype(F32)).astype(BF16)
    total = (nt(ones, high) + nt(ones, low))[0:1, :] / gain_row[...]
    query_gain = (query_gains[0][0:1, :] + query_gains[1][0:1, :]) + (
        query_gains[2][0:1, :] + query_gains[3][0:1, :]
    )
    extra[0:8, :] = jnp.zeros((8, 768), F32)
    extra[8:56, :] = small[...]
    extra[0:1, :] = total[:, 0:768]
    extra[1:2, 0:256] = total[:, 768:1024]
    extra[1:2, 256:384] = query_gain
    extra[1:2, 384:512] = key_gain[0:1, :]
    query_rows, pair_rows, out_rows = query_total.astype(BF16), pair_total.astype(BF16), out_total.astype(BF16)
    for block in range(16):
        y_rel = (block // 4 - y_at + 4) % 4
        z_rel = (block % 4 - z_at + 4) % 4
        for side in range(2):
            at = (2 * block + side) * 32
            rel = y_rel * 4 + z_rel if side == 0 else z_rel * 4 + y_rel

            def put(target):
                target[rel, :, 0:256] = query_rows[at : at + 32]
                target[rel, :, 256:512] = pair_rows[at : at + 32]
                target[rel, :, 512:768] = out_rows[at : at + 32]

            pl.when(core == side)(partial(put, keep))
            pl.when(core != side)(partial(put, send))


def split3(value):
    high = value.astype(BF16).astype(F32)
    middle = (value - high).astype(BF16).astype(F32)
    low = value - high - middle
    return jnp.concatenate([high, middle, low, jnp.zeros((20, 768), F32)], axis=0).astype(BF16)


def join3(rows):
    value = rows.astype(F32)
    return value[0:4] + value[4:8] + value[8:12]


def ride_first_body(keep, got, extra, extra_got, *outs):
    gain = split3(extra[0:4, :] + extra_got[0:4, :])
    router = (extra[8:56, :] + extra_got[8:56, :]).astype(BF16)
    for first in range(4):
        for second in range(4):
            at = first * 4 + second
            outs[first][second * 32 : (second + 1) * 32, :] = (
                keep[at].astype(F32) + got[at].astype(F32)
            ).astype(BF16)
        outs[first][128:160, :] = gain
        outs[first][160:208, :] = router


def add4(own, g1, g2, g3, start, stop):
    return own[start:stop, :].astype(F32) + (
        g1[start:stop, :].astype(F32) + (g2[start:stop, :].astype(F32) + g3[start:stop, :].astype(F32))
    )


def add_gains(own, g1, g2, g3, start):
    stop = start + 32
    return (join3(own[start:stop, :]) + join3(g1[start:stop, :])) + (
        join3(g2[start:stop, :]) + join3(g3[start:stop, :])
    )


def ride_second_body(own, g1, g2, g3, *outs):
    rows = add4(own, g1, g2, g3, 0, 128)
    gain = split3(add_gains(own, g1, g2, g3, 128))
    router = add4(own, g1, g2, g3, 160, 208).astype(BF16)
    for second in range(4):
        outs[second][0:32, :] = rows[second * 32 : (second + 1) * 32].astype(BF16)
        outs[second][32:64, :] = gain
        outs[second][64:112, :] = router


def ride_last_body(own, g1, g2, g3, query, pair, out_w, attn, query_gain, key_gain, router, ffn):
    rows = add4(own, g1, g2, g3, 0, 32)
    query[...] = rows[:, 0:256]
    pair[:, 0, :] = rows[:, 256:384]
    pair[:, 1, :] = rows[:, 384:512]
    out_w[...] = rows[:, 512:768]
    gain = add_gains(own, g1, g2, g3, 32)
    attn[:, 0:768] = gain[0:1, :]
    attn[:, 768:1024] = gain[1:2, 0:256]
    query_gain[...] = gain[1:2, 256:384]
    key_gain[...] = gain[1:2, 384:512]
    total = add4(own, g1, g2, g3, 64, 112)
    router[:, 0:768] = total[0:32]
    router[0:16, 768:1024] = total[32:48, 0:256]
    router[16:32, 768:1024] = total[32:48, 256:512]
    for quarter in range(4):
        ffn[:, quarter * 256 : (quarter + 1) * 256] = total[32 + quarter : 33 + quarter, 512:768]


def input_body(p0, p1, p2, x, gain, grad_mid, out):
    upstream = p0[...].astype(F32) + (p1[...].astype(F32) + p2[...].astype(F32))
    xf = x[...].astype(F32)
    scale = row_scale(xf)
    normed = xf * scale
    grad_normed = upstream * gain[...]
    out[...] = grad_mid[...] + scale * (
        grad_normed - normed * jnp.mean(grad_normed * normed, axis=1, keepdims=True)
    )


def place_of(index):
    return index // 8, (index // 2) % 4, index % 2


def index_of(y, z, core):
    return (y % 4) * 8 + (z % 4) * 2 + core


def shift_yz(tensor, dy, dz, flip=0):
    pairs = []
    for d in range(32):
        y, z, core = place_of(d)
        pairs.append((d, index_of(y + dy, z + dz, core ^ flip)))
    return lax.ppermute(tensor, "dp", pairs)


def shift_axis(tensor, axis, step):
    pairs = []
    for d in range(32):
        y, z, core = place_of(d)
        if (core == 0) == (axis == 0):
            pairs.append((d, index_of(y + step, z, core)))
        else:
            pairs.append((d, index_of(y, z + step, core)))
    return lax.ppermute(tensor, "dp", pairs)


def shift_mp(tensor, step):
    return lax.ppermute(tensor, "mp", [(i, (i + step) % 4) for i in range(4)])


def gather_weights(shard, chunks):
    rows = jnp.stack([shard] + [shift_axis(shard, 0, -s) for s in (1, 2, 3)])
    rows = after(rows, chunks[1], chunks[3])
    own = jnp.concatenate([rows] + [shift_axis(rows, 1, -s) for s in (1, 2, 3)], axis=0)
    near = own
    own = after(own, chunks)
    return near, own, shift_yz(own, 0, 0, 1)


def gather_mp(tensor):
    plus, minus = shift_mp(tensor, -1), shift_mp(tensor, 1)
    half = tensor.shape[0] // 2
    far = jnp.concatenate([shift_mp(plus[:half], -1), shift_mp(minus[half:], 1)], axis=0)
    return [tensor, plus, far, minus]


def after(value, *others):
    return lax.optimization_barrier((value, others))[0]


def add_low(left, *others):
    total = left.astype(F32)
    for one in others:
        total = total + one.astype(F32)
    return total.astype(BF16)


PLANES = [[core + 2 * k for k in range(16)] for core in range(2)]
STEPS = (0, 1, -1, 2)


def shards(
    layer_input,
    lengths,
    routes,
    attn_gain,
    query_gain,
    key_gain,
    query_weight,
    key_value_weight,
    out_weight,
    ffn_gain,
    router_weight,
    gate_weight,
    up_weight,
    down_weight,
    cotangent,
):
    dp_at = lax.axis_index("dp").astype(jnp.int32)
    mp_at = lax.axis_index("mp").astype(jnp.int32)
    y_at, z_at, core = dp_at // 8, (dp_at // 2) % 4, dp_at % 2
    length = lengths[0].astype(jnp.int32)
    cos_np, sin_np = rope_tables()
    cos_tab, sin_tab = jnp.asarray(cos_np), jnp.asarray(sin_np)
    spread4, spread2 = jnp.asarray(spread(4), BF16), jnp.asarray(spread(2), BF16)
    attn_row = attn_gain.reshape(1, WIDTH)
    ffn_row = ffn_gain.reshape(1, WIDTH)
    pad = jnp.zeros((PITCH - HDIM,), F32)
    head_gain = jnp.concatenate([query_gain, pad] * 4 + [key_gain, pad] * 2).reshape(1, 768)
    router = router_weight.T

    chunks = gather_mp(layer_input)
    chunk_at = [(mp_at + r) % 4 for r in range(4)]
    shard = jnp.concatenate([query_weight, key_value_weight.reshape(32, 256), out_weight], axis=0)
    shards_near, shards_own, shards_other = gather_weights(shard, chunks)

    cot_all = lax.all_gather(cotangent, "dp", axis=0, tiled=False, axis_index_groups=PLANES)
    ranks, coded = call(
        start_body,
        [((EXPERTS, TOK), F32), ((SIDE, WIDTH), BF16)],
        after((routes,), shards_near),
        scalars=jnp.stack([mp_at, length]),
    )
    weights_own = (gate_weight, up_weight, down_weight)
    weights_other = tuple(shift_yz(after(w, shards_other), 0, 0, 1) for w in weights_own)

    out = call(
        project_body,
        [((LEN, WIDTH), BF16), ((WIDTH, 1024), BF16), ((WIDTH, 768), BF16)]
        + [((TOK, 512), F32)] * 4
        + [((TOK, 256), F32)] * 4
        + [((TOK, 512), BF16)] * 4
        + [((LEN, 256), BF16), ((LEN, 256), BF16), ((WIDTH, 512), BF16)]
        + [((TOK, PITCH), F32)] * 4,
        (shards_own, shards_other, *chunks, attn_row, head_gain, cos_tab, sin_tab, spread4, spread2),
        scalars=jnp.stack([y_at, z_at, core, mp_at, length]),
        any_out=range(11),
        near=range(11, 18),
        scratch=[
            pltpu.VMEM((LEN, WIDTH), BF16),
            pltpu.VMEM((LEN, 512), F32),
            pltpu.VMEM((LEN, 256), F32),
            pltpu.VMEM((WIDTH, 1024), BF16),
            pltpu.VMEM((WIDTH, 768), BF16),
            pltpu.SemaphoreType.DMA((14,)),
        ],
        mb=40,
        lazy=True,
    )
    h1, proj, weights_in, raw, raw_pair, qa = out[0], out[1], out[2], out[3:7], out[7:11], out[11:15]
    ka, va, out_w, turn_tab = out[15], out[16], out[17], out[18:22]

    qa = list(after(tuple(qa), weights_other))
    mixed, qb = [None] * 4, [None] * 4
    def attend(r, parts=1):
        *made, mixed[r], qb[r] = call(
            attend_body,
            [((TOK // parts, WIDTH), BF16)] * parts + [((TOK, 512), BF16)] * 2,
            (qa[r], ka, va, out_w),
            any_out=(parts, parts + 1),
            scratch=[pltpu.VMEM((TOK, 512), BF16), pltpu.VMEM((TOK, 512), BF16), pltpu.SemaphoreType.DMA((2,))],
            near=range(parts),
            local=(0, 1, 2, 3),
        )
        return made

    branch_up, branch_down = attend(2, 2)
    branch_up, branch_down = shift_mp(branch_up, 1), shift_mp(branch_down, -1)
    (part_up,), (part_down,) = attend(1), attend(3)
    part_up, part_down = call(
        near_body,
        [((TOK, WIDTH), BF16)] * 2,
        (part_up, part_down, branch_up, branch_down),
        near=(0, 1),
        local=range(4),
    )
    (branch,) = attend(0)
    arrived = (branch, shift_mp(part_up, 1), shift_mp(part_down, -1))
    x_mid, h2 = call(
        middle_body,
        [((TOK, WIDTH), F32), ((ROWS, WIDTH), BF16)],
        (layer_input, *arrived, ffn_row, coded),
        near=(1,),
        local=(1, 2, 3),
    )
    (gates,) = call(gates_body, [((EXPERTS, TOK), F32)], (h2, router, ranks))

    plus, minus = shift_axis(h2, 0, -1), shift_axis(h2, 0, 1)
    far_a, far_b = shift_axis(plus[:144], 0, -1), shift_axis(minus[144:], 0, 1)
    near_a, near_b = jnp.stack([h2, plus]), jnp.stack([minus, jnp.concatenate([far_a, far_b], axis=0)])
    plus_a, plus_b = shift_axis(near_a, 1, -1), shift_axis(near_b, 1, -1)
    minus_a, minus_b = shift_axis(near_a, 1, 1), shift_axis(near_b, 1, 1)
    units = [(near_a, near_b), (plus_a, plus_b), (minus_a, minus_b), None]

    first_at = jnp.where(core == 0, y_at, z_at)
    second_at = jnp.where(core == 0, z_at, y_at)
    saved = None
    backs = []
    for u, step in enumerate(STEPS):
        if u == 1:
            far_plus, far_minus = after((plus_a, minus_b), backs[0])
            units[3] = (shift_axis(far_plus, 1, -1), shift_axis(far_minus, 1, 1))
            units[2] = after(units[2], units[3])
        if u == 2:
            plus_b = shift_axis(backs[1][1], 1, 1)
        if u == 3:
            minus_a = shift_axis(backs[2][0], 1, -1)
            units[3] = after(units[3], plus_b)
        second = (second_at + step + 4) % 4
        order = []
        for s in STEPS:
            first = (first_at + s + 4) % 4
            order.append(jnp.where(core == 0, first * 4 + second, second * 4 + first))
        sc = jnp.stack(order + [dp_at, dp_at + 1 - 2 * core]).astype(jnp.int32)
        pieces = tuple(one.shape[0] for one in units[u])
        args = (*units[u], cot_all, router, *weights_own, *weights_other)
        any_in = [len(pieces)]
        aliases = None
        if saved is not None:
            base = len(args)
            aliases = {base + i: (0 if i == 0 else i + 2) for i in range(6)}
            any_in += list(range(base, base + 6))
            args = args + tuple(saved)
        made = call(
            partial(experts_body, pieces, u),
            [
                ((16, TOK, WIDTH), BF16),
                ((2, ROWS, WIDTH), BF16),
                ((2, ROWS, WIDTH), BF16),
                ((2, 16 * CAP, WIDTH), BF16),
                ((2, 16 * CAP, WIDTH), BF16),
                ((2, 16 * CAP, FF), BF16),
                ((2, 16 * CAP, FF), BF16),
                ((2, 16 * CAP, FF), BF16),
            ],
            args,
            scalars=sc,
            any_in=any_in,
            any_out=range(8),
            scratch=[
                pltpu.VMEM((4, TOK, WIDTH), BF16),
                pltpu.VMEM((4, TOK, WIDTH), BF16),
                pltpu.VMEM((4, ROWS, WIDTH), BF16),
                pltpu.VMEM((2, 4 * CAP, WIDTH), BF16),
                pltpu.VMEM((2, 4 * CAP, WIDTH), BF16),
                pltpu.VMEM((2, 4 * CAP, WIDTH), BF16),
                pltpu.VMEM((2, 4 * CAP, FF), BF16),
                pltpu.VMEM((2, 4 * CAP, FF), BF16),
                pltpu.VMEM((2, 4 * CAP, FF), BF16),
                pltpu.SemaphoreType.DMA((32,)),
            ],
            aliases=aliases,
            local=(*range(len(pieces)), *range(len(pieces) + 2, len(pieces) + 8)),
            mb=36,
            lazy=True,
        )
        backs.append(made[1:3])
        saved = [made[0]] + list(made[3:])
    y_out, taken, push, hidden, grad_gate, grad_up = saved

    (b0_a, b0_b), (bp_a, _), (_, bm_b), (bf_a, bf_b) = backs
    half_a, half_b = shift_axis(bf_a, 1, 1), shift_axis(bf_b, 1, -1)
    saved = (taken, push, hidden, grad_gate, grad_up)
    for_other = expert_weights(after(saved, minus_a), 1, mp_at)
    for_other = after(for_other, half_a, half_b)
    plus_late, minus_late = add_low(bp_a, half_a), add_low(bm_b, half_b)
    plus_a, minus_b = shift_axis(plus_late, 1, 1), shift_axis(minus_late, 1, -1)
    from_other = shift_yz(for_other[0], 0, 0, 1)
    shard_grads = expert_weights(after(saved, plus_late, minus_late), 0, mp_at, (from_other,))
    shard_far = shift_mp(shard_grads[3], 1), shift_mp(shard_grads[4], -1)
    b0_a, b0_b = after((b0_a, b0_b), shard_grads)
    line_a = add_low(b0_a, plus_a, minus_a)
    line_b = add_low(b0_b, plus_b, minus_b)
    cut = ROWS // 2 + 8
    far_up, far_down = shift_axis(line_b[1, :cut], 0, 1), shift_axis(line_b[1, cut:], 0, -1)
    send_up = jnp.concatenate([add_low(line_a[1, :cut], far_up), line_a[1, cut:]], axis=0)
    send_down = jnp.concatenate([line_b[0, :cut], add_low(line_b[0, cut:], far_down)], axis=0)
    shard_near = call(
        shard_near_body,
        [((768, FF), BF16)] * 2,
        (shard_grads[1], shard_grads[2], *shard_far),
        near=(0, 1),
        local=range(4),
    )
    send_up, send_down = after((send_up, send_down), shard_near)
    got_up, got_down = shift_axis(send_up, 0, 1), shift_axis(send_down, 0, -1)
    grad_mid, grad_rows, small = call(
        token_back_body,
        [((TOK, WIDTH), F32), ((TOK, WIDTH), BF16), ((48, 768), F32)],
        (line_a[0], got_up, got_down, h2, x_mid, ranks, gates, router, ffn_row, cotangent),
        scalars=jnp.stack([mp_at, length]),
        near=(1,),
        local=(0, 1, 2),
        lazy=True,
    )

    returned = lax.psum_scatter(
        after(y_out, grad_rows).reshape(16 * TOK, WIDTH), "dp", scatter_dimension=0, tiled=True, axis_index_groups=PLANES
    )
    both = None
    grad_query, query_gains, slim = [None] * 4, [None] * 4, [None] * 4
    def sum_mp(t):
        return t + (shift_mp(t, 1) + shift_mp(t, 2) + shift_mp(t, 3))

    rows = [grad_rows, shift_mp(grad_rows, -1), None, shift_mp(grad_rows, 1)]
    for turn, r in enumerate((0, 1, 3, 2)):
        if turn == 2:
            near_a, near_b = after((rows[1], rows[3]), grad_query[1])
            rows[2] = jnp.concatenate(
                [shift_mp(near_a[: TOK // 2], -1), shift_mp(near_b[TOK // 2 :], 1)], axis=0
            )
        if turn == 1:
            shard_near = after(shard_near, rows[1], rows[3], grad_query[0])
            shards_got = shift_mp(shard_near[0], 1), shift_mp(shard_near[1], -1)
            rows[r] = after(rows[r], rows[3])
        args = (rows[r], out_w, qb[r], mixed[r], ka, va, raw[r], head_gain, turn_tab[r], spread4)
        first = both is None
        grad_query[r], query_gains[r], slim[r], both = call(
            partial(attend_back_body, first),
            [((TOK, 512), BF16), ((8, PITCH), F32), ((TOK, 256), BF16), ((2, LEN, 256), F32)],
            args if first else args + (both,),
            any_in=() if first else (len(args),),
            any_out=(3,),
            scratch=[pltpu.VMEM((2, LEN, 256), F32), pltpu.SemaphoreType.DMA((4,))],
            aliases=None if first else {len(args): 3},
            local=(0, 1, 4, 5),
            mb=32,
            lazy=True,
        )
    far_up, far_down, wide, key_gain_part = call(
        keys_back_body,
        [((TOK // 2, WIDTH), BF16)] * 2 + [((LEN, 512), BF16), ((8, PITCH), F32)],
        (after(both, shards_got), *raw_pair, *turn_tab, head_gain, grad_query[2], proj),
        near=range(4),
        mb=32,
        lazy=True,
    )
    far_up, far_down = shift_mp(far_up, 1), shift_mp(far_down, -1)
    keep, send, extra = call(
        tail_body,
        [((16, 32, 768), BF16), ((16, 32, 768), BF16), ((56, 768), F32)],
        (
            wide,
            key_gain_part,
            small,
            spread2,
            spread4,
            weights_in,
            attn_row,
            *rows,
            *mixed,
            h1,
            *slim,
            *query_gains,
        ),
        scalars=jnp.stack([y_at, z_at, core]),
        scratch=[pltpu.VMEM((LEN, 256), BF16)],
        near=range(3),
        local=(0, 1),
        mb=40,
        lazy=True,
    )
    send = after(send, far_up, far_down)
    extra = sum_mp(extra)
    part_up, part_down, part_own = call(
        parts_body,
        [((TOK, WIDTH), BF16)] * 3,
        (wide, far_up, far_down, proj, *(grad_query[r] for r in (1, 3, 0))),
        near=range(3),
        local=(0, 1, 2),
        lazy=True,
    )
    part_up, part_down = shift_mp(part_up, 1), shift_mp(part_down, -1)
    layer_output = (x_mid + returned.astype(F32)).astype(BF16)
    expert_grads = shard_grads[0].astype(F32) + (shards_got[0].astype(F32) + shards_got[1].astype(F32))
    expert_outs = (
        expert_grads[0:256].reshape(1, 256, FF),
        expert_grads[256:512].reshape(1, 256, FF),
        jnp.concatenate([expert_grads[512:640], expert_grads[640:768]], axis=1).reshape(1, 128, WIDTH),
    )
    first_msg = call(
        ride_first_body,
        [((208, 768), BF16)] * 4,
        (keep, shift_yz(send, 0, 0, 1), extra, shift_yz(extra, 0, 0, 1)),
        near=range(4),
        local=range(4),
    )
    second_msg = call(
        ride_second_body,
        [((112, 768), BF16)] * 4,
        after((first_msg[0], *(shift_axis(first_msg[s], 0, s) for s in (1, 2, 3))), part_up, part_down, layer_output, expert_outs),
        near=range(4),
        local=range(4),
    )
    query_w_grad, pair_w_grad, out_w_grad, attn_grad, query_gain_grad, key_gain_grad, router_grad, ffn_grad = call(
        ride_last_body,
        [
            ((32, 256), F32),
            ((32, 2, 128), F32),
            ((32, 256), F32),
            ((1, WIDTH), F32),
            ((1, PITCH), F32),
            ((1, PITCH), F32),
            ((EXPERTS, WIDTH), F32),
            ((1, WIDTH), F32),
        ],
        (second_msg[0], *(shift_axis(second_msg[s], 1, s) for s in (1, 2, 3))),
        local=range(4),
    )
    (input_grad,) = call(
        input_body,
        [((TOK, WIDTH), F32)],
        (part_own, part_up, part_down, layer_input, attn_row, grad_mid),
        local=(0, 1, 2),
    )

    return (
        layer_output,
        input_grad,
        attn_grad.reshape(WIDTH),
        query_gain_grad[0, :HDIM],
        key_gain_grad[0, :HDIM],
        query_w_grad,
        pair_w_grad,
        out_w_grad,
        ffn_grad.reshape(WIDTH),
        router_grad.T,
        *expert_outs,
    )


def solution(mesh):
    tokens = P(("dp", "mp"), None)
    in_specs = (
        tokens,
        P("dp"),
        tokens,
        P(),
        P(),
        P(),
        P("dp", "mp"),
        P("dp", None, "mp"),
        P("dp", "mp"),
        P(),
        P(),
        P("dp", None, None),
        P("dp", None, None),
        P("dp", None, None),
        tokens,
    )
    out_specs = (
        tokens,
        tokens,
        P(),
        P(),
        P(),
        P("dp", "mp"),
        P("dp", None, "mp"),
        P("dp", "mp"),
        P(),
        P(),
        P("dp", "mp", None),
        P("dp", "mp", None),
        P("dp", "mp", None),
    )
    return jax.shard_map(shards, mesh=mesh, in_specs=in_specs, out_specs=out_specs, check_vma=False)
```
